512 devices in a mesh: rep: 8 (over z_hi, x), dp: 64 (over y, z_lo, core).
Axes of the slice: x: 4, y: 8, z: 8 (z_hi: 2, z_lo: 4; z = z_hi * 4 + z_lo), core: 2. Of those that a mesh axis runs over, the one named last changes fastest.
Arguments:
- query_states: bfloat16 [8, 512, 32, 4096], P('rep', 'dp'), may hold values from -6 to 6
- query_lengths: int32 [8, 512], P('rep', 'dp'), may hold values from 1 to 32, as said below
- norm_gain: float32 [4096], replicated, may hold values from 0.5 to 2
- positives: bfloat16 [8, 512, 4096], P('rep', 'dp'), may hold values from -0.25 to 0.25
- mined_pool: bfloat16 [8, 1024, 4096], P('rep', 'dp'), may hold values from -0.25 to 0.25
- hard_ids: int32 [8, 512, 7], P('rep', 'dp'), may hold values from 0 to 1023, as said below
Outputs:
- query_grad: bfloat16 [8, 512, 32, 4096], P('rep', 'dp')
- positive_gradient: float32 [8, 512, 4096], P('rep', 'dp')
- pool_grad: float32 [8, 1024, 4096], P('rep', 'dp')
- gain_grad: float32 [4096], replicated
The draws below stay inside these ranges and needn't reach their ends.
Inputs may be any that keep to these rules, and one draw needn't show every extreme that they name: `query_lengths`: in each group some query has 32 tokens. `hard_ids`: rows r * 16 to (r + 1) * 16 - 1 of a group's mined passages lie on device r of dp. The 56 ids of one device's queries name at most 2 rows of any one device; in every group one device's rows are named exactly 2 times by the queries of every device.
All inputs are finite; a program needn't handle non-finite values.
Results may differ from the reference program's by a relative error of at most 0.0039.
Values may be sent and summed in bfloat16 or wider, within the bound.
No kernel may reach another device: no remote copies, remote signals or barrier semaphores. Data moves between devices by JAX's collectives and lax.ppermute only.
A program may use at most 64 MiB of HBM per device.

```python
import math
from functools import partial
import jax
import jax.numpy as jnp
from jax import lax

D = 4096
QTOK = 32
HARD = 7
Q_DEV = 8
NEG_DEV = 16
GROUPS = 8
OWNERS = 64
Q_ALL = 512
POOL = 1024
CAP = 2


def shared_signs(key):
    key = jax.random.fold_in(key, 103)
    return (2 * jax.random.randint(key, (GROUPS, Q_ALL, D), 0, 2) - 1).astype(jnp.float32)


def shared_ids(key):
    key = jax.random.fold_in(key, 9)
    key_list = jax.random.split(key, 4)
    request_count = Q_DEV * HARD
    hot_owner = jax.random.randint(key_list[0], (GROUPS, 1, 1), 0, OWNERS)
    perm_keys = jax.random.split(key_list[1], GROUPS * OWNERS)
    others = jax.vmap(lambda subkey: jax.random.permutation(subkey, OWNERS - 1))(perm_keys)
    others = others.reshape(GROUPS, OWNERS, OWNERS - 1)
    others = others + (others >= hot_owner).astype(jnp.int32)
    position = jnp.arange(request_count)
    cycle_index = jnp.maximum(position - CAP, 0) % (OWNERS - 1)
    sequence = jnp.take(others, cycle_index, axis=2)
    owner_index = jnp.where(position[None, None, :] < CAP, hot_owner, sequence)
    shuffle_keys = jax.random.split(key_list[2], GROUPS * OWNERS)
    shuffle = jax.vmap(lambda subkey: jax.random.permutation(subkey, request_count))(shuffle_keys)
    shuffle = shuffle.reshape(GROUPS, OWNERS, request_count)
    owner_index = jnp.take_along_axis(owner_index, shuffle, axis=2)
    row_index = jax.random.randint(key_list[3], (GROUPS, OWNERS, request_count), 0, NEG_DEV)
    passage_ids = owner_index * NEG_DEV + row_index
    return passage_ids.reshape(GROUPS, Q_ALL, HARD).astype(jnp.int32)


def draw_query_lengths(key, part):
    key = jax.random.fold_in(key, 5)
    key_values, key_choice = jax.random.split(key)
    values = jax.random.randint(key_values, (GROUPS, Q_ALL), 1, QTOK + 1)
    chosen = jax.random.randint(key_choice, (GROUPS, 1), 0, Q_ALL)
    full_length = jnp.arange(Q_ALL)[None, :] == chosen
    return jnp.where(full_length, QTOK, values).astype(jnp.int32)


def draw_hard_ids(key, part):
    return shared_ids(key)


def draw_query_states(key, part):
    topics = shared_signs(key)
    key = jax.random.fold_in(key, 21)
    key_noise = jax.random.fold_in(key, 0)
    shape_all = (GROUPS, Q_ALL, QTOK, D)
    jitter = jnp.clip(jax.random.normal(key_noise, shape_all, jnp.float32), -3.0, 3.0)
    return (topics[:, :, None, :] + jitter).astype(jnp.bfloat16)


def draw_positives(key, part):
    topics = shared_signs(key)
    key = jax.random.fold_in(key, 31)
    shape_all = (GROUPS, Q_ALL, D)
    jitter = 0.015625 * jnp.clip(jax.random.normal(key, shape_all, jnp.float32), -6.0, 6.0)
    return jnp.clip(0.1 * D ** (-0.5) * topics + jitter, -0.25, 0.25).astype(jnp.bfloat16)


def draw_mined_pool(key, part):
    topics = shared_signs(key)
    passage_ids = shared_ids(key)
    key = jax.random.fold_in(key, 41)

    def summed(group_pair):
        group_signs, group_ids = group_pair
        naming = jnp.sum((group_ids[None, :, :] == jnp.arange(POOL)[:, None, None]).astype(jnp.float32), axis=2)
        return (jnp.dot(naming, group_signs, precision=lax.Precision.HIGHEST), jnp.sum(naming, axis=1))
    sign_sum, namers = lax.map(summed, (topics, passage_ids))
    pulled = 0.15 * D ** (-0.5) * sign_sum / jnp.sqrt(jnp.maximum(namers, 1.0))[:, :, None]
    shape_all = (GROUPS, POOL, D)
    jitter = 0.015625 * jnp.clip(jax.random.normal(key, shape_all, jnp.float32), -6.0, 6.0)
    return jnp.clip(pulled + jitter, -0.25, 0.25).astype(jnp.bfloat16)


def setup_inputs(seed: int = 0) -> dict:
    key_of = jax.random.split(jax.random.key(seed), 7)
    return {
        "query_states": draw_query_states(jax.random.fold_in(key_of[6], 71), 0),
        "query_lengths": draw_query_lengths(jax.random.fold_in(key_of[6], 71), 0),
        "norm_gain": jnp.clip(jnp.exp(jax.random.uniform(key_of[2], (D,), jnp.float32, math.log(0.5), math.log(2.0))), 0.5, 2.0),
        "positives": draw_positives(jax.random.fold_in(key_of[6], 71), 0),
        "mined_pool": draw_mined_pool(jax.random.fold_in(key_of[6], 71), 0),
        "hard_ids": draw_hard_ids(jax.random.fold_in(key_of[6], 71), 0),
    }


SOFTMAX_WARMTH = 0.02
QUERY_SCALE = 512.0
POOL_SCALE = 16.0
HIGHEST_ACCURACY = lax.Precision.HIGHEST

def embed(states, lengths, gain):
    square = lax.optimization_barrier(jnp.mean(states * states, axis=-1, keepdims=True))
    normed = states * lax.rsqrt(square + 1e-05) * gain
    positions = jnp.arange(states.shape[1]).astype(jnp.int32)
    token_mask = (positions[None, :] < lengths[:, None]).astype(jnp.float32)
    pooled = lax.optimization_barrier(jnp.sum(normed * token_mask[:, :, None], axis=1)) / lengths[:, None].astype(jnp.float32)
    return pooled * lax.rsqrt(lax.optimization_barrier(jnp.sum(pooled * pooled, axis=-1, keepdims=True)) + 1e-06)

def one_group(gain, batch):
    states, lengths, grouped_keys, pool_group, passage_ids = batch
    states32 = states.astype(jnp.float32)
    embedded32, pullback = jax.vjp(lambda values_in, gain_in: embed(values_in, lengths, gain_in), states32, gain)
    embedded_rows = embedded32.astype(jnp.bfloat16)
    embedding_single = embedded_rows.astype(jnp.float32)
    similarity_matrix = jnp.dot(embedded_rows, grouped_keys.T, preferred_element_type=jnp.float32) / SOFTMAX_WARMTH
    hard_rows = jnp.take(pool_group, passage_ids, axis=0)
    hard_single = hard_rows.astype(jnp.float32)
    hard_similarity = jnp.einsum('rh,rxh->rx', embedding_single, hard_single, precision=HIGHEST_ACCURACY) / SOFTMAX_WARMTH
    exp_pos = jnp.exp(similarity_matrix)
    exponent_hard = jnp.exp(hard_similarity)
    denominator_totals = lax.optimization_barrier(jnp.sum(exp_pos, axis=1)) + lax.optimization_barrier(jnp.sum(exponent_hard, axis=1))
    positive_numerator = jnp.dot(exp_pos.astype(jnp.bfloat16), grouped_keys, preferred_element_type=jnp.float32)
    positive_numerator = positive_numerator + jnp.einsum('qm,qmd->qd', exponent_hard.astype(jnp.bfloat16).astype(jnp.float32), hard_single, precision=HIGHEST_ACCURACY)
    embedding_gradient = (positive_numerator / denominator_totals[:, None] - grouped_keys.astype(jnp.float32)) / SOFTMAX_WARMTH
    states_grad, gain_part = pullback(embedding_gradient)
    softmax_probs = (exp_pos / denominator_totals[:, None]).astype(jnp.bfloat16)
    key_gradient = (jnp.dot(softmax_probs.T, embedded_rows, preferred_element_type=jnp.float32) - embedding_single) / SOFTMAX_WARMTH
    hard_summands = (exponent_hard / denominator_totals[:, None])[:, :, None] * embedding_single[:, None, :] / SOFTMAX_WARMTH
    width = pool_group.shape[1]
    pool_grad = POOL_SCALE * jnp.zeros(pool_group.shape, jnp.float32).at[passage_ids.reshape(-1)].add(hard_summands.reshape(-1, width))
    return ((QUERY_SCALE * states_grad).astype(jnp.bfloat16), key_gradient, pool_grad, gain_part)

def reference(query_states, query_lengths, norm_gain, positives, mined_pool, hard_ids):
    results = lax.map(partial(one_group, norm_gain), (query_states, query_lengths, positives, mined_pool, hard_ids))
    return (results[0], results[1], results[2], lax.optimization_barrier(jnp.sum(results[3], axis=0)))
```

```python
import jax
import jax.numpy as jnp
from jax import lax
from jax.sharding import PartitionSpec as P

TEMPERATURE = 0.02
QUERY_SCALE = 512.0
POOL_SCALE = 16.0


def embed(states, lengths, gain):
    square = jnp.mean(states * states, axis=-1, keepdims=True)
    normed = states * lax.rsqrt(square + 1e-05) * gain
    positions = jnp.arange(states.shape[1])
    token_mask = (positions[None, :] < lengths[:, None]).astype(jnp.float32)
    pooled = jnp.sum(normed * token_mask[:, :, None], axis=1) / lengths[:, None].astype(jnp.float32)
    return pooled * lax.rsqrt(jnp.sum(pooled * pooled, axis=-1, keepdims=True) + 1e-06)


def two_parts(x):
    high = x.astype(jnp.bfloat16)
    low = (x - high.astype(jnp.float32)).astype(jnp.bfloat16)
    return high, low


def to_slices(rows, owners):
    r, d = rows.shape
    return rows.reshape(r, owners, d // owners).transpose(1, 0, 2)


def from_slices(slices):
    owners, r, f = slices.shape
    return slices.transpose(1, 0, 2).reshape(r, owners * f)


def local(query_states, query_lengths, norm_gain, positives, mined_pool, hard_ids):
    owners = lax.axis_size("dp")
    me = lax.axis_index("dp")
    core = me % 2
    states32 = query_states[0].astype(jnp.float32)
    lengths = query_lengths[0]
    own_pos = positives[0]
    own_pool = mined_pool[0]
    ids = hard_ids[0]
    queries, hard = ids.shape
    q_all = queries * owners
    pool_all = own_pool.shape[0] * owners
    width = own_pos.shape[1]
    feats = width // owners

    unit, pullback = jax.vjp(lambda s, g: embed(s, lengths, g), states32, norm_gain)
    embedded, embedded_low = two_parts(unit)

    left = jnp.concatenate([embedded, own_pos], axis=0)
    id_parts = jnp.concatenate([ids // 32, ids % 32], axis=1).astype(jnp.bfloat16)
    id_rows = jnp.pad(id_parts, ((0, 0), (0, feats - 2 * hard)))
    out = jnp.concatenate(
        [
            jnp.concatenate([to_slices(left, owners), to_slices(own_pool, owners)], axis=2),
            jnp.concatenate(
                [
                    to_slices(embedded_low, owners),
                    jnp.broadcast_to(id_rows[None], (owners, queries, feats)),
                ],
                axis=2,
            ),
        ],
        axis=1,
    )
    got = lax.all_to_all(out, "dp", 0, 0, tiled=True)
    e_f = got[:, :queries, :feats].reshape(q_all, feats)
    p_f = got[:, queries : 2 * queries, :feats].reshape(q_all, feats)
    m_f = got[:, : 2 * queries, feats:].reshape(pool_all, feats)
    low_f = got[:, 2 * queries :, :feats].reshape(q_all, feats)
    id_got = got[:, 2 * queries :, feats:].reshape(q_all, feats).astype(jnp.int32)
    ids_all = id_got[:, :hard] * 32 + id_got[:, hard : 2 * hard]

    contract = (((1,), (1,)), ((), ()))
    sim = lax.dot_general(e_f, p_f, contract, preferred_element_type=jnp.float32)
    pool_sim = lax.dot_general(e_f, m_f, contract, preferred_element_type=jnp.float32)
    named = ids_all[:, :, None] == jnp.arange(pool_all)[None, None, :]
    hard_sim = jnp.sum(jnp.where(named, pool_sim[:, None, :], 0.0), axis=2)
    part = jnp.concatenate([sim, jnp.pad(hard_sim, ((0, 0), (0, 128 - hard)))], axis=1)
    part = part.reshape(owners // 2, 2, queries, q_all + 128)
    mine = lax.dynamic_index_in_dim(part, core, 1, keepdims=False)
    theirs = lax.dynamic_index_in_dim(part, 1 - core, 1, keepdims=False)
    theirs = lax.ppermute(theirs, "dp", [(i, i ^ 1) for i in range(owners)])
    same_core = [[2 * i + c for i in range(owners // 2)] for c in range(2)]
    pieces = lax.all_to_all(mine + theirs, "dp", 0, 0, tiled=True, axis_index_groups=same_core)
    scores = jnp.sum(pieces, axis=0) / TEMPERATURE

    column = jnp.arange(q_all + 128)
    exps = jnp.where(column[None, :] < q_all + hard, jnp.exp(scores), 0.0)
    soft = exps / jnp.sum(exps, axis=1, keepdims=True)
    own = column[None, :] == (me * queries + jnp.arange(queries))[:, None]
    along = jnp.sum(soft * scores - jnp.where(own, scores, 0.0), axis=1, keepdims=True)
    soft_high, soft_low = two_parts(soft)
    along_high, along_low = two_parts(along)
    tail = jnp.concatenate(
        [soft_high[:, q_all : q_all + hard], soft_low[:, q_all : q_all + hard], along_high, along_low],
        axis=1,
    )
    sent = jnp.concatenate(
        [soft_high[:, :q_all], jnp.pad(tail, ((0, 0), (0, 128 - 2 * hard - 2)))], axis=1
    )
    weights = lax.all_to_all(
        jnp.broadcast_to(sent[None], (owners, queries, q_all + 128)), "dp", 0, 0, tiled=True
    ).reshape(q_all, q_all + 128)
    w_pos = weights[:, :q_all]
    tails = weights[:, q_all:].astype(jnp.float32)
    w_hard = tails[:, :hard] + tails[:, hard : 2 * hard]
    along_all = tails[:, 2 * hard : 2 * hard + 1] + tails[:, 2 * hard + 1 : 2 * hard + 2]
    spread = jnp.sum(jnp.where(named, w_hard[:, :, None], 0.0), axis=1)
    spread_high, spread_low = two_parts(spread)

    e32 = e_f.astype(jnp.float32)
    numerator = jnp.dot(w_pos, p_f, preferred_element_type=jnp.float32) + jnp.dot(
        spread_high, m_f, preferred_element_type=jnp.float32
    )
    emb_grad = (numerator - p_f.astype(jnp.float32)) / TEMPERATURE
    by_column = (((0,), (0,)), ((), ()))
    key_grad = (
        lax.dot_general(w_pos, e_f, by_column, preferred_element_type=jnp.float32) - e32
    ) / TEMPERATURE
    pool_grad = (POOL_SCALE / TEMPERATURE) * (
        lax.dot_general(spread_high, e_f, by_column, preferred_element_type=jnp.float32)
        + lax.dot_general(spread_low, e_f, by_column, preferred_element_type=jnp.float32)
    )
    unit_f = e32 + low_f.astype(jnp.float32)
    gain_part = jnp.sum((emb_grad - along_all * unit_f) * unit_f, axis=0)
    gain_part = gain_part / lax.dynamic_slice_in_dim(norm_gain, me * feats, feats, 0)
    gain_row = jnp.concatenate(two_parts(gain_part), axis=0)
    back = jnp.concatenate(
        [
            jnp.concatenate(
                [
                    emb_grad.reshape(owners, queries, feats),
                    key_grad.reshape(owners, queries, feats),
                ],
                axis=1,
            ),
            pool_grad.reshape(owners, 2 * queries, feats),
        ],
        axis=2,
    ).astype(jnp.bfloat16)
    back = jnp.concatenate(
        [back, jnp.broadcast_to(gain_row[None, None], (owners, 8, 2 * feats))], axis=1
    )
    home = lax.all_to_all(back, "dp", 0, 0, tiled=True)
    emb_home = from_slices(home[:, :queries, :feats]).astype(jnp.float32)
    key_home = from_slices(home[:, queries : 2 * queries, :feats]).astype(jnp.float32)
    pool_home = from_slices(home[:, : 2 * queries, feats:]).astype(jnp.float32)
    gain_home = home[:, 2 * queries, :].astype(jnp.float32)
    gain_group = (gain_home[:, :feats] + gain_home[:, feats:]).reshape(width // 128, 128)
    groups = lax.axis_size("rep")
    gain_groups = lax.all_to_all(
        jnp.broadcast_to(gain_group[None], (groups, width // 128, 128)), "rep", 0, 0, tiled=True
    )
    gain_grad = jnp.sum(gain_groups, axis=0).reshape(width)
    states_grad, _ = pullback(emb_home)
    query_grad = (QUERY_SCALE * states_grad).astype(jnp.bfloat16)
    return query_grad[None], key_home[None], pool_home[None], gain_grad


def solution(mesh):
    placed = (
        P("rep", "dp", None, None),
        P("rep", "dp"),
        P(),
        P("rep", "dp", None),
        P("rep", "dp", None),
        P("rep", "dp", None),
    )
    return jax.shard_map(
        local,
        mesh=mesh,
        in_specs=placed,
        out_specs=(P("rep", "dp", None, None), P("rep", "dp", None), P("rep", "dp", None), P()),
        check_vma=False,
    )
```

```python
import jax
import jax.numpy as jnp
from jax import lax
from jax.experimental import pallas as pl
from jax.experimental.pallas import tpu as pltpu
from jax.sharding import PartitionSpec as P

TEMPERATURE = 0.02
QUERY_SCALE = 512.0
POOL_SCALE = 16.0
LANES = 128
HALF = 64
F32 = jnp.float32
BF16 = jnp.bfloat16
BY_COLUMN = (((0,), (0,)), ((), ()))
BY_ROW = (((1,), (1,)), ((), ()))


def swap(x):
    return pltpu.roll(x, HALF, 1)


def left_half(rows):
    return lax.broadcasted_iota(jnp.int32, (rows, LANES), 1) < HALF


def embed_kernel(len_ref, x_ref, gain_ref, pos_ref, pool_ref, ids_ref, out_ref, unit_ref, inv_ref, norm_ref, weight_ref):
    queries, width = unit_ref.shape
    tokens = x_ref.shape[0] // queries
    chunks = width // LANES
    token = lax.broadcasted_iota(jnp.int32, (tokens, 1), 0)

    def one_query(i, carry):
        rows = pl.ds(pl.multiple_of(i * tokens, tokens), tokens)
        square = jnp.zeros((tokens, LANES), F32)
        for k in range(chunks):
            v = x_ref[rows, k * LANES : (k + 1) * LANES].astype(F32)
            square += v * v
        inv = lax.rsqrt(jnp.sum(square, axis=1, keepdims=True) / width + 1e-05)
        inv_ref[rows, :] = jnp.broadcast_to(inv, (tokens, LANES))
        length = len_ref[i]
        weight = jnp.where(token < length, inv, 0.0) / length.astype(F32)
        weight_ref[rows, :] = jnp.broadcast_to(weight, (tokens, LANES))
        return carry

    lax.fori_loop(0, queries, one_query, 0)
    for k in range(chunks):
        cols = slice(k * LANES, (k + 1) * LANES)
        v = x_ref[:, cols].astype(F32) * weight_ref[...]
        v = jnp.sum(v.reshape(queries, tokens, LANES), axis=1)
        unit_ref[:, cols] = v * gain_ref[:, cols]
    pooled = unit_ref[...]
    norm = lax.rsqrt(jnp.sum(pooled * pooled, axis=1, keepdims=True) + 1e-06)
    norm_ref[...] = jnp.broadcast_to(norm, norm_ref.shape)
    ids = ids_ref[...]
    lane = lax.broadcasted_iota(jnp.int32, (queries, LANES), 1)
    id_rows = jnp.zeros((queries, LANES), jnp.int32)
    hard = ids.shape[1]
    for m in range(hard):
        one = ids[:, m : m + 1]
        id_rows = jnp.where(lane == m, one >> 5, id_rows)
        id_rows = jnp.where(lane == hard + m, one & 31, id_rows)
    id_rows = id_rows.astype(F32)
    left8, left16 = left_half(queries), left_half(2 * queries)
    for k in range(chunks):
        cols = slice(k * LANES, (k + 1) * LANES)
        unit = unit_ref[:, cols] * norm
        unit_ref[:, cols] = unit
        high = unit.astype(BF16).astype(F32)
        low = unit - high
        upper = jnp.concatenate([high, pos_ref[:, cols].astype(F32)], axis=0)
        pool = pool_ref[:, cols].astype(F32)
        even = jnp.concatenate(
            [jnp.where(left16, upper, swap(pool)), jnp.where(left8, id_rows, swap(low))], axis=0
        )
        odd = jnp.concatenate(
            [jnp.where(left16, swap(upper), pool), jnp.where(left8, id_rows, low)], axis=0
        )
        out_ref[2 * k] = even.astype(BF16)
        out_ref[2 * k + 1] = odd.astype(BF16)


def similar_kernel(
    hard, core_ref, got_ref, gotx_ref, sim_ref, e_ref, unit_ref, own_ref, p_ref, m_ref, ids_ref
):
    core = core_ref[0]
    chips, _, rows, _ = got_ref.shape
    q = rows // 3
    half = chips * q

    def parts(block):
        n = block.shape[0]
        block = block.astype(F32)
        return (
            block[:, :q].reshape(n * q, LANES),
            block[:, q : 2 * q].reshape(n * q, LANES),
            block[:, 2 * q :].reshape(n * q, LANES),
        )

    left = left_half(half)
    ea, pa, ta = parts(got_ref[:, core])
    eb, pb, tb = parts(gotx_ref[:, core])
    e = jnp.where(left, ea, swap(eb))
    e_ref[...] = e.astype(BF16)
    unit_ref[...] = e + jnp.where(left, swap(ta), tb)
    own_ref[...] = jnp.where(left, pa, swap(pb))
    lane = lax.broadcasted_iota(jnp.int32, (half, LANES), 1)
    ids = ta * 32.0 + pltpu.roll(ta, LANES - hard, 1)
    ids = jnp.where(lane < hard, ids, 0.0).astype(jnp.int32)
    ids_ref[...] = ids
    a = got_ref[...].reshape(2 * chips, rows, LANES).astype(F32)
    b = gotx_ref[...].reshape(2 * chips, rows, LANES).astype(F32)
    n = 2 * chips * q
    p = jnp.where(
        left_half(n), a[:, q : 2 * q].reshape(n, LANES), swap(b[:, q : 2 * q].reshape(n, LANES))
    ).astype(BF16)
    m = jnp.where(
        left_half(2 * n),
        swap(a[:, : 2 * q].reshape(2 * n, LANES)),
        b[:, : 2 * q].reshape(2 * n, LANES),
    ).astype(BF16)
    p_ref[...] = p
    m_ref[...] = m
    eh = e.astype(BF16)
    sim_ref[:, :, :n] = lax.dot_general(eh, p, BY_ROW, preferred_element_type=F32).reshape(chips, q, n)
    pool = lax.dot_general(eh, m, BY_ROW, preferred_element_type=F32)
    tail = jnp.zeros((half, LANES), F32)
    within, tile = ids & (LANES - 1), ids >> 7
    for k in range(2 * n // LANES):
        picked = jnp.take_along_axis(
            pool[:, k * LANES : (k + 1) * LANES], within, axis=1, mode="promise_in_bounds"
        )
        tail = jnp.where(tile == k, picked, tail)
    tail = jnp.where(lane < hard, tail, 0.0)
    sim_ref[:, :, n:] = tail.reshape(chips, q, LANES)


def softmax_kernel(hard, me_ref, in_ref, out_ref):
    copies, q, width = out_ref.shape
    n = width - LANES
    scores = jnp.sum(in_ref[...], axis=0) / TEMPERATURE
    column = lax.broadcasted_iota(jnp.int32, (q, width), 1)
    row = lax.broadcasted_iota(jnp.int32, (q, width), 0)
    exps = jnp.where(column < n + hard, jnp.exp(scores), 0.0)
    soft = exps / jnp.sum(exps, axis=1, keepdims=True)
    own = column == row + me_ref[0] * q
    along = jnp.sum(soft * scores - jnp.where(own, scores, 0.0), axis=1, keepdims=True)
    high = along.astype(BF16).astype(F32)
    sent = jnp.where(column == n + hard, high, soft)
    sent = jnp.where(column == n + hard + 1, along - high, sent)
    sent = sent.astype(BF16)
    for k in range(copies):
        out_ref[k] = sent


def slices_kernel(
    hard, me_ref, w_ref, e_ref, unit_ref, own_ref, p_ref, m_ref, ids_ref, gain_ref, out_ref
):
    me = me_ref[0]
    core, chip = lax.rem(me, 2), lax.div(me, 2)
    chips, q, width = w_ref.shape
    n = width - LANES
    half = chips * q
    w = w_ref[...].astype(F32).reshape(half, width)
    tail = w[:, n:]
    w_pos = w[:, :n].astype(BF16)
    ids = ids_ref[...]
    column = lax.broadcasted_iota(jnp.int32, (half, 2 * n), 1)
    spread = jnp.zeros((half, 2 * n), F32)
    for m in range(hard):
        spread += jnp.where(column == ids[:, m : m + 1], tail[:, m : m + 1], 0.0)
    spread = spread.astype(BF16)
    along = tail[:, hard : hard + 1] + tail[:, hard + 1 : hard + 2]
    e = e_ref[...]
    unit = unit_ref[...]
    numerator = jnp.dot(w_pos, p_ref[...], preferred_element_type=F32)
    numerator += jnp.dot(spread, m_ref[...], preferred_element_type=F32)
    emb_grad = (numerator - own_ref[...]) / TEMPERATURE - along * unit
    key = lax.dot_general(w_pos, e, BY_COLUMN, preferred_element_type=F32)
    pool = lax.dot_general(spread, e, BY_COLUMN, preferred_element_type=F32)
    pool = pool * (POOL_SCALE / TEMPERATURE)
    gain = gain_ref[pl.ds(chip, 1), :]
    gain = jnp.where(core == 0, gain, swap(gain))
    gain_part = jnp.sum(emb_grad * unit, axis=0, keepdims=True) / gain
    gain_high = gain_part.astype(BF16).astype(F32)
    row = lax.broadcasted_iota(jnp.int32, (q, LANES), 0)
    gain_rows = jnp.where(row == 0, gain_high, jnp.where(row == 1, gain_part - gain_high, 0.0))
    e32 = e.astype(F32)
    for d in range(2 * chips):
        k, c = d // 2, d % 2
        rows = slice(k * q, (k + 1) * q)
        mine = core == c
        block = jnp.concatenate(
            [
                jnp.where(mine, emb_grad[rows], 0.0),
                (key[d * q : (d + 1) * q] - jnp.where(mine, e32[rows], 0.0)) / TEMPERATURE,
                pool[2 * d * q : 2 * (d + 1) * q],
                gain_rows,
            ],
            axis=0,
        )
        out_ref[d] = block.astype(BF16)


def gain_kernel(in_ref, out_ref):
    copies, chips, _ = out_ref.shape
    q = in_ref.shape[1] // 5
    for k in range(chips):
        a = in_ref[2 * k].astype(F32)[4 * q : 5 * q]
        b = in_ref[2 * k + 1].astype(F32)[4 * q : 5 * q]
        both = jnp.sum(a + swap(b), axis=0, keepdims=True)
        for r in range(copies):
            out_ref[r, k : k + 1] = both


def backward_kernel(
    me_ref, len_ref, in_ref, x_ref, gain_ref, unit_ref, inv_ref, norm_ref, grad_ref, key_ref, pool_ref, h_ref, row_ref
):
    core = lax.rem(me_ref[0], 2)
    queries, width = unit_ref.shape
    tokens = x_ref.shape[0] // queries
    chunks = width // LANES
    q = queries
    dots = jnp.zeros((q, LANES), F32)
    for k in range(chunks):
        cols = slice(k * LANES, (k + 1) * LANES)
        a = in_ref[2 * k].astype(F32)
        b = in_ref[2 * k + 1].astype(F32)
        b = swap(b)
        both = a + b
        key_ref[:, cols] = both[q : 2 * q]
        pool_ref[:, cols] = both[2 * q : 4 * q]
        g = jnp.where(core == 0, a[:q], b[:q])
        h_ref[:, cols] = g
        dots += g * unit_ref[:, cols]
    along = jnp.sum(dots, axis=1, keepdims=True)
    norm = norm_ref[:, :1]
    for k in range(chunks):
        cols = slice(k * LANES, (k + 1) * LANES)
        h = (h_ref[:, cols] - along * unit_ref[:, cols]) * (norm * gain_ref[:, cols])
        for i in range(q):
            row_ref[i, :, cols] = h[i : i + 1]
    token = lax.broadcasted_iota(jnp.int32, (tokens, 1), 0)

    def one_query(i, carry):
        rows = pl.ds(pl.multiple_of(i * tokens, tokens), tokens)
        length = len_ref[i]
        total = jnp.zeros((tokens, LANES), F32)
        for k in range(chunks):
            cols = slice(k * LANES, (k + 1) * LANES)
            total += x_ref[rows, cols].astype(F32) * row_ref[i, :, cols]
        total = jnp.sum(total, axis=1, keepdims=True)
        inv = inv_ref[rows, :][:, :1]
        scale = jnp.where(token < length, QUERY_SCALE * inv, 0.0) / length.astype(F32)
        back = scale * inv * inv * total / width
        for k in range(chunks):
            cols = slice(k * LANES, (k + 1) * LANES)
            x = x_ref[rows, cols].astype(F32)
            grad_ref[rows, cols] = (scale * row_ref[i, :, cols] - back * x).astype(BF16)
        return carry

    lax.fori_loop(0, queries, one_query, 0)


def call(kernel, outs, args, smem, flops, scratch=()):
    specs = [
        pl.BlockSpec(memory_space=pltpu.SMEM if i in smem else pltpu.VMEM) for i in range(len(args))
    ]
    size = sum(a.size * a.dtype.itemsize for a in args) + sum(
        o.size * o.dtype.itemsize for o in outs
    )
    return pl.pallas_call(
        kernel,
        out_shape=list(outs),
        in_specs=specs,
        out_specs=[pl.BlockSpec(memory_space=pltpu.VMEM)] * len(outs),
        scratch_shapes=list(scratch),
        compiler_params=pltpu.CompilerParams(vmem_limit_bytes=40 * 1024 * 1024),
        cost_estimate=pl.CostEstimate(flops=flops, bytes_accessed=size, transcendentals=0),
    )(*args)


def shape(dims, dtype):
    return jax.ShapeDtypeStruct(dims, dtype)


def local(query_states, query_lengths, norm_gain, positives, mined_pool, hard_ids):
    owners = lax.axis_size("dp")
    groups = lax.axis_size("rep")
    me = lax.axis_index("dp").astype(jnp.int32).reshape(1)
    core = lax.rem(me, 2)
    _, queries, tokens, width = query_states.shape
    hard = hard_ids.shape[2]
    chips = owners // 2
    q_all = queries * owners
    half = q_all // 2
    x = query_states.reshape(queries * tokens, width)
    lengths = query_lengths.reshape(queries)
    gain_row = norm_gain.reshape(1, width)
    gain_tiles = norm_gain.reshape(width // LANES, LANES)
    pair = [(i, i ^ 1) for i in range(owners)]
    same_core = [[2 * i + c for i in range(chips)] for c in range(2)]

    out, unit, inv, norm = call(
        embed_kernel,
        [
            shape((owners, 3 * queries, LANES), BF16),
            shape((queries, width), F32),
            shape((queries * tokens, LANES), F32),
            shape((queries, LANES), F32),
        ],
        [lengths, x, gain_row, positives[0], mined_pool[0], hard_ids[0]],
        (0,),
        8_000_000,
        [pltpu.VMEM((queries * tokens, LANES), F32)],
    )
    got = lax.all_to_all(out, "dp", 0, 0, tiled=True).reshape(chips, 2, 3 * queries, LANES)
    gotx = lax.ppermute(got, "dp", pair)

    def similar(*refs):
        similar_kernel(hard, *refs)

    part, e, unit_f, own, p, m, ids = call(
        similar,
        [
            shape((chips, queries, q_all + LANES), F32),
            shape((half, LANES), BF16),
            shape((half, LANES), F32),
            shape((half, LANES), F32),
            shape((q_all, LANES), BF16),
            shape((2 * q_all, LANES), BF16),
            shape((half, LANES), jnp.int32),
        ],
        [core, got, gotx],
        (0,),
        100_000_000,
    )
    pieces = lax.all_to_all(part, "dp", 0, 0, tiled=True, axis_index_groups=same_core)

    def softmax(*refs):
        softmax_kernel(hard, *refs)

    (sent,) = call(
        softmax, [shape((chips, queries, q_all + LANES), BF16)], [me, pieces], (0,), 1_000_000
    )
    weights = lax.all_to_all(sent, "dp", 0, 0, tiled=True, axis_index_groups=same_core)

    def slices(*refs):
        slices_kernel(hard, *refs)

    (back,) = call(
        slices,
        [shape((owners, 5 * queries, LANES), BF16)],
        [me, weights, e, unit_f, own, p, m, ids, gain_tiles],
        (0,),
        200_000_000,
    )
    home = lax.all_to_all(back, "dp", 0, 0, tiled=True)
    (gain_sent,) = call(
        gain_kernel, [shape((groups, width // LANES, LANES), F32)], [home], (), 100_000
    )
    gain_groups = lax.all_to_all(gain_sent, "rep", 0, 0, tiled=True)
    query_grad, key_grad, pool_grad = call(
        backward_kernel,
        [
            shape((queries * tokens, width), BF16),
            shape((queries, width), F32),
            shape((2 * queries, width), F32),
        ],
        [me, lengths, home, x, gain_row, unit, inv, norm],
        (0, 1),
        10_000_000,
        [pltpu.VMEM((queries, width), F32), pltpu.VMEM((queries, 1, width), F32)],
    )
    gain_grad = jnp.sum(gain_groups, axis=0).reshape(width)
    return (
        query_grad.reshape(query_states.shape),
        key_grad[None],
        pool_grad[None],
        gain_grad,
    )


def solution(mesh):
    placed = (
        P("rep", "dp", None, None),
        P("rep", "dp"),
        P(),
        P("rep", "dp", None),
        P("rep", "dp", None),
        P("rep", "dp", None),
    )
    return jax.shard_map(
        local,
        mesh=mesh,
        in_specs=placed,
        out_specs=(P("rep", "dp", None, None), P("rep", "dp", None), P("rep", "dp", None), P()),
        check_vma=False,
    )
```

```python
import jax
import jax.numpy as jnp
from jax import lax
from jax.experimental import pallas as pl
from jax.experimental.pallas import tpu as pltpu
from jax.sharding import PartitionSpec as P

TEMPERATURE = 0.02
QUERY_SCALE = 512.0
POOL_SCALE = 16.0
LANES = 128
F32 = jnp.float32
BF16 = jnp.bfloat16
BY_COLUMN = (((0,), (0,)), ((), ()))
BY_ROW = (((1,), (1,)), ((), ()))


def embed_kernel(
    core_ref, len_hbm, x_hbm, gain_hbm, pos_hbm, pool_hbm, ids_hbm, out_ref, unit_ref, inv_ref, norm_ref,
    len_ref, x_ref, gain_ref, pos_ref, pool_ref, ids_ref, weight_ref, x_sem, small_sem,
):
    queries, width = unit_ref.shape
    tokens = x_ref.shape[1]
    chunks = width // LANES
    small = [
        pltpu.make_async_copy(src, dst, small_sem.at[n])
        for n, (src, dst) in enumerate(
            [
                (len_hbm, len_ref),
                (gain_hbm, gain_ref),
                (pos_hbm, pos_ref),
                (pool_hbm, pool_ref),
                (ids_hbm, ids_ref),
            ]
        )
    ]
    small[0].start()
    states = [
        pltpu.make_async_copy(x_hbm.at[0, i], x_ref.at[i], x_sem.at[i]) for i in range(queries)
    ]
    for copy in states:
        copy.start()
    for copy in small[1:]:
        copy.start()
    small[0].wait()
    token = lax.broadcasted_iota(jnp.int32, (tokens, 1), 0)

    def one_query(i, carry):
        pltpu.make_async_copy(x_hbm.at[0, i], x_ref.at[i], x_sem.at[i]).wait()
        square = jnp.zeros((tokens, LANES), F32)
        for k in range(chunks):
            v = x_ref[i, :, k * LANES : (k + 1) * LANES].astype(F32)
            square += v * v
        inv = lax.rsqrt(jnp.sum(square, axis=1, keepdims=True) / width + 1e-05)
        inv_ref[i] = jnp.broadcast_to(inv, (tokens, LANES))
        length = len_ref[0, i]
        weight = jnp.where(token < length, inv, 0.0) / length.astype(F32)
        weight_ref[i] = jnp.broadcast_to(weight, (tokens, LANES))
        return carry

    lax.fori_loop(0, queries, one_query, 0)
    for copy in small[1:]:
        copy.wait()
    for k in range(chunks):
        cols = slice(k * LANES, (k + 1) * LANES)
        v = jnp.sum(x_ref[:, :, cols].astype(F32) * weight_ref[...], axis=1)
        unit_ref[:, cols] = v * gain_ref[:, cols]
    pooled = unit_ref[...]
    norm = lax.rsqrt(jnp.sum(pooled * pooled, axis=1, keepdims=True) + 1e-06)
    norm_ref[...] = jnp.broadcast_to(norm, norm_ref.shape)
    ids = ids_ref[0]
    hard = ids.shape[1]
    bits = (2 * queries - 1).bit_length()
    half = chunks * 2 * queries
    owner = ids >> bits
    other = jnp.where((owner & 1) == core_ref[0], 0, half)
    place = other + ((owner >> 1) << bits) + (ids & (2 * queries - 1))
    lane = lax.broadcasted_iota(jnp.int32, (queries, LANES), 1)
    id_rows = jnp.zeros((queries, LANES), jnp.int32)
    for m in range(hard):
        one = place[:, m : m + 1]
        id_rows = jnp.where(lane == m, one >> 5, id_rows)
        id_rows = jnp.where(lane == hard + m, one & 31, id_rows)
    id_rows = id_rows.astype(F32)
    for k in range(chunks):
        cols = slice(k * LANES, (k + 1) * LANES)
        unit = unit_ref[:, cols] * norm
        unit_ref[:, cols] = unit
        rows = [unit, id_rows, pos_ref[0, :, cols].astype(F32), pool_ref[0, :, cols].astype(F32)]
        out_ref[k] = jnp.concatenate(rows, axis=0).astype(BF16)


def rows_of(block, first, last):
    return block[:, first:last].reshape(block.shape[0] * (last - first), LANES)


def ids_of(block, q, hard):
    rows = rows_of(block, q, 2 * q)
    lane = lax.broadcasted_iota(jnp.int32, rows.shape, 1)
    ids = rows * 32.0 + pltpu.roll(rows, LANES - hard, 1)
    return jnp.where(lane < hard, ids, 0.0).astype(jnp.int32)


def similar_kernel(hard, got_ref, gotx_ref, sim_ref):
    chips, rows, _ = got_ref.shape
    q = rows // 5
    half = chips * q
    n = 2 * half
    a = got_ref[...].astype(F32)
    b = gotx_ref[...].astype(F32)
    e = rows_of(a, 0, q).astype(BF16)
    p = jnp.concatenate([rows_of(a, 2 * q, 3 * q), rows_of(b, 2 * q, 3 * q)], axis=0).astype(BF16)
    m = jnp.concatenate([rows_of(a, 3 * q, 5 * q), rows_of(b, 3 * q, 5 * q)], axis=0).astype(BF16)
    ids = ids_of(a, q, hard)
    sim_ref[:, :, :n] = lax.dot_general(e, p, BY_ROW, preferred_element_type=F32).reshape(chips, q, n)
    pool = lax.dot_general(e, m, BY_ROW, preferred_element_type=F32)
    tail = jnp.zeros((half, LANES), F32)
    within, tile = ids & (LANES - 1), ids >> 7
    for k in range(2 * n // LANES):
        picked = jnp.take_along_axis(
            pool[:, k * LANES : (k + 1) * LANES], within, axis=1, mode="promise_in_bounds"
        )
        tail = jnp.where(tile == k, picked, tail)
    lane = lax.broadcasted_iota(jnp.int32, (half, LANES), 1)
    tail = jnp.where(lane < hard, tail, 0.0)
    sim_ref[:, :, n:] = tail.reshape(chips, q, LANES)


def softmax_kernel(hard, chip_ref, in_ref, out_ref):
    copies, q, width = out_ref.shape
    n = width - LANES
    scores = jnp.sum(in_ref[...], axis=0) / TEMPERATURE
    column = lax.broadcasted_iota(jnp.int32, (q, width), 1)
    row = lax.broadcasted_iota(jnp.int32, (q, width), 0)
    exps = jnp.where(column < n + hard, jnp.exp(scores), 0.0)
    soft = exps / jnp.sum(exps, axis=1, keepdims=True)
    own = column == row + chip_ref[0] * q
    along = jnp.sum(soft * scores - jnp.where(own, scores, 0.0), axis=1, keepdims=True)
    high = along.astype(BF16).astype(F32)
    sent = jnp.where(column == n + hard, high, soft)
    sent = jnp.where(column == n + hard + 1, along - high, sent)
    sent = sent.astype(BF16)
    for k in range(copies):
        out_ref[k] = sent


def slices_kernel(hard, chip_ref, w_ref, wx_ref, got_ref, gotx_ref, gain_ref, out_ref):
    chips, q, width = w_ref.shape
    n = width - LANES
    half = chips * q
    w = w_ref[...].astype(F32).reshape(half, width)
    wx = wx_ref[...].astype(F32).reshape(half, width)
    a = got_ref[...].astype(F32)
    b = gotx_ref[...].astype(F32)
    tail = jnp.concatenate([w[:, n:], wx[:, n:]], axis=0)
    from_own = jnp.concatenate([w[:, :half], wx[:, half:n]], axis=0).astype(BF16)
    from_other = jnp.concatenate([w[:, half:n], wx[:, :half]], axis=0).astype(BF16)
    idsx = ids_of(b, q, hard)
    ids = jnp.concatenate([ids_of(a, q, hard), idsx ^ n], axis=0)
    column = lax.broadcasted_iota(jnp.int32, (n, n), 1)
    own_spread = jnp.zeros((n, n), F32)
    other_spread = jnp.zeros((n, n), F32)
    for m in range(hard):
        one, weight = ids[:, m : m + 1], tail[:, m : m + 1]
        own_spread += jnp.where(column == one, weight, 0.0)
        other_spread += jnp.where(column == one - n, weight, 0.0)
    own_spread = own_spread.astype(BF16)
    other_spread = other_spread.astype(BF16)
    along = tail[:, hard : hard + 1] + tail[:, hard + 1 : hard + 2]
    e32 = jnp.concatenate([rows_of(a, 0, q), rows_of(b, 0, q)], axis=0)
    e = e32.astype(BF16)
    own_pos, other_pos = rows_of(a, 2 * q, 3 * q), rows_of(b, 2 * q, 3 * q)

    def dot(left, right):
        return jnp.dot(left, right.astype(BF16), preferred_element_type=F32)

    numerator = dot(from_own, own_pos) + dot(from_other, other_pos)
    numerator += dot(own_spread, rows_of(a, 3 * q, 5 * q))
    numerator += dot(other_spread, rows_of(b, 3 * q, 5 * q))
    pos = jnp.concatenate([own_pos, other_pos], axis=0)
    emb_grad = (numerator - pos) / TEMPERATURE - along * e32
    key = lax.dot_general(from_own, e, BY_COLUMN, preferred_element_type=F32)
    key = (key - e32[:half]) / TEMPERATURE
    pool = lax.dot_general(own_spread, e, BY_COLUMN, preferred_element_type=F32)
    pool = pool * (POOL_SCALE / TEMPERATURE)
    gain = gain_ref[pl.ds(chip_ref[0], 1), :]
    gain_part = jnp.sum(emb_grad * e32, axis=0, keepdims=True) / gain
    gain_high = gain_part.astype(BF16).astype(F32)
    row = lax.broadcasted_iota(jnp.int32, (q, LANES), 0)
    gain_rows = jnp.where(row == 0, gain_high, jnp.where(row == 1, gain_part - gain_high, 0.0))
    for k in range(chips):
        rows = slice(k * q, (k + 1) * q)
        block = [emb_grad[rows], key[rows], pool[2 * k * q : 2 * (k + 1) * q], gain_rows]
        out_ref[k] = jnp.concatenate(block, axis=0).astype(BF16)


def gain_kernel(in_ref, out_ref):
    copies, chips, _ = out_ref.shape
    q = in_ref.shape[1] // 5
    for k in range(chips):
        rows = in_ref[k].astype(F32)[4 * q : 5 * q]
        both = jnp.sum(rows, axis=0, keepdims=True)
        for r in range(copies):
            out_ref[r, k : k + 1] = both


def backward_kernel(
    len_ref, in_ref, x_ref, gain_ref, unit_ref, inv_ref, norm_ref, grad_ref, key_ref, pool_ref, h_ref, row_ref
):
    queries, width = unit_ref.shape
    tokens = x_ref.shape[1]
    chunks = width // LANES
    q = queries
    dots = jnp.zeros((q, LANES), F32)
    for k in range(chunks):
        cols = slice(k * LANES, (k + 1) * LANES)
        block = in_ref[k].astype(F32)
        key_ref[:, cols] = block[q : 2 * q]
        pool_ref[:, cols] = block[2 * q : 4 * q]
        g = block[:q]
        h_ref[:, cols] = g
        dots += g * unit_ref[:, cols]
    along = jnp.sum(dots, axis=1, keepdims=True)
    norm = norm_ref[:, :1]
    for k in range(chunks):
        cols = slice(k * LANES, (k + 1) * LANES)
        h = (h_ref[:, cols] - along * unit_ref[:, cols]) * (norm * gain_ref[:, cols])
        for i in range(q):
            row_ref[i, :, cols] = h[i : i + 1]
    token = lax.broadcasted_iota(jnp.int32, (tokens, 1), 0)

    def one_query(i, carry):
        length = len_ref[i]
        total = jnp.zeros((tokens, LANES), F32)
        for k in range(chunks):
            cols = slice(k * LANES, (k + 1) * LANES)
            total += x_ref[i, :, cols].astype(F32) * row_ref[i, :, cols]
        total = jnp.sum(total, axis=1, keepdims=True)
        inv = inv_ref[i][:, :1]
        scale = jnp.where(token < length, QUERY_SCALE * inv, 0.0) / length.astype(F32)
        back = scale * inv * inv * total / width
        for k in range(chunks):
            cols = slice(k * LANES, (k + 1) * LANES)
            x = x_ref[i, :, cols].astype(F32)
            grad_ref[i, :, cols] = (scale * row_ref[i, :, cols] - back * x).astype(BF16)
        return carry

    lax.fori_loop(0, queries, one_query, 0)


def call(kernel, outs, args, flops, smem=(), hbm=(), scratch=()):
    def space(i):
        return pltpu.SMEM if i in smem else pltpu.HBM if i in hbm else pltpu.VMEM

    size = sum(a.size * a.dtype.itemsize for a in args) + sum(
        o.size * o.dtype.itemsize for o in outs
    )
    return pl.pallas_call(
        kernel,
        out_shape=list(outs),
        in_specs=[pl.BlockSpec(memory_space=space(i)) for i in range(len(args))],
        out_specs=[pl.BlockSpec(memory_space=pltpu.VMEM)] * len(outs),
        scratch_shapes=list(scratch),
        compiler_params=pltpu.CompilerParams(vmem_limit_bytes=40 * 1024 * 1024),
        cost_estimate=pl.CostEstimate(flops=flops, bytes_accessed=size, transcendentals=0),
    )(*args)


def shape(dims, dtype):
    return jax.ShapeDtypeStruct(dims, dtype)


def local(query_states, query_lengths, norm_gain, positives, mined_pool, hard_ids):
    owners = lax.axis_size("dp")
    groups = lax.axis_size("rep")
    me = lax.axis_index("dp").astype(jnp.int32).reshape(1)
    core, chip = lax.rem(me, 2), lax.div(me, 2)
    _, queries, tokens, width = query_states.shape
    hard = hard_ids.shape[2]
    chips = owners // 2
    q_all = queries * owners
    lengths = query_lengths.reshape(queries)
    gain_row = norm_gain.reshape(1, width)
    gain_tiles = norm_gain.reshape(chips, LANES)
    pair = [(i, i ^ 1) for i in range(owners)]
    same_core = [[2 * i + c for i in range(chips)] for c in range(2)]

    def among_chips(x):
        return lax.all_to_all(x, "dp", 0, 0, tiled=True, axis_index_groups=same_core)

    def bound(kernel):
        return lambda *refs: kernel(hard, *refs)

    out, unit, inv, norm = call(
        embed_kernel,
        [
            shape((chips, 5 * queries, LANES), BF16),
            shape((queries, width), F32),
            shape((queries, tokens, LANES), F32),
            shape((queries, LANES), F32),
        ],
        [core, query_lengths, query_states, gain_row, positives, mined_pool, hard_ids],
        8_000_000,
        (0,),
        (1, 2, 3, 4, 5, 6),
        [
            pltpu.SMEM((1, queries), jnp.int32),
            pltpu.VMEM((queries, tokens, width), BF16),
            pltpu.VMEM((1, width), F32),
            pltpu.VMEM((1, queries, width), BF16),
            pltpu.VMEM((1, 2 * queries, width), BF16),
            pltpu.VMEM((1, queries, hard), jnp.int32),
            pltpu.VMEM((queries, tokens, LANES), F32),
            pltpu.SemaphoreType.DMA((queries,)),
            pltpu.SemaphoreType.DMA((5,)),
        ],
    )
    got = among_chips(out)
    gotx = lax.ppermute(got, "dp", pair)

    (part,) = call(
        bound(similar_kernel),
        [shape((chips, queries, q_all + LANES), F32)],
        [got, gotx],
        100_000_000,
    )
    pieces = among_chips(part)
    (sent,) = call(
        bound(softmax_kernel),
        [shape((chips, queries, q_all + LANES), BF16)],
        [chip, pieces],
        1_000_000,
        (0,),
    )
    weights = among_chips(sent)
    weightsx = lax.ppermute(weights, "dp", pair)

    (back,) = call(
        bound(slices_kernel),
        [shape((chips, 5 * queries, LANES), BF16)],
        [chip, weights, weightsx, got, gotx, gain_tiles],
        400_000_000,
        (0,),
    )
    home = among_chips(back)
    (gain_sent,) = call(
        gain_kernel, [shape((groups, width // LANES, LANES), F32)], [home], 100_000
    )
    gain_groups = lax.all_to_all(gain_sent, "rep", 0, 0, tiled=True)
    query_grad, key_grad, pool_grad = call(
        backward_kernel,
        [
            shape((queries, tokens, width), BF16),
            shape((queries, width), F32),
            shape((2 * queries, width), F32),
        ],
        [lengths, home, query_states[0], gain_row, unit, inv, norm],
        10_000_000,
        (0,),
        (),
        [pltpu.VMEM((queries, width), F32), pltpu.VMEM((queries, 1, width), F32)],
    )
    gain_grad = jnp.sum(gain_groups, axis=0).reshape(width)
    return query_grad[None], key_grad[None], pool_grad[None], gain_grad


def solution(mesh):
    placed = (
        P("rep", "dp", None, None),
        P("rep", "dp"),
        P(),
        P("rep", "dp", None),
        P("rep", "dp", None),
        P("rep", "dp", None),
    )
    return jax.shard_map(
        local,
        mesh=mesh,
        in_specs=placed,
        out_specs=(P("rep", "dp", None, None), P("rep", "dp", None), P("rep", "dp", None), P()),
        check_vma=False,
    )
```

```python
import jax
import jax.numpy as jnp
from jax import lax
from jax.experimental import pallas as pl
from jax.experimental.pallas import tpu as pltpu
from jax.sharding import PartitionSpec as P

TEMPERATURE = 0.02
QUERY_SCALE = 512.0
POOL_SCALE = 16.0
LANES = 128
F32 = jnp.float32
BF16 = jnp.bfloat16
BY_COLUMN = (((0,), (0,)), ((), ()))
BY_ROW = (((1,), (1,)), ((), ()))


def embed_kernel(
    core_ref, len_hbm, x_hbm, gain_hbm, pos_hbm, pool_hbm, ids_hbm, out_ref, unit_ref, inv_ref, norm_ref,
    len_ref, x_ref, gain_ref, pos_ref, pool_ref, ids_ref, weight_ref, x_sem, small_sem,
):
    queries, width = unit_ref.shape
    tokens = x_ref.shape[1]
    chunks = width // LANES
    small = [
        pltpu.make_async_copy(src, dst, small_sem.at[n])
        for n, (src, dst) in enumerate(
            [
                (len_hbm, len_ref),
                (gain_hbm, gain_ref),
                (pos_hbm, pos_ref),
                (pool_hbm, pool_ref),
                (ids_hbm, ids_ref),
            ]
        )
    ]
    small[0].start()
    states = [
        pltpu.make_async_copy(x_hbm.at[0, i], x_ref.at[i], x_sem.at[i]) for i in range(queries)
    ]
    for copy in states:
        copy.start()
    for copy in small[1:]:
        copy.start()
    small[0].wait()
    token = lax.broadcasted_iota(jnp.int32, (tokens, 1), 0)

    def one_query(i, carry):
        pltpu.make_async_copy(x_hbm.at[0, i], x_ref.at[i], x_sem.at[i]).wait()
        square = jnp.zeros((tokens, LANES), F32)
        for k in range(chunks):
            v = x_ref[i, :, k * LANES : (k + 1) * LANES].astype(F32)
            square += v * v
        inv = lax.rsqrt(jnp.sum(square, axis=1, keepdims=True) / width + 1e-05)
        inv_ref[i] = jnp.broadcast_to(inv, (tokens, LANES))
        length = len_ref[0, i]
        weight = jnp.where(token < length, inv, 0.0) / length.astype(F32)
        weight_ref[i] = jnp.broadcast_to(weight, (tokens, LANES))
        return carry

    lax.fori_loop(0, queries, one_query, 0)
    for copy in small[1:]:
        copy.wait()
    for k in range(chunks):
        cols = slice(k * LANES, (k + 1) * LANES)
        v = jnp.sum(x_ref[:, :, cols].astype(F32) * weight_ref[...], axis=1)
        unit_ref[:, cols] = v * gain_ref[:, cols]
    pooled = unit_ref[...]
    norm = lax.rsqrt(jnp.sum(pooled * pooled, axis=1, keepdims=True) + 1e-06)
    norm_ref[...] = jnp.broadcast_to(norm, norm_ref.shape)
    ids = ids_ref[:, 0, :]
    hard = ids.shape[0]
    bits = (2 * queries - 1).bit_length()
    half = chunks * 2 * queries
    owner = ids >> bits
    other = jnp.where((owner & 1) == core_ref[0], 0, half)
    place = other + ((owner >> 1) << bits) + (ids & (2 * queries - 1))
    row = lax.broadcasted_iota(jnp.int32, (hard, LANES), 0)
    lane = lax.broadcasted_iota(jnp.int32, (hard, LANES), 1)

    def lay(x, first):
        to = (lane == row + first).astype(F32).astype(BF16)
        return lax.dot_general(
            x.astype(F32).astype(BF16), to, BY_COLUMN, preferred_element_type=F32
        )

    id_rows = lay(place >> 5, 0) + lay(place & 31, hard)
    for k in range(chunks):
        cols = slice(k * LANES, (k + 1) * LANES)
        unit = unit_ref[:, cols] * norm
        unit_ref[:, cols] = unit
        rows = [unit, id_rows, pos_ref[0, :, cols].astype(F32), pool_ref[0, :, cols].astype(F32)]
        out_ref[k] = jnp.concatenate(rows, axis=0).astype(BF16)


def rows_of(block, first, last):
    return block[:, first:last].reshape(block.shape[0] * (last - first), LANES)


def ids_of(block, q, hard):
    rows = rows_of(block, q, 2 * q)
    lane = lax.broadcasted_iota(jnp.int32, rows.shape, 1)
    ids = rows * 32.0 + pltpu.roll(rows, LANES - hard, 1)
    return jnp.where(lane < hard, ids, 0.0).astype(jnp.int32)


def similar_kernel(hard, got_ref, gotx_ref, sim_ref):
    chips, rows, _ = got_ref.shape
    q = rows // 5
    half = chips * q
    n = 2 * half
    a = got_ref[...].astype(F32)
    b = gotx_ref[...].astype(F32)
    e = rows_of(a, 0, q).astype(BF16)
    p = jnp.concatenate([rows_of(a, 2 * q, 3 * q), rows_of(b, 2 * q, 3 * q)], axis=0).astype(BF16)
    m = jnp.concatenate([rows_of(a, 3 * q, 5 * q), rows_of(b, 3 * q, 5 * q)], axis=0).astype(BF16)
    ids = ids_of(a, q, hard)
    sim_ref[:, :, :n] = lax.dot_general(e, p, BY_ROW, preferred_element_type=F32).reshape(chips, q, n)
    pool = lax.dot_general(e, m, BY_ROW, preferred_element_type=F32)
    tail = jnp.zeros((half, LANES), F32)
    within, tile = ids & (LANES - 1), ids >> 7
    for k in range(2 * n // LANES):
        picked = jnp.take_along_axis(
            pool[:, k * LANES : (k + 1) * LANES], within, axis=1, mode="promise_in_bounds"
        )
        tail = jnp.where(tile == k, picked, tail)
    lane = lax.broadcasted_iota(jnp.int32, (half, LANES), 1)
    tail = jnp.where(lane < hard, tail, 0.0)
    sim_ref[:, :, n:] = tail.reshape(chips, q, LANES)


def softmax_kernel(hard, chip_ref, in_ref, out_ref):
    copies, q, width = out_ref.shape
    n = width - LANES
    scores = jnp.sum(in_ref[...], axis=0) / TEMPERATURE
    column = lax.broadcasted_iota(jnp.int32, (q, width), 1)
    row = lax.broadcasted_iota(jnp.int32, (q, width), 0)
    exps = jnp.where(column < n + hard, jnp.exp(scores), 0.0)
    soft = exps / jnp.sum(exps, axis=1, keepdims=True)
    own = column == row + chip_ref[0] * q
    along = jnp.sum(soft * scores - jnp.where(own, scores, 0.0), axis=1, keepdims=True)
    high = along.astype(BF16).astype(F32)
    sent = jnp.where(column == n + hard, high, soft)
    sent = jnp.where(column == n + hard + 1, along - high, sent)
    sent = sent.astype(BF16)
    for k in range(copies):
        out_ref[k] = sent


def slices_kernel(hard, chip_ref, w_ref, wx_ref, got_ref, gotx_ref, gain_ref, out_ref):
    chips, q, width = w_ref.shape
    n = width - LANES
    half = chips * q
    w = w_ref[...].astype(F32).reshape(half, width)
    wx = wx_ref[...].astype(F32).reshape(half, width)
    a = got_ref[...].astype(F32)
    b = gotx_ref[...].astype(F32)
    tail = jnp.concatenate([w[:, n:], wx[:, n:]], axis=0)
    from_own = jnp.concatenate([w[:, :half], wx[:, half:n]], axis=0).astype(BF16)
    from_other = jnp.concatenate([w[:, half:n], wx[:, :half]], axis=0).astype(BF16)
    idsx = ids_of(b, q, hard)
    ids = jnp.concatenate([ids_of(a, q, hard), idsx ^ n], axis=0)
    column = lax.broadcasted_iota(jnp.int32, (n, n), 1)
    own_spread = jnp.zeros((n, n), F32)
    other_spread = jnp.zeros((n, n), F32)
    for m in range(hard):
        one, weight = ids[:, m : m + 1], tail[:, m : m + 1]
        own_spread += jnp.where(column == one, weight, 0.0)
        other_spread += jnp.where(column == one - n, weight, 0.0)
    own_spread = own_spread.astype(BF16)
    other_spread = other_spread.astype(BF16)
    along = tail[:, hard : hard + 1] + tail[:, hard + 1 : hard + 2]
    e32 = jnp.concatenate([rows_of(a, 0, q), rows_of(b, 0, q)], axis=0)
    e = e32.astype(BF16)
    own_pos, other_pos = rows_of(a, 2 * q, 3 * q), rows_of(b, 2 * q, 3 * q)

    def dot(left, right):
        return jnp.dot(left, right.astype(BF16), preferred_element_type=F32)

    numerator = dot(from_own, own_pos) + dot(from_other, other_pos)
    numerator += dot(own_spread, rows_of(a, 3 * q, 5 * q))
    numerator += dot(other_spread, rows_of(b, 3 * q, 5 * q))
    pos = jnp.concatenate([own_pos, other_pos], axis=0)
    emb_grad = (numerator - pos) / TEMPERATURE - along * e32
    key = lax.dot_general(from_own, e, BY_COLUMN, preferred_element_type=F32)
    key = (key - e32[:half]) / TEMPERATURE
    pool = lax.dot_general(own_spread, e, BY_COLUMN, preferred_element_type=F32)
    pool = pool * (POOL_SCALE / TEMPERATURE)
    gain = gain_ref[pl.ds(chip_ref[0], 1), :]
    gain_part = jnp.sum(emb_grad * e32, axis=0, keepdims=True) / gain
    gain_high = gain_part.astype(BF16).astype(F32)
    row = lax.broadcasted_iota(jnp.int32, (q, LANES), 0)
    gain_rows = jnp.where(row == 0, gain_high, jnp.where(row == 1, gain_part - gain_high, 0.0))
    for k in range(chips):
        rows = slice(k * q, (k + 1) * q)
        block = [emb_grad[rows], key[rows], pool[2 * k * q : 2 * (k + 1) * q], gain_rows]
        out_ref[k] = jnp.concatenate(block, axis=0).astype(BF16)


def gain_kernel(in_ref, out_ref):
    copies, chips, _ = out_ref.shape
    q = in_ref.shape[1] // 5
    for k in range(chips):
        rows = in_ref[k].astype(F32)[4 * q : 5 * q]
        both = jnp.sum(rows, axis=0, keepdims=True)
        for r in range(copies):
            out_ref[r, k : k + 1] = both


def backward_kernel(
    len_ref, in_ref, x_ref, gain_ref, unit_ref, inv_ref, norm_ref, grad_ref, key_ref, pool_ref, h_ref, row_ref
):
    queries, width = unit_ref.shape
    tokens = x_ref.shape[1]
    chunks = width // LANES
    q = queries
    dots = jnp.zeros((q, LANES), F32)
    for k in range(chunks):
        cols = slice(k * LANES, (k + 1) * LANES)
        block = in_ref[k].astype(F32)
        key_ref[:, cols] = block[q : 2 * q]
        pool_ref[:, cols] = block[2 * q : 4 * q]
        g = block[:q]
        h_ref[:, cols] = g
        dots += g * unit_ref[:, cols]
    along = jnp.sum(dots, axis=1, keepdims=True)
    norm = norm_ref[:, :1]
    for k in range(chunks):
        cols = slice(k * LANES, (k + 1) * LANES)
        h = (h_ref[:, cols] - along * unit_ref[:, cols]) * (norm * gain_ref[:, cols])
        for i in range(q):
            row_ref[i, :, cols] = h[i : i + 1]
    token = lax.broadcasted_iota(jnp.int32, (tokens, 1), 0)

    def one_query(i, carry):
        length = len_ref[i]
        total = jnp.zeros((tokens, LANES), F32)
        for k in range(chunks):
            cols = slice(k * LANES, (k + 1) * LANES)
            total += x_ref[i, :, cols].astype(F32) * row_ref[i, :, cols]
        total = jnp.sum(total, axis=1, keepdims=True)
        inv = inv_ref[i][:, :1]
        scale = jnp.where(token < length, QUERY_SCALE * inv, 0.0) / length.astype(F32)
        back = scale * inv * inv * total / width
        for k in range(chunks):
            cols = slice(k * LANES, (k + 1) * LANES)
            x = x_ref[i, :, cols].astype(F32)
            grad_ref[i, :, cols] = (scale * row_ref[i, :, cols] - back * x).astype(BF16)
        return carry

    lax.fori_loop(0, queries, one_query, 0)


def call(kernel, outs, args, flops, smem=(), hbm=(), scratch=(), vmem=40):
    def space(i):
        return pltpu.SMEM if i in smem else pltpu.HBM if i in hbm else pltpu.VMEM

    size = sum(a.size * a.dtype.itemsize for a in args) + sum(
        o.size * o.dtype.itemsize for o in outs
    )
    return pl.pallas_call(
        kernel,
        out_shape=list(outs),
        in_specs=[pl.BlockSpec(memory_space=space(i)) for i in range(len(args))],
        out_specs=[pl.BlockSpec(memory_space=pltpu.VMEM)] * len(outs),
        scratch_shapes=list(scratch),
        compiler_params=pltpu.CompilerParams(vmem_limit_bytes=vmem * 1024 * 1024),
        cost_estimate=pl.CostEstimate(flops=flops, bytes_accessed=size, transcendentals=0),
    )(*args)


def shape(dims, dtype):
    return jax.ShapeDtypeStruct(dims, dtype)


def local(query_states, query_lengths, norm_gain, positives, mined_pool, hard_ids):
    owners = lax.axis_size("dp")
    groups = lax.axis_size("rep")
    me = lax.axis_index("dp").astype(jnp.int32).reshape(1)
    core, chip = lax.rem(me, 2), lax.div(me, 2)
    _, queries, tokens, width = query_states.shape
    hard = hard_ids.shape[2]
    chips = owners // 2
    q_all = queries * owners
    lengths = query_lengths.reshape(queries)
    gain_row = norm_gain.reshape(1, width)
    gain_tiles = norm_gain.reshape(chips, LANES)
    pair = [(i, i ^ 1) for i in range(owners)]
    same_core = [[2 * i + c for i in range(chips)] for c in range(2)]

    def among_chips(x):
        return lax.all_to_all(x, "dp", 0, 0, tiled=True, axis_index_groups=same_core)

    def bound(kernel):
        return lambda *refs: kernel(hard, *refs)

    out, unit, inv, norm = call(
        embed_kernel,
        [
            shape((chips, 5 * queries, LANES), BF16),
            shape((queries, width), F32),
            shape((queries, tokens, LANES), F32),
            shape((queries, LANES), F32),
        ],
        [core, query_lengths, query_states, gain_row, positives, mined_pool, hard_ids.transpose(2, 0, 1)],
        8_000_000,
        (0,),
        (1, 2, 3, 4, 5, 6),
        [
            pltpu.SMEM((1, queries), jnp.int32),
            pltpu.VMEM((queries, tokens, width), BF16),
            pltpu.VMEM((1, width), F32),
            pltpu.VMEM((1, queries, width), BF16),
            pltpu.VMEM((1, 2 * queries, width), BF16),
            pltpu.VMEM((hard, 1, queries), jnp.int32),
            pltpu.VMEM((queries, tokens, LANES), F32),
            pltpu.SemaphoreType.DMA((queries,)),
            pltpu.SemaphoreType.DMA((5,)),
        ],
        60,
    )
    got = among_chips(out)
    gotx = lax.ppermute(got, "dp", pair)

    (part,) = call(
        bound(similar_kernel),
        [shape((chips, queries, q_all + LANES), F32)],
        [got, gotx],
        100_000_000,
    )
    pieces = among_chips(part)
    (sent,) = call(
        bound(softmax_kernel),
        [shape((chips, queries, q_all + LANES), BF16)],
        [chip, pieces],
        1_000_000,
        (0,),
    )
    weights = among_chips(sent)
    weightsx = lax.ppermute(weights, "dp", pair)

    (back,) = call(
        bound(slices_kernel),
        [shape((chips, 5 * queries, LANES), BF16)],
        [chip, weights, weightsx, got, gotx, gain_tiles],
        400_000_000,
        (0,),
    )
    home = among_chips(back)
    (gain_sent,) = call(
        gain_kernel, [shape((groups, width // LANES, LANES), F32)], [home], 100_000
    )
    gain_groups = lax.all_to_all(gain_sent, "rep", 0, 0, tiled=True)
    query_grad, key_grad, pool_grad = call(
        backward_kernel,
        [
            shape((queries, tokens, width), BF16),
            shape((queries, width), F32),
            shape((2 * queries, width), F32),
        ],
        [lengths, home, query_states[0], gain_row, unit, inv, norm],
        10_000_000,
        (0,),
        (),
        [pltpu.VMEM((queries, width), F32), pltpu.VMEM((queries, 1, width), F32)],
    )
    gain_grad = jnp.sum(gain_groups, axis=0).reshape(width)
    return query_grad[None], key_grad[None], pool_grad[None], gain_grad


def solution(mesh):
    placed = (
        P("rep", "dp", None, None),
        P("rep", "dp"),
        P(),
        P("rep", "dp", None),
        P("rep", "dp", None),
        P("rep", "dp", None),
    )
    return jax.shard_map(
        local,
        mesh=mesh,
        in_specs=placed,
        out_specs=(P("rep", "dp", None, None), P("rep", "dp", None), P("rep", "dp", None), P()),
        check_vma=False,
    )
```

```python
import jax
import jax.numpy as jnp
from jax import lax
from jax.experimental import pallas as pl
from jax.experimental.pallas import tpu as pltpu
from jax.sharding import PartitionSpec as P

TEMPERATURE = 0.02
QUERY_SCALE = 512.0
POOL_SCALE = 16.0
LANES = 128
F32 = jnp.float32
BF16 = jnp.bfloat16
F16 = jnp.float16
BY_COLUMN = (((0,), (0,)), ((), ()))
BY_ROW = (((1,), (1,)), ((), ()))


def embed_kernel(
    core_ref, len_hbm, x_hbm, gain_hbm, pos_hbm, pool_hbm, ids_hbm, out_ref, unit_ref, inv_ref, norm_ref,
    len_ref, x_ref, gain_ref, pos_ref, pool_ref, ids_ref, weight_ref, x_sem, small_sem,
):
    queries, width = unit_ref.shape
    tokens = x_ref.shape[1]
    chunks = width // LANES
    small = [
        pltpu.make_async_copy(src, dst, small_sem.at[n])
        for n, (src, dst) in enumerate(
            [
                (len_hbm, len_ref),
                (gain_hbm, gain_ref),
                (pos_hbm, pos_ref),
                (pool_hbm, pool_ref),
                (ids_hbm, ids_ref),
            ]
        )
    ]
    small[0].start()
    states = [
        pltpu.make_async_copy(x_hbm.at[0, i], x_ref.at[i], x_sem.at[i]) for i in range(queries)
    ]
    for copy in states:
        copy.start()
    for copy in small[1:]:
        copy.start()
    small[0].wait()
    token = lax.broadcasted_iota(jnp.int32, (tokens, 1), 0)

    def one_query(i, carry):
        pltpu.make_async_copy(x_hbm.at[0, i], x_ref.at[i], x_sem.at[i]).wait()
        square = jnp.zeros((tokens, LANES), F32)
        for k in range(chunks):
            v = x_ref[i, :, k * LANES : (k + 1) * LANES].astype(F32)
            square += v * v
        inv = lax.rsqrt(jnp.sum(square, axis=1, keepdims=True) / width + 1e-05)
        inv_ref[i] = jnp.broadcast_to(inv, (tokens, LANES))
        length = len_ref[0, i]
        weight = jnp.where(token < length, inv, 0.0) / length.astype(F32)
        weight_ref[i] = jnp.broadcast_to(weight, (tokens, LANES))
        return carry

    lax.fori_loop(0, queries, one_query, 0)
    for copy in small[1:]:
        copy.wait()
    for k in range(chunks):
        cols = slice(k * LANES, (k + 1) * LANES)
        v = jnp.sum(x_ref[:, :, cols].astype(F32) * weight_ref[...], axis=1)
        unit_ref[:, cols] = v * gain_ref[:, cols]
    pooled = unit_ref[...]
    norm = lax.rsqrt(jnp.sum(pooled * pooled, axis=1, keepdims=True) + 1e-06)
    norm_ref[...] = jnp.broadcast_to(norm, norm_ref.shape)
    ids = ids_ref[:, 0, :]
    hard = ids.shape[0]
    bits = (2 * queries - 1).bit_length()
    half = chunks * 2 * queries
    owner = ids >> bits
    other = jnp.where((owner & 1) == core_ref[0], 0, half)
    place = other + ((owner >> 1) << bits) + (ids & (2 * queries - 1))
    row = lax.broadcasted_iota(jnp.int32, (hard, LANES), 0)
    lane = lax.broadcasted_iota(jnp.int32, (hard, LANES), 1)

    def lay(x, first):
        to = (lane == row + first).astype(F32).astype(BF16)
        return lax.dot_general(
            x.astype(F32).astype(BF16), to, BY_COLUMN, preferred_element_type=F32
        )

    id_rows = lay(place >> 5, 0) + lay(place & 31, hard)
    for k in range(chunks):
        cols = slice(k * LANES, (k + 1) * LANES)
        unit = unit_ref[:, cols] * norm
        unit_ref[:, cols] = unit
        rows = [unit, id_rows, pos_ref[0, :, cols].astype(F32), pool_ref[0, :, cols].astype(F32)]
        out_ref[k] = jnp.concatenate(rows, axis=0).astype(BF16)


def rows_of(block, first, last):
    return block[:, first:last].reshape(block.shape[0] * (last - first), LANES)


def ids_of(block, q, hard):
    rows = rows_of(block, q, 2 * q)
    lane = lax.broadcasted_iota(jnp.int32, rows.shape, 1)
    ids = rows * 32.0 + pltpu.roll(rows, LANES - hard, 1)
    return jnp.where(lane < hard, ids, 0.0).astype(jnp.int32)


def similar_kernel(hard, got_ref, gotx_ref, sim_ref):
    chips, rows, _ = got_ref.shape
    q = rows // 5
    half = chips * q
    n = 2 * half
    a = got_ref[...].astype(F32)
    b = gotx_ref[...].astype(F32)
    e = rows_of(a, 0, q).astype(BF16)
    p = jnp.concatenate([rows_of(a, 2 * q, 3 * q), rows_of(b, 2 * q, 3 * q)], axis=0).astype(BF16)
    m = jnp.concatenate([rows_of(a, 3 * q, 5 * q), rows_of(b, 3 * q, 5 * q)], axis=0).astype(BF16)
    ids = ids_of(a, q, hard)
    sim = lax.dot_general(e, p, BY_ROW, preferred_element_type=F32) / TEMPERATURE
    sim_ref[:, :, :n] = sim.reshape(chips, q, n)
    pool = lax.dot_general(e, m, BY_ROW, preferred_element_type=F32)
    tail = jnp.zeros((half, LANES), F32)
    within, tile = ids & (LANES - 1), ids >> 7
    for k in range(2 * n // LANES):
        picked = jnp.take_along_axis(
            pool[:, k * LANES : (k + 1) * LANES], within, axis=1, mode="promise_in_bounds"
        )
        tail = jnp.where(tile == k, picked, tail)
    lane = lax.broadcasted_iota(jnp.int32, (half, LANES), 1)
    tail = jnp.where(lane < hard, tail / TEMPERATURE, 0.0)
    sim_ref[:, :, n:] = tail.reshape(chips, q, LANES)


def softmax_kernel(hard, chip_ref, in_ref, out_ref):
    copies, q, width = out_ref.shape
    n = width - LANES
    scores = in_ref[...]
    column = lax.broadcasted_iota(jnp.int32, (q, width), 1)
    row = lax.broadcasted_iota(jnp.int32, (q, width), 0)
    exps = jnp.where(column < n + hard, jnp.exp(scores), 0.0)
    soft = exps / jnp.sum(exps, axis=1, keepdims=True)
    own = column == row + chip_ref[0] * q
    along = jnp.sum(soft * scores - jnp.where(own, scores, 0.0), axis=1, keepdims=True)
    high = along.astype(BF16).astype(F32)
    sent = jnp.where(column == n + hard, high, soft)
    sent = jnp.where(column == n + hard + 1, along - high, sent)
    sent = sent.astype(BF16)
    for k in range(copies):
        out_ref[k] = sent


def slices_kernel(hard, chip_ref, w_ref, wx_ref, got_ref, gotx_ref, gain_ref, out_ref):
    chips, q, width = w_ref.shape
    n = width - LANES
    half = chips * q
    w = w_ref[...].astype(F32).reshape(half, width)
    wx = wx_ref[...].astype(F32).reshape(half, width)
    a = got_ref[...].astype(F32)
    b = gotx_ref[...].astype(F32)
    tail = jnp.concatenate([w[:, n:], wx[:, n:]], axis=0)
    from_own = jnp.concatenate([w[:, :half], wx[:, half:n]], axis=0).astype(BF16)
    from_other = jnp.concatenate([w[:, half:n], wx[:, :half]], axis=0).astype(BF16)
    idsx = ids_of(b, q, hard)
    ids = jnp.concatenate([ids_of(a, q, hard), idsx ^ n], axis=0)
    column = lax.broadcasted_iota(jnp.int32, (n, n), 1)
    own_spread = jnp.zeros((n, n), F32)
    other_spread = jnp.zeros((n, n), F32)
    for m in range(hard):
        one, weight = ids[:, m : m + 1], tail[:, m : m + 1]
        own_spread += jnp.where(column == one, weight, 0.0)
        other_spread += jnp.where(column == one - n, weight, 0.0)
    own_spread = own_spread.astype(BF16)
    other_spread = other_spread.astype(BF16)
    along = tail[:, hard : hard + 1] + tail[:, hard + 1 : hard + 2]
    e32 = jnp.concatenate([rows_of(a, 0, q), rows_of(b, 0, q)], axis=0)
    e = e32.astype(BF16)
    own_pos, other_pos = rows_of(a, 2 * q, 3 * q), rows_of(b, 2 * q, 3 * q)

    def dot(left, right):
        return jnp.dot(left, right.astype(BF16), preferred_element_type=F32)

    numerator = dot(from_own, own_pos) + dot(from_other, other_pos)
    numerator += dot(own_spread, rows_of(a, 3 * q, 5 * q))
    numerator += dot(other_spread, rows_of(b, 3 * q, 5 * q))
    pos = jnp.concatenate([own_pos, other_pos], axis=0)
    emb_grad = (numerator - pos) / TEMPERATURE - along * e32
    key = lax.dot_general(from_own, e, BY_COLUMN, preferred_element_type=F32)
    key = (key - e32[:half]) / TEMPERATURE
    pool = lax.dot_general(own_spread, e, BY_COLUMN, preferred_element_type=F32)
    pool = pool * (POOL_SCALE / TEMPERATURE)
    gain = gain_ref[pl.ds(chip_ref[0], 1), :]
    gain_part = jnp.sum(emb_grad * e32, axis=0, keepdims=True) / gain
    gain_high = gain_part.astype(BF16).astype(F32)
    row = lax.broadcasted_iota(jnp.int32, (q, LANES), 0)
    gain_rows = jnp.where(row == 0, gain_high, jnp.where(row == 1, gain_part - gain_high, 0.0))
    for k in range(chips):
        rows = slice(k * q, (k + 1) * q)
        block = [emb_grad[rows], key[rows], pool[2 * k * q : 2 * (k + 1) * q], gain_rows]
        out_ref[k] = jnp.concatenate(block, axis=0).astype(BF16)


def gain_kernel(in_ref, out_ref):
    copies, chips, _ = out_ref.shape
    q = in_ref.shape[1] // 5
    for k in range(chips):
        rows = in_ref[k].astype(F32)[4 * q : 5 * q]
        both = jnp.sum(rows, axis=0, keepdims=True)
        for r in range(copies):
            out_ref[r, k : k + 1] = both


def backward_kernel(
    len_ref, in_ref, x_ref, gain_ref, unit_ref, inv_ref, norm_ref, grad_ref, key_ref, pool_ref, h_ref, row_ref
):
    queries, width = unit_ref.shape
    tokens = x_ref.shape[1]
    chunks = width // LANES
    q = queries
    dots = jnp.zeros((q, LANES), F32)
    for k in range(chunks):
        cols = slice(k * LANES, (k + 1) * LANES)
        block = in_ref[k].astype(F32)
        key_ref[:, cols] = block[q : 2 * q]
        pool_ref[:, cols] = block[2 * q : 4 * q]
        g = block[:q]
        h_ref[:, cols] = g
        dots += g * unit_ref[:, cols]
    along = jnp.sum(dots, axis=1, keepdims=True)
    norm = norm_ref[:, :1]
    for k in range(chunks):
        cols = slice(k * LANES, (k + 1) * LANES)
        h = (h_ref[:, cols] - along * unit_ref[:, cols]) * (norm * gain_ref[:, cols])
        for i in range(q):
            row_ref[i, :, cols] = h[i : i + 1]
    token = lax.broadcasted_iota(jnp.int32, (tokens, 1), 0)

    def one_query(i, carry):
        length = len_ref[i]
        total = jnp.zeros((tokens, LANES), F32)
        for k in range(chunks):
            cols = slice(k * LANES, (k + 1) * LANES)
            total += x_ref[i, :, cols].astype(F32) * row_ref[i, :, cols]
        total = jnp.sum(total, axis=1, keepdims=True)
        inv = inv_ref[i][:, :1]
        scale = jnp.where(token < length, QUERY_SCALE * inv, 0.0) / length.astype(F32)
        back = scale * inv * inv * total / width
        for k in range(chunks):
            cols = slice(k * LANES, (k + 1) * LANES)
            x = x_ref[i, :, cols].astype(F32)
            grad_ref[i, :, cols] = (scale * row_ref[i, :, cols] - back * x).astype(BF16)
        return carry

    lax.fori_loop(0, queries, one_query, 0)


def call(kernel, outs, args, flops, smem=(), hbm=(), scratch=(), vmem=40):
    def space(i):
        return pltpu.SMEM if i in smem else pltpu.HBM if i in hbm else pltpu.VMEM

    size = sum(a.size * a.dtype.itemsize for a in args) + sum(
        o.size * o.dtype.itemsize for o in outs
    )
    return pl.pallas_call(
        kernel,
        out_shape=list(outs),
        in_specs=[pl.BlockSpec(memory_space=space(i)) for i in range(len(args))],
        out_specs=[pl.BlockSpec(memory_space=pltpu.VMEM)] * len(outs),
        scratch_shapes=list(scratch),
        compiler_params=pltpu.CompilerParams(vmem_limit_bytes=vmem * 1024 * 1024),
        cost_estimate=pl.CostEstimate(flops=flops, bytes_accessed=size, transcendentals=0),
    )(*args)


def shape(dims, dtype):
    return jax.ShapeDtypeStruct(dims, dtype)


def local(query_states, query_lengths, norm_gain, positives, mined_pool, hard_ids):
    owners = lax.axis_size("dp")
    groups = lax.axis_size("rep")
    me = lax.axis_index("dp").astype(jnp.int32).reshape(1)
    core, chip = lax.rem(me, 2), lax.div(me, 2)
    _, queries, tokens, width = query_states.shape
    hard = hard_ids.shape[2]
    chips = owners // 2
    q_all = queries * owners
    lengths = query_lengths.reshape(queries)
    gain_row = norm_gain.reshape(1, width)
    gain_tiles = norm_gain.reshape(chips, LANES)
    pair = [(i, i ^ 1) for i in range(owners)]
    same_core = [[2 * i + c for i in range(chips)] for c in range(2)]

    def among_chips(x):
        return lax.all_to_all(x, "dp", 0, 0, tiled=True, axis_index_groups=same_core)

    def bound(kernel):
        return lambda *refs: kernel(hard, *refs)

    out, unit, inv, norm = call(
        embed_kernel,
        [
            shape((chips, 5 * queries, LANES), BF16),
            shape((queries, width), F32),
            shape((queries, tokens, LANES), F32),
            shape((queries, LANES), F32),
        ],
        [core, query_lengths, query_states, gain_row, positives, mined_pool, hard_ids.transpose(2, 0, 1)],
        8_000_000,
        (0,),
        (1, 2, 3, 4, 5, 6),
        [
            pltpu.SMEM((1, queries), jnp.int32),
            pltpu.VMEM((queries, tokens, width), BF16),
            pltpu.VMEM((1, width), F32),
            pltpu.VMEM((1, queries, width), BF16),
            pltpu.VMEM((1, 2 * queries, width), BF16),
            pltpu.VMEM((hard, 1, queries), jnp.int32),
            pltpu.VMEM((queries, tokens, LANES), F32),
            pltpu.SemaphoreType.DMA((queries,)),
            pltpu.SemaphoreType.DMA((5,)),
        ],
        60,
    )
    got = among_chips(out)
    gotx = lax.ppermute(got, "dp", pair)

    (part,) = call(
        bound(similar_kernel),
        [shape((chips, queries, q_all + LANES), F32)],
        [got, gotx],
        100_000_000,
    )
    scores = jnp.sum(among_chips(part.astype(F16)).astype(F32), axis=0)
    (sent,) = call(
        bound(softmax_kernel),
        [shape((chips, queries, q_all + LANES), BF16)],
        [chip, scores],
        1_000_000,
        (0,),
    )
    weights = among_chips(sent)
    weightsx = lax.ppermute(weights, "dp", pair)

    (back,) = call(
        bound(slices_kernel),
        [shape((chips, 5 * queries, LANES), BF16)],
        [chip, weights, weightsx, got, gotx, gain_tiles],
        400_000_000,
        (0,),
    )
    home = among_chips(back)
    (gain_sent,) = call(
        gain_kernel, [shape((groups, width // LANES, LANES), F32)], [home], 100_000
    )
    gain_groups = lax.all_to_all(gain_sent, "rep", 0, 0, tiled=True)
    query_grad, key_grad, pool_grad = call(
        backward_kernel,
        [
            shape((queries, tokens, width), BF16),
            shape((queries, width), F32),
            shape((2 * queries, width), F32),
        ],
        [lengths, home, query_states[0], gain_row, unit, inv, norm],
        10_000_000,
        (0,),
        (),
        [pltpu.VMEM((queries, width), F32), pltpu.VMEM((queries, 1, width), F32)],
    )
    gain_grad = jnp.sum(gain_groups, axis=0).reshape(width)
    return query_grad[None], key_grad[None], pool_grad[None], gain_grad


def solution(mesh):
    placed = (
        P("rep", "dp", None, None),
        P("rep", "dp"),
        P(),
        P("rep", "dp", None),
        P("rep", "dp", None),
        P("rep", "dp", None),
    )
    return jax.shard_map(
        local,
        mesh=mesh,
        in_specs=placed,
        out_specs=(P("rep", "dp", None, None), P("rep", "dp", None), P("rep", "dp", None), P()),
        check_vma=False,
    )
```

```python
import jax
import jax.numpy as jnp
from jax import lax
from jax.experimental import pallas as pl
from jax.experimental.pallas import tpu as pltpu
from jax.sharding import PartitionSpec as P

TEMPERATURE = 0.02
QUERY_SCALE = 512.0
POOL_SCALE = 16.0
LANES = 128
F32 = jnp.float32
BF16 = jnp.bfloat16
F16 = jnp.float16
BY_COLUMN = (((0,), (0,)), ((), ()))
BY_ROW = (((1,), (1,)), ((), ()))


def embed_kernel(
    core_ref, len_hbm, x_hbm, gain_hbm, pos_hbm, pool_hbm, ids_hbm, out_ref, unit_ref, inv_ref, norm_ref,
    len_ref, x_ref, gain_ref, pos_ref, pool_ref, ids_ref, row_ref, x_sem, small_sem,
):
    queries, width = unit_ref.shape
    tokens = x_ref.shape[1]
    chunks = width // LANES
    small = [
        pltpu.make_async_copy(src, dst, small_sem.at[n])
        for n, (src, dst) in enumerate(
            [
                (len_hbm, len_ref),
                (gain_hbm, gain_ref),
                (pos_hbm, pos_ref),
                (pool_hbm, pool_ref),
                (ids_hbm, ids_ref),
            ]
        )
    ]
    small[0].start()
    states = [
        pltpu.make_async_copy(x_hbm.at[0, i], x_ref.at[i], x_sem.at[i]) for i in range(queries)
    ]
    for copy in states:
        copy.start()
    for copy in small[1:]:
        copy.start()
    small[0].wait()
    token = lax.broadcasted_iota(jnp.int32, (tokens, 1), 0)

    def one_query(i, carry):
        pltpu.make_async_copy(x_hbm.at[0, i], x_ref.at[i], x_sem.at[i]).wait()
        square = jnp.zeros((tokens, LANES), F32)
        for k in range(chunks):
            v = x_ref[i, :, k * LANES : (k + 1) * LANES].astype(F32)
            square += v * v
        inv = lax.rsqrt(jnp.sum(square, axis=1, keepdims=True) / width + 1e-05)
        inv_ref[i] = jnp.broadcast_to(inv, (tokens, LANES))
        length = len_ref[0, i]
        weight = jnp.where(token < length, inv, 0.0) / length.astype(F32)
        for k in range(chunks):
            cols = slice(k * LANES, (k + 1) * LANES)
            v = x_ref[i, :, cols].astype(F32) * weight
            row_ref[i, :, cols] = jnp.sum(v, axis=0, keepdims=True)
        return carry

    lax.fori_loop(0, queries, one_query, 0)
    for copy in small[1:]:
        copy.wait()
    square = jnp.zeros((queries, LANES), F32)
    for k in range(chunks):
        cols = slice(k * LANES, (k + 1) * LANES)
        pooled = jnp.concatenate([row_ref[i, :, cols] for i in range(queries)], axis=0)
        pooled = pooled * gain_ref[:, cols]
        unit_ref[:, cols] = pooled
        square += pooled * pooled
    norm = lax.rsqrt(jnp.sum(square, axis=1, keepdims=True) + 1e-06)
    norm_ref[...] = jnp.broadcast_to(norm, norm_ref.shape)
    ids = ids_ref[:, 0, :]
    hard = ids.shape[0]
    bits = (2 * queries - 1).bit_length()
    half = chunks * 2 * queries
    owner = ids >> bits
    other = jnp.where((owner & 1) == core_ref[0], 0, half)
    place = other + ((owner >> 1) << bits) + (ids & (2 * queries - 1))
    row = lax.broadcasted_iota(jnp.int32, (hard, LANES), 0)
    lane = lax.broadcasted_iota(jnp.int32, (hard, LANES), 1)

    def lay(x, first):
        to = (lane == row + first).astype(F32).astype(BF16)
        return lax.dot_general(
            x.astype(F32).astype(BF16), to, BY_COLUMN, preferred_element_type=F32
        )

    id_rows = lay(place >> 5, 0) + lay(place & 31, hard)
    for k in range(chunks):
        cols = slice(k * LANES, (k + 1) * LANES)
        unit = unit_ref[:, cols] * norm
        unit_ref[:, cols] = unit
        rows = [unit, id_rows, pos_ref[0, :, cols].astype(F32), pool_ref[0, :, cols].astype(F32)]
        out_ref[k] = jnp.concatenate(rows, axis=0).astype(BF16)


def rows_of(block, first, last):
    return block[:, first:last].reshape(block.shape[0] * (last - first), LANES)


def ids_of(block, q, hard):
    rows = rows_of(block, q, 2 * q)
    lane = lax.broadcasted_iota(jnp.int32, rows.shape, 1)
    ids = rows * 32.0 + pltpu.roll(rows, LANES - hard, 1)
    return jnp.where(lane < hard, ids, 0.0).astype(jnp.int32)


def similar_kernel(hard, got_ref, gotx_ref, sim_ref):
    chips, rows, _ = got_ref.shape
    q = rows // 5
    half = chips * q
    n = 2 * half
    a = got_ref[...].astype(F32)
    b = gotx_ref[...].astype(F32)
    e = rows_of(a, 0, q).astype(BF16)
    p = jnp.concatenate([rows_of(a, 2 * q, 3 * q), rows_of(b, 2 * q, 3 * q)], axis=0).astype(BF16)
    m = jnp.concatenate([rows_of(a, 3 * q, 5 * q), rows_of(b, 3 * q, 5 * q)], axis=0).astype(BF16)
    ids = ids_of(a, q, hard)
    sim = lax.dot_general(e, p, BY_ROW, preferred_element_type=F32) / TEMPERATURE
    sim_ref[:, :, :n] = sim.reshape(chips, q, n)
    pool = lax.dot_general(e, m, BY_ROW, preferred_element_type=F32)
    tail = jnp.zeros((half, LANES), F32)
    within, tile = ids & (LANES - 1), ids >> 7
    for k in range(2 * n // LANES):
        picked = jnp.take_along_axis(
            pool[:, k * LANES : (k + 1) * LANES], within, axis=1, mode="promise_in_bounds"
        )
        tail = jnp.where(tile == k, picked, tail)
    lane = lax.broadcasted_iota(jnp.int32, (half, LANES), 1)
    tail = jnp.where(lane < hard, tail / TEMPERATURE, 0.0)
    sim_ref[:, :, n:] = tail.reshape(chips, q, LANES)


def softmax_kernel(hard, chip_ref, in_ref, out_ref):
    copies, q, width = out_ref.shape
    n = width - LANES
    scores = in_ref[...]
    column = lax.broadcasted_iota(jnp.int32, (q, width), 1)
    row = lax.broadcasted_iota(jnp.int32, (q, width), 0)
    exps = jnp.where(column < n + hard, jnp.exp(scores), 0.0)
    soft = exps / jnp.sum(exps, axis=1, keepdims=True)
    own = column == row + chip_ref[0] * q
    along = jnp.sum(soft * scores - jnp.where(own, scores, 0.0), axis=1, keepdims=True)
    high = along.astype(BF16).astype(F32)
    sent = jnp.where(column == n + hard, high, soft)
    sent = jnp.where(column == n + hard + 1, along - high, sent)
    sent = sent.astype(BF16)
    for k in range(copies):
        out_ref[k] = sent


def share(w, ids, hard, own_cols, other_cols, a, b, e, pos):
    q = a.shape[1] // 5
    half = w.shape[0]
    n = 2 * half
    tail = w[:, n:]
    from_own, from_other = w[:, own_cols].astype(BF16), w[:, other_cols].astype(BF16)
    column = lax.broadcasted_iota(jnp.int32, (half, n), 1)
    own_spread = jnp.zeros((half, n), F32)
    other_spread = jnp.zeros((half, n), F32)
    for m in range(hard):
        one, weight = ids[:, m : m + 1], tail[:, m : m + 1]
        own_spread += jnp.where(column == one, weight, 0.0)
        other_spread += jnp.where(column == one - n, weight, 0.0)
    own_spread = own_spread.astype(BF16)
    other_spread = other_spread.astype(BF16)

    def dot(left, block, first, last):
        return jnp.dot(left, rows_of(block, first, last).astype(BF16), preferred_element_type=F32)

    numerator = dot(from_own, a, 2 * q, 3 * q) + dot(from_other, b, 2 * q, 3 * q)
    numerator += dot(own_spread, a, 3 * q, 5 * q) + dot(other_spread, b, 3 * q, 5 * q)
    along = tail[:, hard : hard + 1] + tail[:, hard + 1 : hard + 2]
    emb_grad = (numerator - pos) / TEMPERATURE - along * e
    eh = e.astype(BF16)
    key = lax.dot_general(from_own, eh, BY_COLUMN, preferred_element_type=F32)
    pool = lax.dot_general(own_spread, eh, BY_COLUMN, preferred_element_type=F32)
    return emb_grad, key, pool, jnp.sum(emb_grad * e, axis=0, keepdims=True)


def own_kernel(hard, w_ref, got_ref, gotx_ref, emb_ref, key_ref, pool_ref, gain_ref):
    chips, q, width = w_ref.shape
    half = chips * q
    a = got_ref[...].astype(F32)
    b = gotx_ref[...].astype(F32)
    w = w_ref[...].astype(F32).reshape(half, width)
    e = rows_of(a, 0, q)
    emb_ref[...], key, pool_ref[...], gain_ref[...] = share(
        w, ids_of(a, q, hard), hard, slice(0, half), slice(half, 2 * half), a, b, e, rows_of(a, 2 * q, 3 * q)
    )
    key_ref[...] = key - e


def slices_kernel(
    hard, chip_ref, wx_ref, got_ref, gotx_ref, gain_ref, emb_ref, key_ref, pool_ref, part_ref, out_ref
):
    chips, q, width = wx_ref.shape
    half = chips * q
    a = got_ref[...].astype(F32)
    b = gotx_ref[...].astype(F32)
    w = wx_ref[...].astype(F32).reshape(half, width)
    ids = ids_of(b, q, hard) ^ (2 * half)
    e = rows_of(b, 0, q)
    _, key, pool, gain_part = share(
        w, ids, hard, slice(half, 2 * half), slice(0, half), a, b, e, rows_of(b, 2 * q, 3 * q)
    )
    emb_grad = emb_ref[...]
    key = (key + key_ref[...]) / TEMPERATURE
    pool = (pool + pool_ref[...]) * (POOL_SCALE / TEMPERATURE)
    gain_part = (gain_part + part_ref[...]) / gain_ref[pl.ds(chip_ref[0], 1), :]
    gain_high = gain_part.astype(BF16).astype(F32)
    row = lax.broadcasted_iota(jnp.int32, (q, LANES), 0)
    gain_rows = jnp.where(row == 0, gain_high, jnp.where(row == 1, gain_part - gain_high, 0.0))
    for k in range(chips):
        rows = slice(k * q, (k + 1) * q)
        block = [emb_grad[rows], key[rows], pool[2 * k * q : 2 * (k + 1) * q], gain_rows]
        out_ref[k] = jnp.concatenate(block, axis=0).astype(BF16)


def gain_kernel(in_ref, out_ref):
    copies, chips, _ = out_ref.shape
    q = in_ref.shape[1] // 5
    for k in range(chips):
        rows = in_ref[k].astype(F32)[4 * q : 5 * q]
        both = jnp.sum(rows, axis=0, keepdims=True)
        for r in range(copies):
            out_ref[r, k : k + 1] = both


def backward_kernel(
    len_ref, in_ref, x_ref, gain_ref, unit_ref, inv_ref, norm_ref, grad_ref, key_ref, pool_ref, h_ref, row_ref
):
    queries, width = unit_ref.shape
    tokens = x_ref.shape[1]
    chunks = width // LANES
    q = queries
    dots = jnp.zeros((q, LANES), F32)
    for k in range(chunks):
        cols = slice(k * LANES, (k + 1) * LANES)
        block = in_ref[k].astype(F32)
        key_ref[:, cols] = block[q : 2 * q]
        pool_ref[:, cols] = block[2 * q : 4 * q]
        g = block[:q]
        h_ref[:, cols] = g
        dots += g * unit_ref[:, cols]
    along = jnp.sum(dots, axis=1, keepdims=True)
    norm = norm_ref[:, :1]
    for k in range(chunks):
        cols = slice(k * LANES, (k + 1) * LANES)
        h = (h_ref[:, cols] - along * unit_ref[:, cols]) * (norm * gain_ref[:, cols])
        for i in range(q):
            row_ref[i, :, cols] = h[i : i + 1]
    token = lax.broadcasted_iota(jnp.int32, (tokens, 1), 0)

    def one_query(i, carry):
        length = len_ref[i]
        total = jnp.zeros((tokens, LANES), F32)
        for k in range(chunks):
            cols = slice(k * LANES, (k + 1) * LANES)
            total += x_ref[i, :, cols].astype(F32) * row_ref[i, :, cols]
        total = jnp.sum(total, axis=1, keepdims=True)
        inv = inv_ref[i][:, :1]
        scale = jnp.where(token < length, QUERY_SCALE * inv, 0.0) / length.astype(F32)
        back = scale * inv * inv * total / width
        for k in range(chunks):
            cols = slice(k * LANES, (k + 1) * LANES)
            x = x_ref[i, :, cols].astype(F32)
            grad_ref[i, :, cols] = (scale * row_ref[i, :, cols] - back * x).astype(BF16)
        return carry

    lax.fori_loop(0, queries, one_query, 0)


def call(kernel, outs, args, flops, smem=(), hbm=(), scratch=(), vmem=40):
    def space(i):
        return pltpu.SMEM if i in smem else pltpu.HBM if i in hbm else pltpu.VMEM

    size = sum(a.size * a.dtype.itemsize for a in args) + sum(
        o.size * o.dtype.itemsize for o in outs
    )
    return pl.pallas_call(
        kernel,
        out_shape=list(outs),
        in_specs=[pl.BlockSpec(memory_space=space(i)) for i in range(len(args))],
        out_specs=[pl.BlockSpec(memory_space=pltpu.VMEM)] * len(outs),
        scratch_shapes=list(scratch),
        compiler_params=pltpu.CompilerParams(vmem_limit_bytes=vmem * 1024 * 1024),
        cost_estimate=pl.CostEstimate(flops=flops, bytes_accessed=size, transcendentals=0),
    )(*args)


def shape(dims, dtype):
    return jax.ShapeDtypeStruct(dims, dtype)


def local(query_states, query_lengths, norm_gain, positives, mined_pool, hard_ids):
    owners = lax.axis_size("dp")
    groups = lax.axis_size("rep")
    me = lax.axis_index("dp").astype(jnp.int32).reshape(1)
    core, chip = lax.rem(me, 2), lax.div(me, 2)
    _, queries, tokens, width = query_states.shape
    hard = hard_ids.shape[2]
    chips = owners // 2
    q_all = queries * owners
    lengths = query_lengths.reshape(queries)
    gain_row = norm_gain.reshape(1, width)
    gain_tiles = norm_gain.reshape(chips, LANES)
    pair = [(i, i ^ 1) for i in range(owners)]
    same_core = [[2 * i + c for i in range(chips)] for c in range(2)]

    def among_chips(x):
        return lax.all_to_all(x, "dp", 0, 0, tiled=True, axis_index_groups=same_core)

    def bound(kernel):
        return lambda *refs: kernel(hard, *refs)

    out, unit, inv, norm = call(
        embed_kernel,
        [
            shape((chips, 5 * queries, LANES), BF16),
            shape((queries, width), F32),
            shape((queries, tokens, LANES), F32),
            shape((queries, LANES), F32),
        ],
        [core, query_lengths, query_states, gain_row, positives, mined_pool, hard_ids.transpose(2, 0, 1)],
        8_000_000,
        (0,),
        (1, 2, 3, 4, 5, 6),
        [
            pltpu.SMEM((1, queries), jnp.int32),
            pltpu.VMEM((queries, tokens, width), BF16),
            pltpu.VMEM((1, width), F32),
            pltpu.VMEM((1, queries, width), BF16),
            pltpu.VMEM((1, 2 * queries, width), BF16),
            pltpu.VMEM((hard, 1, queries), jnp.int32),
            pltpu.VMEM((queries, 1, width), F32),
            pltpu.SemaphoreType.DMA((queries,)),
            pltpu.SemaphoreType.DMA((5,)),
        ],
        60,
    )
    got = among_chips(out)
    gotx = lax.ppermute(got, "dp", pair)

    (part,) = call(
        bound(similar_kernel),
        [shape((chips, queries, q_all + LANES), F32)],
        [got, gotx],
        100_000_000,
    )
    scores = jnp.sum(among_chips(part.astype(F16)).astype(F32), axis=0)
    (sent,) = call(
        bound(softmax_kernel),
        [shape((chips, queries, q_all + LANES), BF16)],
        [chip, scores],
        1_000_000,
        (0,),
    )
    weights = among_chips(sent)
    weightsx = lax.ppermute(weights, "dp", pair)

    half = q_all // 2
    shares = call(
        bound(own_kernel),
        [
            shape((half, LANES), F32),
            shape((half, LANES), F32),
            shape((q_all, LANES), F32),
            shape((1, LANES), F32),
        ],
        [weights, got, gotx],
        200_000_000,
    )
    (back,) = call(
        bound(slices_kernel),
        [shape((chips, 5 * queries, LANES), BF16)],
        [chip, weightsx, got, gotx, gain_tiles, *shares],
        200_000_000,
        (0,),
    )
    home = among_chips(back)
    (gain_sent,) = call(
        gain_kernel, [shape((groups, width // LANES, LANES), F32)], [home], 100_000
    )
    gain_groups = lax.all_to_all(gain_sent, "rep", 0, 0, tiled=True)
    query_grad, key_grad, pool_grad = call(
        backward_kernel,
        [
            shape((queries, tokens, width), BF16),
            shape((queries, width), F32),
            shape((2 * queries, width), F32),
        ],
        [lengths, home, query_states[0], gain_row, unit, inv, norm],
        10_000_000,
        (0,),
        (),
        [pltpu.VMEM((queries, width), F32), pltpu.VMEM((queries, 1, width), F32)],
    )
    gain_grad = jnp.sum(gain_groups, axis=0).reshape(width)
    return query_grad[None], key_grad[None], pool_grad[None], gain_grad


def solution(mesh):
    placed = (
        P("rep", "dp", None, None),
        P("rep", "dp"),
        P(),
        P("rep", "dp", None),
        P("rep", "dp", None),
        P("rep", "dp", None),
    )
    return jax.shard_map(
        local,
        mesh=mesh,
        in_specs=placed,
        out_specs=(P("rep", "dp", None, None), P("rep", "dp", None), P("rep", "dp", None), P()),
        check_vma=False,
    )
```

```python
import jax
import jax.numpy as jnp
from jax import lax
from jax.experimental import pallas as pl
from jax.experimental.pallas import tpu as pltpu
from jax.sharding import PartitionSpec as P

TEMPERATURE = 0.02
QUERY_SCALE = 512.0
POOL_SCALE = 16.0
LANES = 128
F32 = jnp.float32
BF16 = jnp.bfloat16
F16 = jnp.float16
BY_COLUMN = (((0,), (0,)), ((), ()))
BY_ROW = (((1,), (1,)), ((), ()))


def embed_kernel(
    me_ref, len_hbm, x_hbm, gain_hbm, pos_hbm, pool_hbm, ids_hbm, out_ref, unit_ref, inv_ref, norm_ref,
    len_ref, x_ref, gain_ref, pos_ref, pool_ref, ids_ref, row_ref, x_sem, small_sem,
):
    queries, width = unit_ref.shape
    tokens = x_ref.shape[1]
    chunks = width // LANES
    small = [
        pltpu.make_async_copy(src, dst, small_sem.at[n])
        for n, (src, dst) in enumerate(
            [
                (len_hbm, len_ref),
                (gain_hbm, gain_ref),
                (pos_hbm, pos_ref),
                (pool_hbm, pool_ref),
                (ids_hbm, ids_ref),
            ]
        )
    ]
    small[0].start()
    states = [
        pltpu.make_async_copy(x_hbm.at[0, i], x_ref.at[i], x_sem.at[i]) for i in range(queries)
    ]
    for copy in states:
        copy.start()
    for copy in small[1:]:
        copy.start()
    small[0].wait()
    token = lax.broadcasted_iota(jnp.int32, (tokens, 1), 0)

    def one_query(i, carry):
        pltpu.make_async_copy(x_hbm.at[0, i], x_ref.at[i], x_sem.at[i]).wait()
        square = jnp.zeros((tokens, LANES), F32)
        for k in range(chunks):
            v = x_ref[i, :, k * LANES : (k + 1) * LANES].astype(F32)
            square += v * v
        inv = lax.rsqrt(jnp.sum(square, axis=1, keepdims=True) / width + 1e-05)
        inv_ref[i] = jnp.broadcast_to(inv, (tokens, LANES))
        length = len_ref[0, i]
        weight = jnp.where(token < length, inv, 0.0) / length.astype(F32)
        for k in range(chunks):
            cols = slice(k * LANES, (k + 1) * LANES)
            v = x_ref[i, :, cols].astype(F32) * weight
            row_ref[i, :, cols] = jnp.sum(v, axis=0, keepdims=True)
        return carry

    lax.fori_loop(0, queries, one_query, 0)
    for copy in small[1:]:
        copy.wait()
    square = jnp.zeros((queries, LANES), F32)
    for k in range(chunks):
        cols = slice(k * LANES, (k + 1) * LANES)
        pooled = jnp.concatenate([row_ref[i, :, cols] for i in range(queries)], axis=0)
        pooled = pooled * gain_ref[:, cols]
        unit_ref[:, cols] = pooled
        square += pooled * pooled
    norm = lax.rsqrt(jnp.sum(square, axis=1, keepdims=True) + 1e-06)
    norm_ref[...] = jnp.broadcast_to(norm, norm_ref.shape)
    ids = ids_ref[:, 0, :]
    hard = ids.shape[0]
    bits = (2 * queries - 1).bit_length()
    half = chunks * 2 * queries
    owner = ids >> bits
    other = jnp.where((owner & 1) == (me_ref[0] & 1), 0, half)
    place = other + ((owner >> 1) << bits) + (ids & (2 * queries - 1))
    row = lax.broadcasted_iota(jnp.int32, (hard, LANES), 0)
    lane = lax.broadcasted_iota(jnp.int32, (hard, LANES), 1)

    def lay(x, first):
        to = (lane == row + first).astype(F32).astype(BF16)
        return lax.dot_general(
            x.astype(F32).astype(BF16), to, BY_COLUMN, preferred_element_type=F32
        )

    id_rows = lay(place >> 5, 0) + lay(place & 31, hard)
    for k in range(chunks):
        cols = slice(k * LANES, (k + 1) * LANES)
        unit = unit_ref[:, cols] * norm
        unit_ref[:, cols] = unit
        rows = [unit, id_rows, pos_ref[0, :, cols].astype(F32), pool_ref[0, :, cols].astype(F32)]
        out_ref[k] = jnp.concatenate(rows, axis=0).astype(BF16)


def rows_of(block, first, last):
    return block[:, first:last].reshape(block.shape[0] * (last - first), LANES)


def ids_of(block, q, hard):
    rows = rows_of(block, q, 2 * q)
    lane = lax.broadcasted_iota(jnp.int32, rows.shape, 1)
    ids = rows * 32.0 + pltpu.roll(rows, LANES - hard, 1)
    return jnp.where(lane < hard, ids, 0.0).astype(jnp.int32)


def similar_kernel(hard, got_ref, gotx_ref, sim_ref):
    chips, rows, _ = got_ref.shape
    q = rows // 5
    half = chips * q
    n = 2 * half
    a = got_ref[...].astype(F32)
    b = gotx_ref[...].astype(F32)
    e = rows_of(a, 0, q).astype(BF16)
    p = jnp.concatenate([rows_of(a, 2 * q, 3 * q), rows_of(b, 2 * q, 3 * q)], axis=0).astype(BF16)
    m = jnp.concatenate([rows_of(a, 3 * q, 5 * q), rows_of(b, 3 * q, 5 * q)], axis=0).astype(BF16)
    ids = ids_of(a, q, hard)
    sim = lax.dot_general(e, p, BY_ROW, preferred_element_type=F32) / TEMPERATURE
    sim_ref[:, :, :n] = sim.reshape(chips, q, n)
    pool = lax.dot_general(e, m, BY_ROW, preferred_element_type=F32)
    tail = jnp.zeros((half, LANES), F32)
    within, tile = ids & (LANES - 1), ids >> 7
    for k in range(2 * n // LANES):
        picked = jnp.take_along_axis(
            pool[:, k * LANES : (k + 1) * LANES], within, axis=1, mode="promise_in_bounds"
        )
        tail = jnp.where(tile == k, picked, tail)
    lane = lax.broadcasted_iota(jnp.int32, (half, LANES), 1)
    tail = jnp.where(lane < hard, tail / TEMPERATURE, 0.0)
    sim_ref[:, :, n:] = tail.reshape(chips, q, LANES)


def softmax_kernel(hard, me_ref, in_ref, out_ref):
    copies, q, width = out_ref.shape
    n = width - LANES
    scores = in_ref[...]
    column = lax.broadcasted_iota(jnp.int32, (q, width), 1)
    row = lax.broadcasted_iota(jnp.int32, (q, width), 0)
    exps = jnp.where(column < n + hard, jnp.exp(scores), 0.0)
    soft = exps / jnp.sum(exps, axis=1, keepdims=True)
    own = column == row + (me_ref[0] >> 1) * q
    along = jnp.sum(soft * scores - jnp.where(own, scores, 0.0), axis=1, keepdims=True)
    high = along.astype(BF16).astype(F32)
    sent = jnp.where(column == n + hard, high, soft)
    sent = jnp.where(column == n + hard + 1, along - high, sent)
    sent = sent.astype(BF16)
    for k in range(copies):
        out_ref[k] = sent


def share(w, ids, hard, own_cols, other_cols, a, b, e, pos):
    q = a.shape[1] // 5
    half = w.shape[0]
    n = 2 * half
    tail = w[:, n:]
    from_own, from_other = w[:, own_cols].astype(BF16), w[:, other_cols].astype(BF16)
    column = lax.broadcasted_iota(jnp.int32, (half, n), 1)
    own_spread = jnp.zeros((half, n), F32)
    other_spread = jnp.zeros((half, n), F32)
    for m in range(hard):
        one, weight = ids[:, m : m + 1], tail[:, m : m + 1]
        own_spread += jnp.where(column == one, weight, 0.0)
        other_spread += jnp.where(column == one - n, weight, 0.0)
    own_spread = own_spread.astype(BF16)
    other_spread = other_spread.astype(BF16)

    def dot(left, block, first, last):
        return jnp.dot(left, rows_of(block, first, last).astype(BF16), preferred_element_type=F32)

    numerator = dot(from_own, a, 2 * q, 3 * q) + dot(from_other, b, 2 * q, 3 * q)
    numerator += dot(own_spread, a, 3 * q, 5 * q) + dot(other_spread, b, 3 * q, 5 * q)
    along = tail[:, hard : hard + 1] + tail[:, hard + 1 : hard + 2]
    emb_grad = (numerator - pos) / TEMPERATURE - along * e
    eh = e.astype(BF16)
    key = lax.dot_general(from_own, eh, BY_COLUMN, preferred_element_type=F32)
    pool = lax.dot_general(own_spread, eh, BY_COLUMN, preferred_element_type=F32)
    return emb_grad, key, pool, jnp.sum(emb_grad * e, axis=0, keepdims=True)


def own_kernel(hard, w_ref, got_ref, gotx_ref, emb_ref, key_ref, pool_ref, gain_ref):
    chips, q, width = w_ref.shape
    half = chips * q
    a = got_ref[...].astype(F32)
    b = gotx_ref[...].astype(F32)
    w = w_ref[...].astype(F32).reshape(half, width)
    e = rows_of(a, 0, q)
    emb_ref[...], key, pool_ref[...], gain_ref[...] = share(
        w, ids_of(a, q, hard), hard, slice(0, half), slice(half, 2 * half), a, b, e, rows_of(a, 2 * q, 3 * q)
    )
    key_ref[...] = key - e


def slices_kernel(
    hard, me_ref, wx_ref, got_ref, gotx_ref, gain_ref, emb_ref, key_ref, pool_ref, part_ref, out_ref
):
    chips, q, width = wx_ref.shape
    half = chips * q
    a = got_ref[...].astype(F32)
    b = gotx_ref[...].astype(F32)
    w = wx_ref[...].astype(F32).reshape(half, width)
    ids = ids_of(b, q, hard) ^ (2 * half)
    e = rows_of(b, 0, q)
    _, key, pool, gain_part = share(
        w, ids, hard, slice(half, 2 * half), slice(0, half), a, b, e, rows_of(b, 2 * q, 3 * q)
    )
    emb_grad = emb_ref[...]
    key = (key + key_ref[...]) / TEMPERATURE
    pool = (pool + pool_ref[...]) * (POOL_SCALE / TEMPERATURE)
    gain_part = (gain_part + part_ref[...]) / gain_ref[pl.ds(me_ref[0] >> 1, 1), :]
    gain_high = gain_part.astype(BF16).astype(F32)
    row = lax.broadcasted_iota(jnp.int32, (q, LANES), 0)
    gain_rows = jnp.where(row == 0, gain_high, jnp.where(row == 1, gain_part - gain_high, 0.0))
    for k in range(chips):
        rows = slice(k * q, (k + 1) * q)
        block = [emb_grad[rows], key[rows], pool[2 * k * q : 2 * (k + 1) * q], gain_rows]
        out_ref[k] = jnp.concatenate(block, axis=0).astype(BF16)


def gain_kernel(in_ref, out_ref):
    copies, _, _ = out_ref.shape
    q = in_ref.shape[1] // 5
    both = jnp.sum(in_ref[:, 4 * q :].astype(F32), axis=1)
    for r in range(copies):
        out_ref[r] = both


def backward_kernel(
    len_ref, in_ref, x_ref, gain_ref, unit_ref, inv_ref, norm_ref, grad_ref, key_ref, pool_ref, h_ref, row_ref
):
    queries, width = unit_ref.shape
    tokens = x_ref.shape[1]
    chunks = width // LANES
    q = queries
    dots = jnp.zeros((q, LANES), F32)
    for k in range(chunks):
        cols = slice(k * LANES, (k + 1) * LANES)
        block = in_ref[k].astype(F32)
        key_ref[:, cols] = block[q : 2 * q]
        pool_ref[:, cols] = block[2 * q : 4 * q]
        g = block[:q]
        h_ref[:, cols] = g
        dots += g * unit_ref[:, cols]
    along = jnp.sum(dots, axis=1, keepdims=True)
    norm = norm_ref[:, :1]
    for k in range(chunks):
        cols = slice(k * LANES, (k + 1) * LANES)
        h = (h_ref[:, cols] - along * unit_ref[:, cols]) * (norm * gain_ref[:, cols])
        for i in range(q):
            row_ref[i, :, cols] = h[i : i + 1]
    token = lax.broadcasted_iota(jnp.int32, (tokens, 1), 0)

    def one_query(i, carry):
        length = len_ref[i]
        total = jnp.zeros((tokens, LANES), F32)
        for k in range(chunks):
            cols = slice(k * LANES, (k + 1) * LANES)
            total += x_ref[i, :, cols].astype(F32) * row_ref[i, :, cols]
        total = jnp.sum(total, axis=1, keepdims=True)
        inv = inv_ref[i][:, :1]
        scale = jnp.where(token < length, QUERY_SCALE * inv, 0.0) / length.astype(F32)
        back = scale * inv * inv * total / width
        for k in range(chunks):
            cols = slice(k * LANES, (k + 1) * LANES)
            x = x_ref[i, :, cols].astype(F32)
            grad_ref[i, :, cols] = (scale * row_ref[i, :, cols] - back * x).astype(BF16)
        return carry

    lax.fori_loop(0, queries, one_query, 0)


def call(kernel, outs, args, flops, smem=(), hbm=(), scratch=(), vmem=40):
    def space(i):
        return pltpu.SMEM if i in smem else pltpu.HBM if i in hbm else pltpu.VMEM

    size = sum(a.size * a.dtype.itemsize for a in args) + sum(
        o.size * o.dtype.itemsize for o in outs
    )
    return pl.pallas_call(
        kernel,
        out_shape=list(outs),
        in_specs=[pl.BlockSpec(memory_space=space(i)) for i in range(len(args))],
        out_specs=[pl.BlockSpec(memory_space=pltpu.VMEM)] * len(outs),
        scratch_shapes=list(scratch),
        compiler_params=pltpu.CompilerParams(vmem_limit_bytes=vmem * 1024 * 1024),
        cost_estimate=pl.CostEstimate(flops=flops, bytes_accessed=size, transcendentals=0),
    )(*args)


def shape(dims, dtype):
    return jax.ShapeDtypeStruct(dims, dtype)


def local(query_states, query_lengths, norm_gain, positives, mined_pool, hard_ids):
    owners = lax.axis_size("dp")
    groups = lax.axis_size("rep")
    me = lax.axis_index("dp").astype(jnp.int32).reshape(1)
    _, queries, tokens, width = query_states.shape
    hard = hard_ids.shape[2]
    chips = owners // 2
    q_all = queries * owners
    lengths = query_lengths.reshape(queries)
    gain_row = norm_gain.reshape(1, width)
    gain_tiles = norm_gain.reshape(chips, LANES)
    pair = [(i, i ^ 1) for i in range(owners)]
    same_core = [[2 * i + c for i in range(chips)] for c in range(2)]

    def among_chips(x):
        return lax.all_to_all(x, "dp", 0, 0, tiled=True, axis_index_groups=same_core)

    def bound(kernel):
        return lambda *refs: kernel(hard, *refs)

    out, unit, inv, norm = call(
        embed_kernel,
        [
            shape((chips, 5 * queries, LANES), BF16),
            shape((queries, width), F32),
            shape((queries, tokens, LANES), F32),
            shape((queries, LANES), F32),
        ],
        [me, query_lengths, query_states, gain_row, positives, mined_pool, hard_ids.transpose(2, 0, 1)],
        8_000_000,
        (0,),
        (1, 2, 3, 4, 5, 6),
        [
            pltpu.SMEM((1, queries), jnp.int32),
            pltpu.VMEM((queries, tokens, width), BF16),
            pltpu.VMEM((1, width), F32),
            pltpu.VMEM((1, queries, width), BF16),
            pltpu.VMEM((1, 2 * queries, width), BF16),
            pltpu.VMEM((hard, 1, queries), jnp.int32),
            pltpu.VMEM((queries, 1, width), F32),
            pltpu.SemaphoreType.DMA((queries,)),
            pltpu.SemaphoreType.DMA((5,)),
        ],
        60,
    )
    got = among_chips(out)
    gotx = lax.ppermute(got, "dp", pair)

    (part,) = call(
        bound(similar_kernel),
        [shape((chips, queries, q_all + LANES), F32)],
        [got, gotx],
        100_000_000,
    )
    scores = jnp.sum(among_chips(part.astype(F16)).astype(F32), axis=0)
    (sent,) = call(
        bound(softmax_kernel),
        [shape((chips, queries, q_all + LANES), BF16)],
        [me, scores],
        1_000_000,
        (0,),
    )
    weights = among_chips(sent)
    weightsx = lax.ppermute(weights, "dp", pair)

    half = q_all // 2
    shares = call(
        bound(own_kernel),
        [
            shape((half, LANES), F32),
            shape((half, LANES), F32),
            shape((q_all, LANES), F32),
            shape((1, LANES), F32),
        ],
        [weights, got, gotx],
        200_000_000,
    )
    (back,) = call(
        bound(slices_kernel),
        [shape((chips, 5 * queries, LANES), BF16)],
        [me, weightsx, got, gotx, gain_tiles, *shares],
        200_000_000,
        (0,),
    )
    home = among_chips(back)
    (gain_sent,) = call(
        gain_kernel, [shape((groups, width // LANES, LANES), F32)], [home], 100_000
    )
    gain_groups = lax.all_to_all(gain_sent, "rep", 0, 0, tiled=True)
    query_grad, key_grad, pool_grad = call(
        backward_kernel,
        [
            shape((queries, tokens, width), BF16),
            shape((queries, width), F32),
            shape((2 * queries, width), F32),
        ],
        [lengths, home, query_states[0], gain_row, unit, inv, norm],
        10_000_000,
        (0,),
        (),
        [pltpu.VMEM((queries, width), F32), pltpu.VMEM((queries, 1, width), F32)],
    )
    gain_grad = jnp.sum(gain_groups, axis=0).reshape(width)
    return query_grad[None], key_grad[None], pool_grad[None], gain_grad


def solution(mesh):
    placed = (
        P("rep", "dp", None, None),
        P("rep", "dp"),
        P(),
        P("rep", "dp", None),
        P("rep", "dp", None),
        P("rep", "dp", None),
    )
    return jax.shard_map(
        local,
        mesh=mesh,
        in_specs=placed,
        out_specs=(P("rep", "dp", None, None), P("rep", "dp", None), P("rep", "dp", None), P()),
        check_vma=False,
    )
```

```python
import jax
import jax.numpy as jnp
from jax import lax
from jax.experimental import pallas as pl
from jax.experimental.pallas import tpu as pltpu
from jax.sharding import PartitionSpec as P

TEMPERATURE = 0.02
QUERY_SCALE = 512.0
POOL_SCALE = 16.0
LANES = 128
PART = 8
F32 = jnp.float32
BF16 = jnp.bfloat16
F16 = jnp.float16
BY_COLUMN = (((0,), (0,)), ((), ()))
BY_ROW = (((1,), (1,)), ((), ()))


def embed_kernel(
    me_ref, len_hbm, x_hbm, gain_hbm, pos_hbm, pool_hbm, ids_hbm,
    out_hbm, unit_hbm, inv_hbm, norm_hbm, out_ref, unit_ref, inv_ref, norm_ref, out_sem, len_ref, x_ref, gain_ref, pos_ref, pool_ref, ids_ref, row_ref, x_sem, small_sem,
):
    queries, width = unit_ref.shape
    tokens = x_ref.shape[1]
    chunks = width // LANES
    small = [
        pltpu.make_async_copy(src, dst, small_sem.at[n])
        for n, (src, dst) in enumerate(
            [
                (len_hbm, len_ref),
                (gain_hbm, gain_ref),
                (pos_hbm, pos_ref),
                (pool_hbm, pool_ref),
                (ids_hbm, ids_ref),
            ]
        )
    ]
    small[0].start()
    states = [
        pltpu.make_async_copy(x_hbm.at[0, i], x_ref.at[i], x_sem.at[i]) for i in range(queries)
    ]
    for copy in states:
        copy.start()
    for copy in small[1:]:
        copy.start()
    small[0].wait()
    token = lax.broadcasted_iota(jnp.int32, (tokens, 1), 0)

    def one_query(i, carry):
        pltpu.make_async_copy(x_hbm.at[0, i], x_ref.at[i], x_sem.at[i]).wait()
        square = jnp.zeros((tokens, LANES), F32)
        for k in range(chunks):
            v = x_ref[i, :, k * LANES : (k + 1) * LANES].astype(F32)
            square += v * v
        inv = lax.rsqrt(jnp.sum(square, axis=1, keepdims=True) / width + 1e-05)
        inv_ref[i] = jnp.broadcast_to(inv, (tokens, LANES))
        length = len_ref[0, i]
        weight = jnp.where(token < length, inv, 0.0) / length.astype(F32)
        for k in range(chunks):
            cols = slice(k * LANES, (k + 1) * LANES)
            v = x_ref[i, :, cols].astype(F32) * weight
            row_ref[i, :, cols] = jnp.sum(v, axis=0, keepdims=True)
        return carry

    lax.fori_loop(0, queries, one_query, 0)
    for copy in small[1:]:
        copy.wait()
    square = jnp.zeros((queries, LANES), F32)
    for k in range(chunks):
        cols = slice(k * LANES, (k + 1) * LANES)
        pooled = jnp.concatenate([row_ref[i, :, cols] for i in range(queries)], axis=0)
        pooled = pooled * gain_ref[:, cols]
        unit_ref[:, cols] = pooled
        square += pooled * pooled
    norm = lax.rsqrt(jnp.sum(square, axis=1, keepdims=True) + 1e-06)
    norm_ref[...] = jnp.broadcast_to(norm, norm_ref.shape)
    done = [
        pltpu.make_async_copy(inv_ref, inv_hbm, out_sem.at[0]),
        pltpu.make_async_copy(norm_ref, norm_hbm, out_sem.at[1]),
    ]
    for copy in done:
        copy.start()
    ids = ids_ref[:, 0, :]
    hard = ids.shape[0]
    bits = (2 * queries - 1).bit_length()
    half = chunks * 2 * queries
    owner = ids >> bits
    other = jnp.where((owner & 1) == (me_ref[0] & 1), 0, half)
    place = other + ((owner >> 1) << bits) + (ids & (2 * queries - 1))
    row = lax.broadcasted_iota(jnp.int32, (hard, LANES), 0)
    lane = lax.broadcasted_iota(jnp.int32, (hard, LANES), 1)

    def lay(x, first):
        to = (lane == row + first).astype(F32).astype(BF16)
        return lax.dot_general(
            x.astype(F32).astype(BF16), to, BY_COLUMN, preferred_element_type=F32
        )

    id_rows = lay(place >> 5, 0) + lay(place & 31, hard)
    for k in range(chunks):
        cols = slice(k * LANES, (k + 1) * LANES)
        unit = unit_ref[:, cols] * norm
        unit_ref[:, cols] = unit
        rows = [unit, id_rows, pos_ref[0, :, cols].astype(F32), pool_ref[0, :, cols].astype(F32)]
        out_ref[k] = jnp.concatenate(rows, axis=0).astype(BF16)
        if (k + 1) % PART == 0:
            part = pl.ds(k + 1 - PART, PART)
            done.append(
                pltpu.make_async_copy(out_ref.at[part], out_hbm.at[part], out_sem.at[3 + k // PART])
            )
            done[-1].start()
    done.append(pltpu.make_async_copy(unit_ref, unit_hbm, out_sem.at[2]))
    done[-1].start()
    for copy in done:
        copy.wait()


def rows_of(block, first, last):
    return block[:, first:last].reshape(block.shape[0] * (last - first), LANES)


def ids_of(block, q, hard):
    rows = rows_of(block, q, 2 * q)
    lane = lax.broadcasted_iota(jnp.int32, rows.shape, 1)
    ids = rows * 32.0 + pltpu.roll(rows, LANES - hard, 1)
    return jnp.where(lane < hard, ids, 0.0).astype(jnp.int32)


def similar_kernel(hard, got_ref, gotx_ref, sim_ref):
    chips, rows, _ = got_ref.shape
    q = rows // 5
    half = chips * q
    n = 2 * half
    a = got_ref[...].astype(F32)
    b = gotx_ref[...].astype(F32)
    e = rows_of(a, 0, q).astype(BF16)
    p = jnp.concatenate([rows_of(a, 2 * q, 3 * q), rows_of(b, 2 * q, 3 * q)], axis=0).astype(BF16)
    m = jnp.concatenate([rows_of(a, 3 * q, 5 * q), rows_of(b, 3 * q, 5 * q)], axis=0).astype(BF16)
    ids = ids_of(a, q, hard)
    sim = lax.dot_general(e, p, BY_ROW, preferred_element_type=F32) / TEMPERATURE
    sim_ref[:, :, :n] = sim.reshape(chips, q, n)
    pool = lax.dot_general(e, m, BY_ROW, preferred_element_type=F32)
    tail = jnp.zeros((half, LANES), F32)
    within, tile = ids & (LANES - 1), ids >> 7
    for k in range(2 * n // LANES):
        picked = jnp.take_along_axis(
            pool[:, k * LANES : (k + 1) * LANES], within, axis=1, mode="promise_in_bounds"
        )
        tail = jnp.where(tile == k, picked, tail)
    lane = lax.broadcasted_iota(jnp.int32, (half, LANES), 1)
    tail = jnp.where(lane < hard, tail / TEMPERATURE, 0.0)
    sim_ref[:, :, n:] = tail.reshape(chips, q, LANES)


def softmax_kernel(hard, me_ref, in_ref, out_ref):
    copies, q, width = out_ref.shape
    n = width - LANES
    scores = in_ref[...]
    column = lax.broadcasted_iota(jnp.int32, (q, width), 1)
    row = lax.broadcasted_iota(jnp.int32, (q, width), 0)
    exps = jnp.where(column < n + hard, jnp.exp(scores), 0.0)
    soft = exps / jnp.sum(exps, axis=1, keepdims=True)
    own = column == row + (me_ref[0] >> 1) * q
    along = jnp.sum(soft * scores - jnp.where(own, scores, 0.0), axis=1, keepdims=True)
    high = along.astype(BF16).astype(F32)
    sent = jnp.where(column == n + hard, high, soft)
    sent = jnp.where(column == n + hard + 1, along - high, sent)
    sent = sent.astype(BF16)
    for k in range(copies):
        out_ref[k] = sent


def share(w, ids, hard, own_cols, other_cols, a, b, e, pos):
    q = a.shape[1] // 5
    half = w.shape[0]
    n = 2 * half
    tail = w[:, n:]
    from_own, from_other = w[:, own_cols].astype(BF16), w[:, other_cols].astype(BF16)
    column = lax.broadcasted_iota(jnp.int32, (half, n), 1)
    own_spread = jnp.zeros((half, n), F32)
    other_spread = jnp.zeros((half, n), F32)
    for m in range(hard):
        one, weight = ids[:, m : m + 1], tail[:, m : m + 1]
        own_spread += jnp.where(column == one, weight, 0.0)
        other_spread += jnp.where(column == one - n, weight, 0.0)
    own_spread = own_spread.astype(BF16)
    other_spread = other_spread.astype(BF16)

    def dot(left, block, first, last):
        return jnp.dot(left, rows_of(block, first, last).astype(BF16), preferred_element_type=F32)

    numerator = dot(from_own, a, 2 * q, 3 * q) + dot(from_other, b, 2 * q, 3 * q)
    numerator += dot(own_spread, a, 3 * q, 5 * q) + dot(other_spread, b, 3 * q, 5 * q)
    along = tail[:, hard : hard + 1] + tail[:, hard + 1 : hard + 2]
    emb_grad = (numerator - pos) / TEMPERATURE - along * e
    eh = e.astype(BF16)
    key = lax.dot_general(from_own, eh, BY_COLUMN, preferred_element_type=F32)
    pool = lax.dot_general(own_spread, eh, BY_COLUMN, preferred_element_type=F32)
    return emb_grad, key, pool, jnp.sum(emb_grad * e, axis=0, keepdims=True)


def own_kernel(hard, w_ref, got_ref, gotx_ref, emb_ref, key_ref, pool_ref, gain_ref):
    chips, q, width = w_ref.shape
    half = chips * q
    a = got_ref[...].astype(F32)
    b = gotx_ref[...].astype(F32)
    w = w_ref[...].astype(F32).reshape(half, width)
    e = rows_of(a, 0, q)
    emb_ref[...], key, pool_ref[...], gain_ref[...] = share(
        w, ids_of(a, q, hard), hard, slice(0, half), slice(half, 2 * half), a, b, e, rows_of(a, 2 * q, 3 * q)
    )
    key_ref[...] = key - e


def slices_kernel(
    hard, me_ref, wx_ref, got_ref, gotx_ref, gain_ref, emb_ref, key_ref, pool_ref, part_ref, out_ref
):
    chips, q, width = wx_ref.shape
    half = chips * q
    a = got_ref[...].astype(F32)
    b = gotx_ref[...].astype(F32)
    w = wx_ref[...].astype(F32).reshape(half, width)
    ids = ids_of(b, q, hard) ^ (2 * half)
    e = rows_of(b, 0, q)
    _, key, pool, gain_part = share(
        w, ids, hard, slice(half, 2 * half), slice(0, half), a, b, e, rows_of(b, 2 * q, 3 * q)
    )
    emb_grad = emb_ref[...]
    key = (key + key_ref[...]) / TEMPERATURE
    pool = (pool + pool_ref[...]) * (POOL_SCALE / TEMPERATURE)
    gain_part = (gain_part + part_ref[...]) / gain_ref[pl.ds(me_ref[0] >> 1, 1), :]
    gain_high = gain_part.astype(BF16).astype(F32)
    row = lax.broadcasted_iota(jnp.int32, (q, LANES), 0)
    gain_rows = jnp.where(row == 0, gain_high, jnp.where(row == 1, gain_part - gain_high, 0.0))
    for k in range(chips):
        rows = slice(k * q, (k + 1) * q)
        block = [emb_grad[rows], key[rows], pool[2 * k * q : 2 * (k + 1) * q], gain_rows]
        out_ref[k] = jnp.concatenate(block, axis=0).astype(BF16)


def gain_kernel(in_ref, out_ref):
    copies, _, _ = out_ref.shape
    q = in_ref.shape[1] // 5
    both = jnp.sum(in_ref[:, 4 * q :].astype(F32), axis=1)
    for r in range(copies):
        out_ref[r] = both


def backward_kernel(
    len_ref, in_ref, x_ref, gain_ref, unit_ref, inv_ref, norm_ref, grad_hbm, key_hbm, pool_hbm,
    h_ref, row_ref, grad_ref, key_ref, pool_ref, grad_sem, small_sem,
):
    queries, width = unit_ref.shape
    tokens = x_ref.shape[1]
    chunks = width // LANES
    q = queries
    dots = jnp.zeros((q, LANES), F32)
    for k in range(chunks):
        cols = slice(k * LANES, (k + 1) * LANES)
        block = in_ref[k].astype(F32)
        key_ref[:, cols] = block[q : 2 * q]
        pool_ref[:, cols] = block[2 * q : 4 * q]
        g = block[:q]
        h_ref[:, cols] = g
        dots += g * unit_ref[:, cols]
    small = [
        pltpu.make_async_copy(key_ref, key_hbm, small_sem.at[0]),
        pltpu.make_async_copy(pool_ref, pool_hbm, small_sem.at[1]),
    ]
    for copy in small:
        copy.start()
    along = jnp.sum(dots, axis=1, keepdims=True)
    norm = norm_ref[:, :1]
    for k in range(chunks):
        cols = slice(k * LANES, (k + 1) * LANES)
        h = (h_ref[:, cols] - along * unit_ref[:, cols]) * (norm * gain_ref[:, cols])
        for i in range(q):
            row_ref[i, :, cols] = h[i : i + 1]
    token = lax.broadcasted_iota(jnp.int32, (tokens, 1), 0)

    def one_query(i, carry):
        length = len_ref[i]
        total = jnp.zeros((tokens, LANES), F32)
        for k in range(chunks):
            cols = slice(k * LANES, (k + 1) * LANES)
            total += x_ref[i, :, cols].astype(F32) * row_ref[i, :, cols]
        total = jnp.sum(total, axis=1, keepdims=True)
        inv = inv_ref[i][:, :1]
        scale = jnp.where(token < length, QUERY_SCALE * inv, 0.0) / length.astype(F32)
        back = scale * inv * inv * total / width
        for k in range(chunks):
            cols = slice(k * LANES, (k + 1) * LANES)
            x = x_ref[i, :, cols].astype(F32)
            grad_ref[i, :, cols] = (scale * row_ref[i, :, cols] - back * x).astype(BF16)
        pltpu.make_async_copy(grad_ref.at[i], grad_hbm.at[i], grad_sem.at[i]).start()
        return carry

    lax.fori_loop(0, queries, one_query, 0)
    for i in range(queries):
        pltpu.make_async_copy(grad_ref.at[i], grad_hbm.at[i], grad_sem.at[i]).wait()
    for copy in small:
        copy.wait()


def call(kernel, outs, args, flops, smem=(), hbm=(), scratch=(), vmem=40, out_hbm=False):
    def space(i):
        return pltpu.SMEM if i in smem else pltpu.HBM if i in hbm else pltpu.VMEM

    size = sum(a.size * a.dtype.itemsize for a in args) + sum(
        o.size * o.dtype.itemsize for o in outs
    )
    return pl.pallas_call(
        kernel,
        out_shape=list(outs),
        in_specs=[pl.BlockSpec(memory_space=space(i)) for i in range(len(args))],
        out_specs=[pl.BlockSpec(memory_space=pltpu.HBM if out_hbm else pltpu.VMEM)] * len(outs),
        scratch_shapes=list(scratch),
        compiler_params=pltpu.CompilerParams(vmem_limit_bytes=vmem * 1024 * 1024),
        cost_estimate=pl.CostEstimate(flops=flops, bytes_accessed=size, transcendentals=0),
    )(*args)


def shape(dims, dtype):
    return jax.ShapeDtypeStruct(dims, dtype)


def local(query_states, query_lengths, norm_gain, positives, mined_pool, hard_ids):
    owners = lax.axis_size("dp")
    groups = lax.axis_size("rep")
    me = lax.axis_index("dp").astype(jnp.int32).reshape(1)
    _, queries, tokens, width = query_states.shape
    hard = hard_ids.shape[2]
    chips = owners // 2
    q_all = queries * owners
    lengths = query_lengths.reshape(queries)
    gain_row = norm_gain.reshape(1, width)
    gain_tiles = norm_gain.reshape(chips, LANES)
    pair = [(i, i ^ 1) for i in range(owners)]
    same_core = [[2 * i + c for i in range(chips)] for c in range(2)]

    def among_chips(x):
        return lax.all_to_all(x, "dp", 0, 0, tiled=True, axis_index_groups=same_core)

    def bound(kernel):
        return lambda *refs: kernel(hard, *refs)

    out, unit, inv, norm = call(
        embed_kernel,
        [
            shape((chips, 5 * queries, LANES), BF16),
            shape((queries, width), F32),
            shape((queries, tokens, LANES), F32),
            shape((queries, LANES), F32),
        ],
        [me, query_lengths, query_states, gain_row, positives, mined_pool, hard_ids.transpose(2, 0, 1)],
        8_000_000,
        (0,),
        (1, 2, 3, 4, 5, 6),
        [
            pltpu.VMEM((chips, 5 * queries, LANES), BF16),
            pltpu.VMEM((queries, width), F32),
            pltpu.VMEM((queries, tokens, LANES), F32),
            pltpu.VMEM((queries, LANES), F32),
            pltpu.SemaphoreType.DMA((3 + chips // PART,)),
            pltpu.SMEM((1, queries), jnp.int32),
            pltpu.VMEM((queries, tokens, width), BF16),
            pltpu.VMEM((1, width), F32),
            pltpu.VMEM((1, queries, width), BF16),
            pltpu.VMEM((1, 2 * queries, width), BF16),
            pltpu.VMEM((hard, 1, queries), jnp.int32),
            pltpu.VMEM((queries, 1, width), F32),
            pltpu.SemaphoreType.DMA((queries,)),
            pltpu.SemaphoreType.DMA((5,)),
        ],
        60,
        True,
    )
    got = among_chips(out)
    gotx = lax.ppermute(got, "dp", pair)

    (part,) = call(
        bound(similar_kernel),
        [shape((chips, queries, q_all + LANES), F32)],
        [got, gotx],
        100_000_000,
    )
    scores = jnp.sum(among_chips(part.astype(F16)).astype(F32), axis=0)
    (sent,) = call(
        bound(softmax_kernel),
        [shape((chips, queries, q_all + LANES), BF16)],
        [me, scores],
        1_000_000,
        (0,),
    )
    weights = among_chips(sent)
    weightsx = lax.ppermute(weights, "dp", pair)

    half = q_all // 2
    shares = call(
        bound(own_kernel),
        [
            shape((half, LANES), F32),
            shape((half, LANES), F32),
            shape((q_all, LANES), F32),
            shape((1, LANES), F32),
        ],
        [weights, got, gotx],
        200_000_000,
    )
    (back,) = call(
        bound(slices_kernel),
        [shape((chips, 5 * queries, LANES), BF16)],
        [me, weightsx, got, gotx, gain_tiles, *shares],
        200_000_000,
        (0,),
    )
    home = among_chips(back)
    (gain_sent,) = call(
        gain_kernel, [shape((groups, width // LANES, LANES), F32)], [home], 100_000
    )
    gain_groups = lax.all_to_all(gain_sent, "rep", 0, 0, tiled=True)
    query_grad, key_grad, pool_grad = call(
        backward_kernel,
        [
            shape((queries, tokens, width), BF16),
            shape((queries, width), F32),
            shape((2 * queries, width), F32),
        ],
        [lengths, home, query_states[0], gain_row, unit, inv, norm],
        10_000_000,
        (0,),
        (),
        [
            pltpu.VMEM((queries, width), F32),
            pltpu.VMEM((queries, 1, width), F32),
            pltpu.VMEM((queries, tokens, width), BF16),
            pltpu.VMEM((queries, width), F32),
            pltpu.VMEM((2 * queries, width), F32),
            pltpu.SemaphoreType.DMA((queries,)),
            pltpu.SemaphoreType.DMA((2,)),
        ],
        out_hbm=True,
    )
    gain_grad = jnp.sum(gain_groups, axis=0).reshape(width)
    return query_grad[None], key_grad[None], pool_grad[None], gain_grad


def solution(mesh):
    placed = (
        P("rep", "dp", None, None),
        P("rep", "dp"),
        P(),
        P("rep", "dp", None),
        P("rep", "dp", None),
        P("rep", "dp", None),
    )
    return jax.shard_map(
        local,
        mesh=mesh,
        in_specs=placed,
        out_specs=(P("rep", "dp", None, None), P("rep", "dp", None), P("rep", "dp", None), P()),
        check_vma=False,
    )
```

```python
import jax
import jax.numpy as jnp
from jax import lax
from jax.experimental import pallas as pl
from jax.experimental.pallas import tpu as pltpu
from jax.sharding import PartitionSpec as P

TEMPERATURE = 0.02
QUERY_SCALE = 512.0
POOL_SCALE = 16.0
LANES = 128
F32 = jnp.float32
BF16 = jnp.bfloat16
F16 = jnp.float16
BY_COLUMN = (((0,), (0,)), ((), ()))
BY_ROW = (((1,), (1,)), ((), ()))


def embed_kernel(
    me_ref, len_hbm, x_hbm, gain_hbm, pos_hbm, pool_hbm, ids_hbm, out_ref, unit_ref, inv_ref, norm_ref,
    len_ref, x_ref, gain_ref, pos_ref, pool_ref, ids_ref, row_ref, x_sem, small_sem,
):
    queries, width = unit_ref.shape
    tokens = x_ref.shape[1]
    chunks = width // LANES
    small = [
        pltpu.make_async_copy(src, dst, small_sem.at[n])
        for n, (src, dst) in enumerate(
            [
                (len_hbm, len_ref),
                (gain_hbm, gain_ref),
                (pos_hbm, pos_ref),
                (pool_hbm, pool_ref),
                (ids_hbm, ids_ref),
            ]
        )
    ]
    small[0].start()
    states = [
        pltpu.make_async_copy(x_hbm.at[0, i], x_ref.at[i], x_sem.at[i]) for i in range(queries)
    ]
    for copy in states:
        copy.start()
    for copy in small[1:]:
        copy.start()
    small[0].wait()
    token = lax.broadcasted_iota(jnp.int32, (tokens, 1), 0)

    def one_query(i, carry):
        pltpu.make_async_copy(x_hbm.at[0, i], x_ref.at[i], x_sem.at[i]).wait()
        square = jnp.zeros((tokens, LANES), F32)
        for k in range(chunks):
            v = x_ref[i, :, k * LANES : (k + 1) * LANES].astype(F32)
            square += v * v
        inv = lax.rsqrt(jnp.sum(square, axis=1, keepdims=True) / width + 1e-05)
        inv_ref[i] = jnp.broadcast_to(inv, (tokens, LANES))
        length = len_ref[0, i]
        weight = jnp.where(token < length, inv, 0.0) / length.astype(F32)
        for k in range(chunks):
            cols = slice(k * LANES, (k + 1) * LANES)
            v = x_ref[i, :, cols].astype(F32) * weight
            row_ref[i, :, cols] = jnp.sum(v, axis=0, keepdims=True)
        return carry

    lax.fori_loop(0, queries, one_query, 0)
    for copy in small[1:]:
        copy.wait()
    square = jnp.zeros((queries, LANES), F32)
    for k in range(chunks):
        cols = slice(k * LANES, (k + 1) * LANES)
        pooled = jnp.concatenate([row_ref[i, :, cols] for i in range(queries)], axis=0)
        pooled = pooled * gain_ref[:, cols]
        unit_ref[:, cols] = pooled
        square += pooled * pooled
    norm = lax.rsqrt(jnp.sum(square, axis=1, keepdims=True) + 1e-06)
    norm_ref[...] = jnp.broadcast_to(norm, norm_ref.shape)
    ids = ids_ref[:, 0, :]
    hard = ids.shape[0]
    bits = (2 * queries - 1).bit_length()
    half = chunks * 2 * queries
    owner = ids >> bits
    other = jnp.where((owner & 1) == (me_ref[0] & 1), 0, half)
    place = other + ((owner >> 1) << bits) + (ids & (2 * queries - 1))
    row = lax.broadcasted_iota(jnp.int32, (hard, LANES), 0)
    lane = lax.broadcasted_iota(jnp.int32, (hard, LANES), 1)

    def lay(x, first):
        to = (lane == row + first).astype(F32).astype(BF16)
        return lax.dot_general(
            x.astype(F32).astype(BF16), to, BY_COLUMN, preferred_element_type=F32
        )

    count = jnp.zeros(place.shape, jnp.int32)
    for m in range(hard):
        count += (place == place[m : m + 1]).astype(jnp.int32)
    id_rows = lay(place >> 5, 0) + lay(place & 31, hard) + lay(count, 2 * hard)
    for k in range(chunks):
        cols = slice(k * LANES, (k + 1) * LANES)
        unit = unit_ref[:, cols] * norm
        unit_ref[:, cols] = unit
        rows = [pool_ref[0, :, cols].astype(F32), unit, pos_ref[0, :, cols].astype(F32), id_rows]
        out_ref[k] = jnp.concatenate(rows, axis=0).astype(BF16)


def rows_of(block, first, last):
    return block[:, first:last].reshape(block.shape[0] * (last - first), LANES)


def ids_of(rows, hard):
    lane = lax.broadcasted_iota(jnp.int32, rows.shape, 1)
    ids = rows * 32.0 + pltpu.roll(rows, LANES - hard, 1)
    return jnp.where(lane < hard, ids, 0.0).astype(jnp.int32)


def similar_kernel(hard, got_ref, gotx_ref, sim_ref):
    chips, rows, _ = got_ref.shape
    q = rows // 5
    half = chips * q
    n = 2 * half
    a = got_ref[:, 2 * q :].astype(F32)
    b = gotx_ref[:, 2 * q :].astype(F32)
    e = rows_of(a, 0, q).astype(BF16)
    p = jnp.concatenate([rows_of(a, q, 2 * q), rows_of(b, q, 2 * q)], axis=0).astype(BF16)
    own_pool = got_ref[:, : 2 * q].reshape(n, LANES)
    other_pool = gotx_ref[:, : 2 * q].reshape(n, LANES)
    ids = ids_of(rows_of(a, 2 * q, 3 * q), hard)
    sim = lax.dot_general(e, p, BY_ROW, preferred_element_type=F32) / TEMPERATURE
    sim_ref[:, :, :n] = sim.reshape(chips, q, n)
    own_sim = lax.dot_general(e, own_pool, BY_ROW, preferred_element_type=F32)
    other_sim = lax.dot_general(e, other_pool, BY_ROW, preferred_element_type=F32)
    tail = jnp.zeros((half, LANES), F32)
    within, tile = ids & (LANES - 1), ids >> 7
    for k in range(2 * n // LANES):
        part = own_sim if k < n // LANES else other_sim
        first = k * LANES % n
        picked = jnp.take_along_axis(
            part[:, first : first + LANES], within, axis=1, mode="promise_in_bounds"
        )
        tail = jnp.where(tile == k, picked, tail)
    lane = lax.broadcasted_iota(jnp.int32, (half, LANES), 1)
    tail = jnp.where(lane < hard, tail / TEMPERATURE, 0.0)
    sim_ref[:, :, n:] = tail.reshape(chips, q, LANES)


def softmax_kernel(hard, me_ref, in_ref, out_ref):
    copies, q, width = out_ref.shape
    n = width - LANES
    scores = in_ref[...]
    column = lax.broadcasted_iota(jnp.int32, (q, width), 1)
    row = lax.broadcasted_iota(jnp.int32, (q, width), 0)
    exps = jnp.where(column < n + hard, jnp.exp(scores), 0.0)
    soft = exps / jnp.sum(exps, axis=1, keepdims=True)
    own = column == row + (me_ref[0] >> 1) * q
    along = jnp.sum(soft * scores - jnp.where(own, scores, 0.0), axis=1, keepdims=True)
    high = along.astype(BF16).astype(F32)
    sent = jnp.where(column == n + hard, high, soft)
    sent = jnp.where(column == n + hard + 1, along - high, sent)
    sent = sent.astype(BF16)
    for k in range(copies):
        out_ref[k] = sent


def share(w, flip, hard, own_cols, other_cols, pos_all, pools, e, pos, id_rows):
    half = w.shape[0]
    n = 2 * half
    tail = w[:, n:]
    from_own, from_other = w[:, own_cols].astype(BF16), w[:, other_cols].astype(BF16)
    ids = ids_of(id_rows, hard) ^ flip
    weights = tail * pltpu.roll(id_rows, LANES - 2 * hard, 1)
    column = lax.broadcasted_iota(jnp.int32, (half, n), 1)
    own_spread = jnp.zeros((half, n), F32)
    other_spread = jnp.zeros((half, n), F32)
    for m in range(hard):
        one, weight = ids[:, m : m + 1], weights[:, m : m + 1]
        own_spread = jnp.where(column == one, weight, own_spread)
        other_spread = jnp.where(column == one - n, weight, other_spread)
    own_spread = own_spread.astype(BF16)
    other_spread = other_spread.astype(BF16)

    def dot(left, right):
        return jnp.dot(left, right, preferred_element_type=F32)

    numerator = dot(from_own, pos_all[0].astype(BF16)) + dot(from_other, pos_all[1].astype(BF16))
    numerator += dot(own_spread, pools[0]) + dot(other_spread, pools[1])
    along = tail[:, hard : hard + 1] + tail[:, hard + 1 : hard + 2]
    emb_grad = (numerator - pos) / TEMPERATURE - along * e
    eh = e.astype(BF16)
    key = lax.dot_general(from_own, eh, BY_COLUMN, preferred_element_type=F32)
    pool = lax.dot_general(own_spread, eh, BY_COLUMN, preferred_element_type=F32)
    return emb_grad, key, pool, jnp.sum(emb_grad * e, axis=0, keepdims=True)


def blocks(got_ref, gotx_ref, q):
    n = got_ref.shape[0] * 2 * q
    a = got_ref[:, 2 * q :].astype(F32)
    b = gotx_ref[:, 2 * q :].astype(F32)
    pools = got_ref[:, : 2 * q].reshape(n, LANES), gotx_ref[:, : 2 * q].reshape(n, LANES)
    return a, b, (rows_of(a, q, 2 * q), rows_of(b, q, 2 * q)), pools


def own_kernel(hard, w_ref, got_ref, gotx_ref, emb_ref, key_ref, pool_ref, gain_ref):
    chips, q, width = w_ref.shape
    half = chips * q
    a, _, pos_all, pools = blocks(got_ref, gotx_ref, q)
    w = w_ref[...].astype(F32).reshape(half, width)
    e = rows_of(a, 0, q)
    emb_ref[...], key, pool_ref[...], gain_ref[...] = share(
        w, 0, hard, slice(0, half), slice(half, 2 * half), pos_all, pools, e, pos_all[0],
        rows_of(a, 2 * q, 3 * q),
    )
    key_ref[...] = key - e


def slices_kernel(
    hard, me_ref, wx_ref, got_ref, gotx_ref, gain_ref, emb_ref, key_ref, pool_ref, part_ref, out_ref
):
    chips, q, width = wx_ref.shape
    half = chips * q
    _, b, pos_all, pools = blocks(got_ref, gotx_ref, q)
    w = wx_ref[...].astype(F32).reshape(half, width)
    _, key, pool, gain_part = share(
        w, 2 * half, hard, slice(half, 2 * half), slice(0, half), pos_all, pools, rows_of(b, 0, q), pos_all[1],
        rows_of(b, 2 * q, 3 * q),
    )
    emb_grad = emb_ref[...]
    key = (key + key_ref[...]) / TEMPERATURE
    pool = (pool + pool_ref[...]) * (POOL_SCALE / TEMPERATURE)
    gain_part = (gain_part + part_ref[...]) / gain_ref[pl.ds(me_ref[0] >> 1, 1), :]
    gain_high = gain_part.astype(BF16).astype(F32)
    row = lax.broadcasted_iota(jnp.int32, (q, LANES), 0)
    gain_rows = jnp.where(row == 0, gain_high, jnp.where(row == 1, gain_part - gain_high, 0.0))
    for k in range(chips):
        rows = slice(k * q, (k + 1) * q)
        block = [emb_grad[rows], key[rows], pool[2 * k * q : 2 * (k + 1) * q], gain_rows]
        out_ref[k] = jnp.concatenate(block, axis=0).astype(BF16)


def gain_kernel(in_ref, out_ref):
    copies, _, _ = out_ref.shape
    q = in_ref.shape[1] // 5
    both = jnp.sum(in_ref[:, 4 * q :].astype(F32), axis=1)
    for r in range(copies):
        out_ref[r] = both


def backward_kernel(
    len_ref, in_ref, x_ref, gain_ref, unit_ref, inv_ref, norm_ref, grad_ref, key_ref, pool_ref, h_ref, row_ref
):
    queries, width = unit_ref.shape
    tokens = x_ref.shape[1]
    chunks = width // LANES
    q = queries
    dots = jnp.zeros((q, LANES), F32)
    for k in range(chunks):
        cols = slice(k * LANES, (k + 1) * LANES)
        block = in_ref[k].astype(F32)
        key_ref[:, cols] = block[q : 2 * q]
        pool_ref[:, cols] = block[2 * q : 4 * q]
        g = block[:q]
        h_ref[:, cols] = g
        dots += g * unit_ref[:, cols]
    along = jnp.sum(dots, axis=1, keepdims=True)
    norm = norm_ref[:, :1]
    for k in range(chunks):
        cols = slice(k * LANES, (k + 1) * LANES)
        h = (h_ref[:, cols] - along * unit_ref[:, cols]) * (norm * gain_ref[:, cols])
        for i in range(q):
            row_ref[i, :, cols] = h[i : i + 1]
    token = lax.broadcasted_iota(jnp.int32, (tokens, 1), 0)

    def one_query(i, carry):
        length = len_ref[i]
        total = jnp.zeros((tokens, LANES), F32)
        for k in range(chunks):
            cols = slice(k * LANES, (k + 1) * LANES)
            total += x_ref[i, :, cols].astype(F32) * row_ref[i, :, cols]
        total = jnp.sum(total, axis=1, keepdims=True)
        inv = inv_ref[i][:, :1]
        scale = jnp.where(token < length, QUERY_SCALE * inv, 0.0) / length.astype(F32)
        back = scale * inv * inv * total / width
        for k in range(chunks):
            cols = slice(k * LANES, (k + 1) * LANES)
            x = x_ref[i, :, cols].astype(F32)
            grad_ref[i, :, cols] = (scale * row_ref[i, :, cols] - back * x).astype(BF16)
        return carry

    lax.fori_loop(0, queries, one_query, 0)


def call(kernel, outs, args, flops, smem=(), hbm=(), scratch=(), vmem=40):
    def space(i):
        return pltpu.SMEM if i in smem else pltpu.HBM if i in hbm else pltpu.VMEM

    size = sum(a.size * a.dtype.itemsize for a in args) + sum(
        o.size * o.dtype.itemsize for o in outs
    )
    return pl.pallas_call(
        kernel,
        out_shape=list(outs),
        in_specs=[pl.BlockSpec(memory_space=space(i)) for i in range(len(args))],
        out_specs=[pl.BlockSpec(memory_space=pltpu.VMEM)] * len(outs),
        scratch_shapes=list(scratch),
        compiler_params=pltpu.CompilerParams(vmem_limit_bytes=vmem * 1024 * 1024),
        cost_estimate=pl.CostEstimate(flops=flops, bytes_accessed=size, transcendentals=0),
    )(*args)


def shape(dims, dtype):
    return jax.ShapeDtypeStruct(dims, dtype)


def local(query_states, query_lengths, norm_gain, positives, mined_pool, hard_ids):
    owners = lax.axis_size("dp")
    groups = lax.axis_size("rep")
    me = lax.axis_index("dp").astype(jnp.int32).reshape(1)
    _, queries, tokens, width = query_states.shape
    hard = hard_ids.shape[2]
    chips = owners // 2
    q_all = queries * owners
    lengths = query_lengths.reshape(queries)
    gain_row = norm_gain.reshape(1, width)
    gain_tiles = norm_gain.reshape(chips, LANES)
    pair = [(i, i ^ 1) for i in range(owners)]
    same_core = [[2 * i + c for i in range(chips)] for c in range(2)]

    def among_chips(x):
        return lax.all_to_all(x, "dp", 0, 0, tiled=True, axis_index_groups=same_core)

    def bound(kernel):
        return lambda *refs: kernel(hard, *refs)

    out, unit, inv, norm = call(
        embed_kernel,
        [
            shape((chips, 5 * queries, LANES), BF16),
            shape((queries, width), F32),
            shape((queries, tokens, LANES), F32),
            shape((queries, LANES), F32),
        ],
        [me, query_lengths, query_states, gain_row, positives, mined_pool, hard_ids.transpose(2, 0, 1)],
        8_000_000,
        (0,),
        (1, 2, 3, 4, 5, 6),
        [
            pltpu.SMEM((1, queries), jnp.int32),
            pltpu.VMEM((queries, tokens, width), BF16),
            pltpu.VMEM((1, width), F32),
            pltpu.VMEM((1, queries, width), BF16),
            pltpu.VMEM((1, 2 * queries, width), BF16),
            pltpu.VMEM((hard, 1, queries), jnp.int32),
            pltpu.VMEM((queries, 1, width), F32),
            pltpu.SemaphoreType.DMA((queries,)),
            pltpu.SemaphoreType.DMA((5,)),
        ],
        60,
    )
    got = among_chips(out)
    gotx = lax.ppermute(got, "dp", pair)

    (part,) = call(
        bound(similar_kernel),
        [shape((chips, queries, q_all + LANES), F32)],
        [got, gotx],
        100_000_000,
    )
    scores = jnp.sum(among_chips(part.astype(F16)).astype(F32), axis=0)
    (sent,) = call(
        bound(softmax_kernel),
        [shape((chips, queries, q_all + LANES), BF16)],
        [me, scores],
        1_000_000,
        (0,),
    )
    weights = among_chips(sent)
    weightsx = lax.ppermute(weights, "dp", pair)

    half = q_all // 2
    shares = call(
        bound(own_kernel),
        [
            shape((half, LANES), F32),
            shape((half, LANES), F32),
            shape((q_all, LANES), F32),
            shape((1, LANES), F32),
        ],
        [weights, got, gotx],
        200_000_000,
    )
    (back,) = call(
        bound(slices_kernel),
        [shape((chips, 5 * queries, LANES), BF16)],
        [me, weightsx, got, gotx, gain_tiles, *shares],
        200_000_000,
        (0,),
    )
    home = among_chips(back)
    (gain_sent,) = call(
        gain_kernel, [shape((groups, width // LANES, LANES), F32)], [home], 100_000
    )
    gain_groups = lax.all_to_all(gain_sent, "rep", 0, 0, tiled=True)
    query_grad, key_grad, pool_grad = call(
        backward_kernel,
        [
            shape((queries, tokens, width), BF16),
            shape((queries, width), F32),
            shape((2 * queries, width), F32),
        ],
        [lengths, home, query_states[0], gain_row, unit, inv, norm],
        10_000_000,
        (0,),
        (),
        [pltpu.VMEM((queries, width), F32), pltpu.VMEM((queries, 1, width), F32)],
    )
    gain_grad = jnp.sum(gain_groups, axis=0).reshape(width)
    return query_grad[None], key_grad[None], pool_grad[None], gain_grad


def solution(mesh):
    placed = (
        P("rep", "dp", None, None),
        P("rep", "dp"),
        P(),
        P("rep", "dp", None),
        P("rep", "dp", None),
        P("rep", "dp", None),
    )
    return jax.shard_map(
        local,
        mesh=mesh,
        in_specs=placed,
        out_specs=(P("rep", "dp", None, None), P("rep", "dp", None), P("rep", "dp", None), P()),
        check_vma=False,
    )
```

```python
import jax
import jax.numpy as jnp
from jax import lax
from jax.experimental import pallas as pl
from jax.experimental.pallas import tpu as pltpu
from jax.sharding import PartitionSpec as P

TEMPERATURE = 0.02
QUERY_SCALE = 512.0
POOL_SCALE = 16.0
LANES = 128
F32 = jnp.float32
BF16 = jnp.bfloat16
F16 = jnp.float16
BY_COLUMN = (((0,), (0,)), ((), ()))
BY_ROW = (((1,), (1,)), ((), ()))


def embed_kernel(
    me_ref, len_hbm, x_hbm, gain_hbm, pos_hbm, pool_hbm, ids_hbm, out_ref, unit_ref, inv_ref, norm_ref,
    len_ref, x_ref, gain_ref, pos_ref, pool_ref, ids_ref, row_ref, x_sem, small_sem,
):
    queries, width = unit_ref.shape
    tokens = x_ref.shape[1]
    chunks = width // LANES
    small = [
        pltpu.make_async_copy(src, dst, small_sem.at[n])
        for n, (src, dst) in enumerate(
            [
                (len_hbm, len_ref),
                (gain_hbm, gain_ref),
                (pos_hbm, pos_ref),
                (pool_hbm, pool_ref),
                (ids_hbm, ids_ref),
            ]
        )
    ]
    small[0].start()
    states = [
        pltpu.make_async_copy(x_hbm.at[0, i], x_ref.at[i], x_sem.at[i]) for i in range(queries)
    ]
    for copy in states:
        copy.start()
    for copy in small[1:]:
        copy.start()
    small[0].wait()
    token = lax.broadcasted_iota(jnp.int32, (tokens, 1), 0)

    def one_query(i, carry):
        pltpu.make_async_copy(x_hbm.at[0, i], x_ref.at[i], x_sem.at[i]).wait()
        square = jnp.zeros((tokens, LANES), F32)
        for k in range(chunks):
            v = x_ref[i, :, k * LANES : (k + 1) * LANES].astype(F32)
            square += v * v
        inv = lax.rsqrt(jnp.sum(square, axis=1, keepdims=True) / width + 1e-05)
        inv_ref[i] = jnp.broadcast_to(inv, (tokens, LANES))
        length = len_ref[0, i]
        weight = jnp.where(token < length, inv, 0.0) / length.astype(F32)
        for k in range(chunks):
            cols = slice(k * LANES, (k + 1) * LANES)
            v = x_ref[i, :, cols].astype(F32) * weight
            row_ref[i, :, cols] = jnp.sum(v, axis=0, keepdims=True)
        return carry

    lax.fori_loop(0, queries, one_query, 0)
    for copy in small[1:]:
        copy.wait()
    square = jnp.zeros((queries, LANES), F32)
    for k in range(chunks):
        cols = slice(k * LANES, (k + 1) * LANES)
        pooled = jnp.concatenate([row_ref[i, :, cols] for i in range(queries)], axis=0)
        pooled = pooled * gain_ref[:, cols]
        unit_ref[:, cols] = pooled
        square += pooled * pooled
    norm = lax.rsqrt(jnp.sum(square, axis=1, keepdims=True) + 1e-06)
    norm_ref[...] = jnp.broadcast_to(norm, norm_ref.shape)
    ids = ids_ref[:, 0, :]
    hard = ids.shape[0]
    bits = (2 * queries - 1).bit_length()
    half = chunks * 2 * queries
    owner = ids >> bits
    other = jnp.where((owner & 1) == (me_ref[0] & 1), 0, half)
    place = other + ((owner >> 1) << bits) + (ids & (2 * queries - 1))
    row = lax.broadcasted_iota(jnp.int32, (hard, LANES), 0)
    lane = lax.broadcasted_iota(jnp.int32, (hard, LANES), 1)

    def lay(x, first):
        to = (lane == row + first).astype(F32).astype(BF16)
        return lax.dot_general(
            x.astype(F32).astype(BF16), to, BY_COLUMN, preferred_element_type=F32
        )

    count = jnp.zeros(place.shape, jnp.int32)
    for m in range(hard):
        count += (place == place[m : m + 1]).astype(jnp.int32)
    id_rows = lay(place >> 5, 0) + lay(place & 31, hard) + lay(count, 2 * hard)
    for k in range(chunks):
        cols = slice(k * LANES, (k + 1) * LANES)
        unit = unit_ref[:, cols] * norm
        unit_ref[:, cols] = unit
        rows = [pool_ref[0, :, cols].astype(F32), unit, pos_ref[0, :, cols].astype(F32), id_rows]
        out_ref[k] = jnp.concatenate(rows, axis=0).astype(BF16)


def rows_of(block, first, last):
    return block[:, first:last].reshape(block.shape[0] * (last - first), LANES)


def ids_of(rows, hard):
    lane = lax.broadcasted_iota(jnp.int32, rows.shape, 1)
    ids = rows * 32.0 + pltpu.roll(rows, LANES - hard, 1)
    return jnp.where(lane < hard, ids, 0.0).astype(jnp.int32)


def half_similar(hard, e, pos, pool, ids, first):
    sim = lax.dot_general(e, pos, BY_ROW, preferred_element_type=F32)
    mined = lax.dot_general(e, pool, BY_ROW, preferred_element_type=F32)
    tail = jnp.zeros(ids.shape, F32)
    within, tile = ids & (LANES - 1), ids >> 7
    for k in range(pool.shape[0] // LANES):
        part = mined[:, k * LANES : (k + 1) * LANES]
        picked = jnp.take_along_axis(part, within, axis=1, mode="promise_in_bounds")
        tail = jnp.where(tile == first + k, picked, tail)
    return sim, tail


def own_similar_kernel(hard, got_ref, sim_ref, tail_ref):
    chips, rows, _ = got_ref.shape
    q = rows // 5
    a = got_ref[:, 2 * q :].astype(F32)
    e, pos = rows_of(a, 0, q).astype(BF16), rows_of(a, q, 2 * q).astype(BF16)
    pool = got_ref[:, : 2 * q].reshape(chips * 2 * q, LANES)
    ids = ids_of(rows_of(a, 2 * q, 3 * q), hard)
    sim_ref[...], tail_ref[...] = half_similar(hard, e, pos, pool, ids, 0)


def similar_kernel(hard, got_ref, gotx_ref, own_ref, own_tail_ref, sim_ref):
    chips, rows, _ = got_ref.shape
    q = rows // 5
    half = chips * q
    n = 2 * half
    a = got_ref[:, 2 * q :].astype(F32)
    b = gotx_ref[:, 2 * q :].astype(F32)
    e, pos = rows_of(a, 0, q).astype(BF16), rows_of(b, q, 2 * q).astype(BF16)
    pool = gotx_ref[:, : 2 * q].reshape(n, LANES)
    ids = ids_of(rows_of(a, 2 * q, 3 * q), hard)
    sim, tail = half_similar(hard, e, pos, pool, ids, n // LANES)
    lane = lax.broadcasted_iota(jnp.int32, (half, LANES), 1)
    tail = jnp.where(lane < hard, (tail + own_tail_ref[...]) / TEMPERATURE, 0.0)
    sim_ref[:, :, :half] = (own_ref[...] / TEMPERATURE).reshape(chips, q, half)
    sim_ref[:, :, half:n] = (sim / TEMPERATURE).reshape(chips, q, half)
    sim_ref[:, :, n:] = tail.reshape(chips, q, LANES)


def softmax_kernel(hard, me_ref, in_ref, out_ref):
    copies, q, width = out_ref.shape
    n = width - LANES
    scores = in_ref[...]
    column = lax.broadcasted_iota(jnp.int32, (q, width), 1)
    row = lax.broadcasted_iota(jnp.int32, (q, width), 0)
    exps = jnp.where(column < n + hard, jnp.exp(scores), 0.0)
    soft = exps / jnp.sum(exps, axis=1, keepdims=True)
    own = column == row + (me_ref[0] >> 1) * q
    along = jnp.sum(soft * scores - jnp.where(own, scores, 0.0), axis=1, keepdims=True)
    high = along.astype(BF16).astype(F32)
    sent = jnp.where(column == n + hard, high, soft)
    sent = jnp.where(column == n + hard + 1, along - high, sent)
    sent = sent.astype(BF16)
    for k in range(copies):
        out_ref[k] = sent


def share(w, flip, hard, own_cols, other_cols, pos_all, pools, e, pos, id_rows):
    half = w.shape[0]
    n = 2 * half
    tail = w[:, n:]
    from_own, from_other = w[:, own_cols].astype(BF16), w[:, other_cols].astype(BF16)
    ids = ids_of(id_rows, hard) ^ flip
    weights = tail * pltpu.roll(id_rows, LANES - 2 * hard, 1)
    column = lax.broadcasted_iota(jnp.int32, (half, n), 1)
    own_spread = jnp.zeros((half, n), F32)
    other_spread = jnp.zeros((half, n), F32)
    for m in range(hard):
        one, weight = ids[:, m : m + 1], weights[:, m : m + 1]
        own_spread = jnp.where(column == one, weight, own_spread)
        other_spread = jnp.where(column == one - n, weight, other_spread)
    own_spread = own_spread.astype(BF16)
    other_spread = other_spread.astype(BF16)

    def dot(left, right):
        return jnp.dot(left, right, preferred_element_type=F32)

    numerator = dot(from_own, pos_all[0].astype(BF16)) + dot(from_other, pos_all[1].astype(BF16))
    numerator += dot(own_spread, pools[0]) + dot(other_spread, pools[1])
    along = tail[:, hard : hard + 1] + tail[:, hard + 1 : hard + 2]
    emb_grad = (numerator - pos) / TEMPERATURE - along * e
    eh = e.astype(BF16)
    key = lax.dot_general(from_own, eh, BY_COLUMN, preferred_element_type=F32)
    pool = lax.dot_general(own_spread, eh, BY_COLUMN, preferred_element_type=F32)
    return emb_grad, key, pool, jnp.sum(emb_grad * e, axis=0, keepdims=True)


def blocks(got_ref, gotx_ref, q):
    n = got_ref.shape[0] * 2 * q
    a = got_ref[:, 2 * q :].astype(F32)
    b = gotx_ref[:, 2 * q :].astype(F32)
    pools = got_ref[:, : 2 * q].reshape(n, LANES), gotx_ref[:, : 2 * q].reshape(n, LANES)
    return a, b, (rows_of(a, q, 2 * q), rows_of(b, q, 2 * q)), pools


def own_kernel(hard, w_ref, got_ref, gotx_ref, emb_ref, key_ref, pool_ref, gain_ref):
    chips, q, width = w_ref.shape
    half = chips * q
    a, _, pos_all, pools = blocks(got_ref, gotx_ref, q)
    w = w_ref[...].astype(F32).reshape(half, width)
    e = rows_of(a, 0, q)
    emb_ref[...], key, pool_ref[...], gain_ref[...] = share(
        w, 0, hard, slice(0, half), slice(half, 2 * half), pos_all, pools, e, pos_all[0],
        rows_of(a, 2 * q, 3 * q),
    )
    key_ref[...] = key - e


def slices_kernel(
    hard, me_ref, wx_ref, got_ref, gotx_ref, gain_ref, emb_ref, key_ref, pool_ref, part_ref, out_ref
):
    chips, q, width = wx_ref.shape
    half = chips * q
    _, b, pos_all, pools = blocks(got_ref, gotx_ref, q)
    w = wx_ref[...].astype(F32).reshape(half, width)
    _, key, pool, gain_part = share(
        w, 2 * half, hard, slice(half, 2 * half), slice(0, half), pos_all, pools, rows_of(b, 0, q), pos_all[1],
        rows_of(b, 2 * q, 3 * q),
    )
    emb_grad = emb_ref[...]
    key = (key + key_ref[...]) / TEMPERATURE
    pool = (pool + pool_ref[...]) * (POOL_SCALE / TEMPERATURE)
    gain_part = (gain_part + part_ref[...]) / gain_ref[pl.ds(me_ref[0] >> 1, 1), :]
    gain_high = gain_part.astype(BF16).astype(F32)
    row = lax.broadcasted_iota(jnp.int32, (q, LANES), 0)
    gain_rows = jnp.where(row == 0, gain_high, jnp.where(row == 1, gain_part - gain_high, 0.0))
    for k in range(chips):
        rows = slice(k * q, (k + 1) * q)
        block = [emb_grad[rows], key[rows], pool[2 * k * q : 2 * (k + 1) * q], gain_rows]
        out_ref[k] = jnp.concatenate(block, axis=0).astype(BF16)


def gain_kernel(in_ref, out_ref):
    copies, _, _ = out_ref.shape
    q = in_ref.shape[1] // 5
    both = jnp.sum(in_ref[:, 4 * q :].astype(F32), axis=1)
    for r in range(copies):
        out_ref[r] = both


def backward_kernel(
    len_ref, in_ref, x_ref, gain_ref, unit_ref, inv_ref, norm_ref, grad_ref, key_ref, pool_ref, h_ref, row_ref
):
    queries, width = unit_ref.shape
    tokens = x_ref.shape[1]
    chunks = width // LANES
    q = queries
    dots = jnp.zeros((q, LANES), F32)
    for k in range(chunks):
        cols = slice(k * LANES, (k + 1) * LANES)
        block = in_ref[k].astype(F32)
        key_ref[:, cols] = block[q : 2 * q]
        pool_ref[:, cols] = block[2 * q : 4 * q]
        g = block[:q]
        h_ref[:, cols] = g
        dots += g * unit_ref[:, cols]
    along = jnp.sum(dots, axis=1, keepdims=True)
    norm = norm_ref[:, :1]
    for k in range(chunks):
        cols = slice(k * LANES, (k + 1) * LANES)
        h = (h_ref[:, cols] - along * unit_ref[:, cols]) * (norm * gain_ref[:, cols])
        for i in range(q):
            row_ref[i, :, cols] = h[i : i + 1]
    token = lax.broadcasted_iota(jnp.int32, (tokens, 1), 0)

    def one_query(i, carry):
        length = len_ref[i]
        total = jnp.zeros((tokens, LANES), F32)
        for k in range(chunks):
            cols = slice(k * LANES, (k + 1) * LANES)
            total += x_ref[i, :, cols].astype(F32) * row_ref[i, :, cols]
        total = jnp.sum(total, axis=1, keepdims=True)
        inv = inv_ref[i][:, :1]
        scale = jnp.where(token < length, QUERY_SCALE * inv, 0.0) / length.astype(F32)
        back = scale * inv * inv * total / width
        for k in range(chunks):
            cols = slice(k * LANES, (k + 1) * LANES)
            x = x_ref[i, :, cols].astype(F32)
            grad_ref[i, :, cols] = (scale * row_ref[i, :, cols] - back * x).astype(BF16)
        return carry

    lax.fori_loop(0, queries, one_query, 0)


def call(kernel, outs, args, flops, smem=(), hbm=(), scratch=(), vmem=40):
    def space(i):
        return pltpu.SMEM if i in smem else pltpu.HBM if i in hbm else pltpu.VMEM

    size = sum(a.size * a.dtype.itemsize for a in args) + sum(
        o.size * o.dtype.itemsize for o in outs
    )
    return pl.pallas_call(
        kernel,
        out_shape=list(outs),
        in_specs=[pl.BlockSpec(memory_space=space(i)) for i in range(len(args))],
        out_specs=[pl.BlockSpec(memory_space=pltpu.VMEM)] * len(outs),
        scratch_shapes=list(scratch),
        compiler_params=pltpu.CompilerParams(vmem_limit_bytes=vmem * 1024 * 1024),
        cost_estimate=pl.CostEstimate(flops=flops, bytes_accessed=size, transcendentals=0),
    )(*args)


def shape(dims, dtype):
    return jax.ShapeDtypeStruct(dims, dtype)


def local(query_states, query_lengths, norm_gain, positives, mined_pool, hard_ids):
    owners = lax.axis_size("dp")
    groups = lax.axis_size("rep")
    me = lax.axis_index("dp").astype(jnp.int32).reshape(1)
    _, queries, tokens, width = query_states.shape
    hard = hard_ids.shape[2]
    chips = owners // 2
    q_all = queries * owners
    lengths = query_lengths.reshape(queries)
    gain_row = norm_gain.reshape(1, width)
    gain_tiles = norm_gain.reshape(chips, LANES)
    pair = [(i, i ^ 1) for i in range(owners)]
    same_core = [[2 * i + c for i in range(chips)] for c in range(2)]

    def among_chips(x):
        return lax.all_to_all(x, "dp", 0, 0, tiled=True, axis_index_groups=same_core)

    def bound(kernel):
        return lambda *refs: kernel(hard, *refs)

    out, unit, inv, norm = call(
        embed_kernel,
        [
            shape((chips, 5 * queries, LANES), BF16),
            shape((queries, width), F32),
            shape((queries, tokens, LANES), F32),
            shape((queries, LANES), F32),
        ],
        [me, query_lengths, query_states, gain_row, positives, mined_pool, hard_ids.transpose(2, 0, 1)],
        8_000_000,
        (0,),
        (1, 2, 3, 4, 5, 6),
        [
            pltpu.SMEM((1, queries), jnp.int32),
            pltpu.VMEM((queries, tokens, width), BF16),
            pltpu.VMEM((1, width), F32),
            pltpu.VMEM((1, queries, width), BF16),
            pltpu.VMEM((1, 2 * queries, width), BF16),
            pltpu.VMEM((hard, 1, queries), jnp.int32),
            pltpu.VMEM((queries, 1, width), F32),
            pltpu.SemaphoreType.DMA((queries,)),
            pltpu.SemaphoreType.DMA((5,)),
        ],
        60,
    )
    got = among_chips(out)
    gotx = lax.ppermute(got, "dp", pair)

    half = q_all // 2
    own = call(
        bound(own_similar_kernel),
        [shape((half, half), F32), shape((half, LANES), F32)],
        [got],
        50_000_000,
    )
    (part,) = call(
        bound(similar_kernel),
        [shape((chips, queries, q_all + LANES), F32)],
        [got, gotx, *own],
        50_000_000,
    )
    scores = jnp.sum(among_chips(part.astype(F16)).astype(F32), axis=0)
    (sent,) = call(
        bound(softmax_kernel),
        [shape((chips, queries, q_all + LANES), BF16)],
        [me, scores],
        1_000_000,
        (0,),
    )
    weights = among_chips(sent)
    weightsx = lax.ppermute(weights, "dp", pair)

    half = q_all // 2
    shares = call(
        bound(own_kernel),
        [
            shape((half, LANES), F32),
            shape((half, LANES), F32),
            shape((q_all, LANES), F32),
            shape((1, LANES), F32),
        ],
        [weights, got, gotx],
        200_000_000,
    )
    (back,) = call(
        bound(slices_kernel),
        [shape((chips, 5 * queries, LANES), BF16)],
        [me, weightsx, got, gotx, gain_tiles, *shares],
        200_000_000,
        (0,),
    )
    home = among_chips(back)
    (gain_sent,) = call(
        gain_kernel, [shape((groups, width // LANES, LANES), F32)], [home], 100_000
    )
    gain_groups = lax.all_to_all(gain_sent, "rep", 0, 0, tiled=True)
    query_grad, key_grad, pool_grad = call(
        backward_kernel,
        [
            shape((queries, tokens, width), BF16),
            shape((queries, width), F32),
            shape((2 * queries, width), F32),
        ],
        [lengths, home, query_states[0], gain_row, unit, inv, norm],
        10_000_000,
        (0,),
        (),
        [pltpu.VMEM((queries, width), F32), pltpu.VMEM((queries, 1, width), F32)],
    )
    gain_grad = jnp.sum(gain_groups, axis=0).reshape(width)
    return query_grad[None], key_grad[None], pool_grad[None], gain_grad


def solution(mesh):
    placed = (
        P("rep", "dp", None, None),
        P("rep", "dp"),
        P(),
        P("rep", "dp", None),
        P("rep", "dp", None),
        P("rep", "dp", None),
    )
    return jax.shard_map(
        local,
        mesh=mesh,
        in_specs=placed,
        out_specs=(P("rep", "dp", None, None), P("rep", "dp", None), P("rep", "dp", None), P()),
        check_vma=False,
    )
```

```python
import jax
import jax.numpy as jnp
from jax import lax
from jax.experimental import pallas as pl
from jax.experimental.pallas import tpu as pltpu
from jax.sharding import PartitionSpec as P

TEMPERATURE = 0.02
QUERY_SCALE = 512.0
POOL_SCALE = 16.0
LANES = 128
F32 = jnp.float32
BF16 = jnp.bfloat16
F16 = jnp.float16
BY_COLUMN = (((0,), (0,)), ((), ()))
BY_ROW = (((1,), (1,)), ((), ()))


def embed_kernel(
    me_ref, len_hbm, x_hbm, gain_hbm, pos_hbm, pool_hbm, ids_hbm, out_ref, unit_ref, inv_ref, norm_ref,
    len_ref, x_ref, gain_ref, pos_ref, pool_ref, ids_ref, row_ref, x_sem, small_sem,
):
    queries, width = unit_ref.shape
    tokens = x_ref.shape[1]
    chunks = width // LANES
    small = [
        pltpu.make_async_copy(src, dst, small_sem.at[n])
        for n, (src, dst) in enumerate(
            [
                (len_hbm, len_ref),
                (gain_hbm, gain_ref),
                (pos_hbm, pos_ref),
                (pool_hbm, pool_ref),
                (ids_hbm, ids_ref),
            ]
        )
    ]
    small[0].start()
    states = [
        pltpu.make_async_copy(x_hbm.at[0, i], x_ref.at[i], x_sem.at[i]) for i in range(queries)
    ]
    for copy in states:
        copy.start()
    for copy in small[1:]:
        copy.start()
    small[0].wait()
    token = lax.broadcasted_iota(jnp.int32, (tokens, 1), 0)

    def one_query(i, carry):
        pltpu.make_async_copy(x_hbm.at[0, i], x_ref.at[i], x_sem.at[i]).wait()
        square = jnp.zeros((tokens, LANES), F32)
        for k in range(chunks):
            v = x_ref[i, :, k * LANES : (k + 1) * LANES].astype(F32)
            square += v * v
        inv = lax.rsqrt(jnp.sum(square, axis=1, keepdims=True) / width + 1e-05)
        inv_ref[i] = jnp.broadcast_to(inv, (tokens, LANES))
        length = len_ref[0, i]
        weight = jnp.where(token < length, inv, 0.0) / length.astype(F32)
        for k in range(chunks):
            cols = slice(k * LANES, (k + 1) * LANES)
            v = x_ref[i, :, cols].astype(F32) * weight
            row_ref[i, :, cols] = jnp.sum(v, axis=0, keepdims=True)
        return carry

    lax.fori_loop(0, queries, one_query, 0)
    for copy in small[1:]:
        copy.wait()
    square = jnp.zeros((queries, LANES), F32)
    for k in range(chunks):
        cols = slice(k * LANES, (k + 1) * LANES)
        pooled = jnp.concatenate([row_ref[i, :, cols] for i in range(queries)], axis=0)
        pooled = pooled * gain_ref[:, cols]
        unit_ref[:, cols] = pooled
        square += pooled * pooled
    norm = lax.rsqrt(jnp.sum(square, axis=1, keepdims=True) + 1e-06)
    norm_ref[...] = jnp.broadcast_to(norm, norm_ref.shape)
    ids = ids_ref[:, 0, :]
    hard = ids.shape[0]
    bits = (2 * queries - 1).bit_length()
    half = chunks * 2 * queries
    owner = ids >> bits
    other = jnp.where((owner & 1) == (me_ref[0] & 1), 0, half)
    place = other + ((owner >> 1) << bits) + (ids & (2 * queries - 1))
    row = lax.broadcasted_iota(jnp.int32, (hard, LANES), 0)
    lane = lax.broadcasted_iota(jnp.int32, (hard, LANES), 1)

    def lay(x, first):
        to = (lane == row + first).astype(F32).astype(BF16)
        return lax.dot_general(
            x.astype(F32).astype(BF16), to, BY_COLUMN, preferred_element_type=F32
        )

    count = jnp.zeros(place.shape, jnp.int32)
    for m in range(hard):
        count += (place == place[m : m + 1]).astype(jnp.int32)
    id_rows = lay(place >> 5, 0) + lay(place & 31, hard) + lay(count, 2 * hard)
    for k in range(chunks):
        cols = slice(k * LANES, (k + 1) * LANES)
        unit = unit_ref[:, cols] * norm
        unit_ref[:, cols] = unit
        rows = [pool_ref[0, :, cols].astype(F32), unit, pos_ref[0, :, cols].astype(F32), id_rows]
        out_ref[k] = jnp.concatenate(rows, axis=0).astype(BF16)


def rows_of(block, first, last):
    return block[:, first:last].reshape(block.shape[0] * (last - first), LANES)


def ids_of(rows, hard):
    lane = lax.broadcasted_iota(jnp.int32, rows.shape, 1)
    ids = rows * 32.0 + pltpu.roll(rows, LANES - hard, 1)
    return jnp.where(lane < hard, ids, 0.0).astype(jnp.int32)


def half_similar(hard, e, pos, pool, ids, first):
    sim = lax.dot_general(e, pos, BY_ROW, preferred_element_type=F32)
    mined = lax.dot_general(e, pool, BY_ROW, preferred_element_type=F32)
    tail = jnp.zeros(ids.shape, F32)
    within, tile = ids & (LANES - 1), ids >> 7
    for k in range(pool.shape[0] // LANES):
        part = mined[:, k * LANES : (k + 1) * LANES]
        picked = jnp.take_along_axis(part, within, axis=1, mode="promise_in_bounds")
        tail = jnp.where(tile == first + k, picked, tail)
    return sim, tail


def own_similar_kernel(hard, got_ref, sim_ref, tail_ref):
    chips, rows, _ = got_ref.shape
    q = rows // 5
    a = got_ref[:, 2 * q :].astype(F32)
    e, pos = rows_of(a, 0, q).astype(BF16), rows_of(a, q, 2 * q).astype(BF16)
    pool = got_ref[:, : 2 * q].reshape(chips * 2 * q, LANES)
    ids = ids_of(rows_of(a, 2 * q, 3 * q), hard)
    sim_ref[...], tail_ref[...] = half_similar(hard, e, pos, pool, ids, 0)


def similar_kernel(hard, got_ref, gotx_ref, own_ref, own_tail_ref, sim_ref):
    chips, rows, _ = got_ref.shape
    q = rows // 5
    half = chips * q
    n = 2 * half
    a = got_ref[:, 2 * q :].astype(F32)
    b = gotx_ref[:, 2 * q :].astype(F32)
    e, pos = rows_of(a, 0, q).astype(BF16), rows_of(b, q, 2 * q).astype(BF16)
    pool = gotx_ref[:, : 2 * q].reshape(n, LANES)
    ids = ids_of(rows_of(a, 2 * q, 3 * q), hard)
    sim, tail = half_similar(hard, e, pos, pool, ids, n // LANES)
    lane = lax.broadcasted_iota(jnp.int32, (half, LANES), 1)
    tail = jnp.where(lane < hard, (tail + own_tail_ref[...]) / TEMPERATURE, 0.0)
    sim_ref[:, :, :half] = (own_ref[...] / TEMPERATURE).reshape(chips, q, half)
    sim_ref[:, :, half:n] = (sim / TEMPERATURE).reshape(chips, q, half)
    sim_ref[:, :, n:] = tail.reshape(chips, q, LANES)


def softmax_kernel(hard, me_ref, in_ref, out_ref):
    copies, q, width = out_ref.shape
    n = width - LANES
    scores = in_ref[...]
    column = lax.broadcasted_iota(jnp.int32, (q, width), 1)
    row = lax.broadcasted_iota(jnp.int32, (q, width), 0)
    exps = jnp.where(column < n + hard, jnp.exp(scores), 0.0)
    soft = exps / jnp.sum(exps, axis=1, keepdims=True)
    own = column == row + (me_ref[0] >> 1) * q
    along = jnp.sum(soft * scores - jnp.where(own, scores, 0.0), axis=1, keepdims=True)
    high = along.astype(BF16).astype(F32)
    sent = jnp.where(column == n + hard, high, soft)
    sent = jnp.where(column == n + hard + 1, along - high, sent)
    sent = sent.astype(BF16)
    for k in range(copies):
        out_ref[k] = sent


def share(w, flip, hard, own_cols, other_cols, pos_all, pools, e, pos, id_rows):
    half = w.shape[0]
    n = 2 * half
    tail = w[:, n:]
    from_own, from_other = w[:, own_cols].astype(BF16), w[:, other_cols].astype(BF16)
    ids = ids_of(id_rows, hard) ^ flip
    weights = tail * pltpu.roll(id_rows, LANES - 2 * hard, 1)
    column = lax.broadcasted_iota(jnp.int32, (half, n), 1)
    own_spread = jnp.zeros((half, n), F32)
    other_spread = jnp.zeros((half, n), F32)
    for m in range(hard):
        one, weight = ids[:, m : m + 1], weights[:, m : m + 1]
        own_spread = jnp.where(column == one, weight, own_spread)
        other_spread = jnp.where(column == one - n, weight, other_spread)
    own_spread = own_spread.astype(BF16)
    other_spread = other_spread.astype(BF16)

    def dot(left, right):
        return jnp.dot(left, right, preferred_element_type=F32)

    numerator = dot(from_own, pos_all[0].astype(BF16)) + dot(from_other, pos_all[1].astype(BF16))
    numerator += dot(own_spread, pools[0]) + dot(other_spread, pools[1])
    along = tail[:, hard : hard + 1] + tail[:, hard + 1 : hard + 2]
    emb_grad = (numerator - pos) / TEMPERATURE - along * e
    eh = e.astype(BF16)
    key = lax.dot_general(from_own, eh, BY_COLUMN, preferred_element_type=F32)
    pool = lax.dot_general(own_spread, eh, BY_COLUMN, preferred_element_type=F32)
    return emb_grad, key, pool, jnp.sum(emb_grad * e, axis=0, keepdims=True)


def blocks(got_ref, gotx_ref, q):
    n = got_ref.shape[0] * 2 * q
    a = got_ref[:, 2 * q :].astype(F32)
    b = gotx_ref[:, 2 * q :].astype(F32)
    pools = got_ref[:, : 2 * q].reshape(n, LANES), gotx_ref[:, : 2 * q].reshape(n, LANES)
    return a, b, (rows_of(a, q, 2 * q), rows_of(b, q, 2 * q)), pools


def own_kernel(hard, w_ref, got_ref, gotx_ref, emb_ref, key_ref, pool_ref, gain_ref):
    chips, q, width = w_ref.shape
    half = chips * q
    a, _, pos_all, pools = blocks(got_ref, gotx_ref, q)
    w = w_ref[...].astype(F32).reshape(half, width)
    e = rows_of(a, 0, q)
    emb_ref[...], key, pool_ref[...], gain_ref[...] = share(
        w, 0, hard, slice(0, half), slice(half, 2 * half), pos_all, pools, e, pos_all[0],
        rows_of(a, 2 * q, 3 * q),
    )
    key_ref[...] = key - e


def slices_kernel(
    hard, me_ref, wx_ref, got_ref, gotx_ref, gain_ref, emb_ref, key_ref, pool_ref, part_ref, out_ref
):
    chips, q, width = wx_ref.shape
    half = chips * q
    _, b, pos_all, pools = blocks(got_ref, gotx_ref, q)
    w = wx_ref[...].astype(F32).reshape(half, width)
    _, key, pool, gain_part = share(
        w, 2 * half, hard, slice(half, 2 * half), slice(0, half), pos_all, pools, rows_of(b, 0, q), pos_all[1],
        rows_of(b, 2 * q, 3 * q),
    )
    emb_grad = emb_ref[...]
    key = (key + key_ref[...]) / TEMPERATURE
    pool = (pool + pool_ref[...]) * (POOL_SCALE / TEMPERATURE)
    gain_part = (gain_part + part_ref[...]) / gain_ref[pl.ds(me_ref[0] >> 1, 1), :]
    gain_high = gain_part.astype(BF16).astype(F32)
    row = lax.broadcasted_iota(jnp.int32, (q, LANES), 0)
    gain_rows = jnp.where(row == 0, gain_high, jnp.where(row == 1, gain_part - gain_high, 0.0))
    for k in range(chips):
        rows = slice(k * q, (k + 1) * q)
        block = [emb_grad[rows], key[rows], pool[2 * k * q : 2 * (k + 1) * q], gain_rows]
        out_ref[k] = jnp.concatenate(block, axis=0).astype(BF16)


def gain_kernel(in_ref, out_ref):
    copies, _, _ = out_ref.shape
    q = in_ref.shape[1] // 5
    both = jnp.sum(in_ref[:, 4 * q :].astype(F32), axis=1)
    for r in range(copies):
        out_ref[r] = both


def backward_kernel(
    len_ref, in_ref, x_ref, gain_ref, unit_ref, inv_ref, norm_ref, grad_hbm, key_hbm, pool_hbm,
    h_ref, row_ref, grad_ref, key_ref, pool_ref, grad_sem, small_sem,
):
    queries, width = unit_ref.shape
    tokens = x_ref.shape[1]
    chunks = width // LANES
    q = queries
    dots = jnp.zeros((q, LANES), F32)
    for k in range(chunks):
        cols = slice(k * LANES, (k + 1) * LANES)
        block = in_ref[k].astype(F32)
        key_ref[:, cols] = block[q : 2 * q]
        pool_ref[:, cols] = block[2 * q : 4 * q]
        g = block[:q]
        h_ref[:, cols] = g
        dots += g * unit_ref[:, cols]
    small = [
        pltpu.make_async_copy(key_ref, key_hbm, small_sem.at[0]),
        pltpu.make_async_copy(pool_ref, pool_hbm, small_sem.at[1]),
    ]
    for copy in small:
        copy.start()
    along = jnp.sum(dots, axis=1, keepdims=True)
    norm = norm_ref[:, :1]
    for k in range(chunks):
        cols = slice(k * LANES, (k + 1) * LANES)
        h = (h_ref[:, cols] - along * unit_ref[:, cols]) * (norm * gain_ref[:, cols])
        for i in range(q):
            row_ref[i, :, cols] = h[i : i + 1]
    token = lax.broadcasted_iota(jnp.int32, (tokens, 1), 0)

    def one_query(i, carry):
        length = len_ref[i]
        total = jnp.zeros((tokens, LANES), F32)
        for k in range(chunks):
            cols = slice(k * LANES, (k + 1) * LANES)
            total += x_ref[i, :, cols].astype(F32) * row_ref[i, :, cols]
        total = jnp.sum(total, axis=1, keepdims=True)
        inv = inv_ref[i][:, :1]
        scale = jnp.where(token < length, QUERY_SCALE * inv, 0.0) / length.astype(F32)
        back = scale * inv * inv * total / width
        for k in range(chunks):
            cols = slice(k * LANES, (k + 1) * LANES)
            x = x_ref[i, :, cols].astype(F32)
            grad_ref[i, :, cols] = (scale * row_ref[i, :, cols] - back * x).astype(BF16)
        pltpu.make_async_copy(grad_ref.at[i], grad_hbm.at[i], grad_sem.at[i]).start()
        return carry

    lax.fori_loop(0, queries, one_query, 0)
    for i in range(queries):
        pltpu.make_async_copy(grad_ref.at[i], grad_hbm.at[i], grad_sem.at[i]).wait()
    for copy in small:
        copy.wait()


def call(kernel, outs, args, flops, smem=(), hbm=(), scratch=(), vmem=40, out_hbm=False):
    def space(i):
        return pltpu.SMEM if i in smem else pltpu.HBM if i in hbm else pltpu.VMEM

    size = sum(a.size * a.dtype.itemsize for a in args) + sum(
        o.size * o.dtype.itemsize for o in outs
    )
    return pl.pallas_call(
        kernel,
        out_shape=list(outs),
        in_specs=[pl.BlockSpec(memory_space=space(i)) for i in range(len(args))],
        out_specs=[pl.BlockSpec(memory_space=pltpu.HBM if out_hbm else pltpu.VMEM)] * len(outs),
        scratch_shapes=list(scratch),
        compiler_params=pltpu.CompilerParams(vmem_limit_bytes=vmem * 1024 * 1024),
        cost_estimate=pl.CostEstimate(flops=flops, bytes_accessed=size, transcendentals=0),
    )(*args)


def shape(dims, dtype):
    return jax.ShapeDtypeStruct(dims, dtype)


def local(query_states, query_lengths, norm_gain, positives, mined_pool, hard_ids):
    owners = lax.axis_size("dp")
    groups = lax.axis_size("rep")
    me = lax.axis_index("dp").astype(jnp.int32).reshape(1)
    _, queries, tokens, width = query_states.shape
    hard = hard_ids.shape[2]
    chips = owners // 2
    q_all = queries * owners
    lengths = query_lengths.reshape(queries)
    gain_row = norm_gain.reshape(1, width)
    gain_tiles = norm_gain.reshape(chips, LANES)
    pair = [(i, i ^ 1) for i in range(owners)]
    same_core = [[2 * i + c for i in range(chips)] for c in range(2)]

    def among_chips(x):
        return lax.all_to_all(x, "dp", 0, 0, tiled=True, axis_index_groups=same_core)

    def bound(kernel):
        return lambda *refs: kernel(hard, *refs)

    out, unit, inv, norm = call(
        embed_kernel,
        [
            shape((chips, 5 * queries, LANES), BF16),
            shape((queries, width), F32),
            shape((queries, tokens, LANES), F32),
            shape((queries, LANES), F32),
        ],
        [me, query_lengths, query_states, gain_row, positives, mined_pool, hard_ids.transpose(2, 0, 1)],
        8_000_000,
        (0,),
        (1, 2, 3, 4, 5, 6),
        [
            pltpu.SMEM((1, queries), jnp.int32),
            pltpu.VMEM((queries, tokens, width), BF16),
            pltpu.VMEM((1, width), F32),
            pltpu.VMEM((1, queries, width), BF16),
            pltpu.VMEM((1, 2 * queries, width), BF16),
            pltpu.VMEM((hard, 1, queries), jnp.int32),
            pltpu.VMEM((queries, 1, width), F32),
            pltpu.SemaphoreType.DMA((queries,)),
            pltpu.SemaphoreType.DMA((5,)),
        ],
        60,
    )
    got = among_chips(out)
    gotx = lax.ppermute(got, "dp", pair)

    half = q_all // 2
    own = call(
        bound(own_similar_kernel),
        [shape((half, half), F32), shape((half, LANES), F32)],
        [got],
        50_000_000,
    )
    (part,) = call(
        bound(similar_kernel),
        [shape((chips, queries, q_all + LANES), F32)],
        [got, gotx, *own],
        50_000_000,
    )
    scores = jnp.sum(among_chips(part.astype(F16)).astype(F32), axis=0)
    (sent,) = call(
        bound(softmax_kernel),
        [shape((chips, queries, q_all + LANES), BF16)],
        [me, scores],
        1_000_000,
        (0,),
    )
    weights = among_chips(sent)
    weightsx = lax.ppermute(weights, "dp", pair)

    half = q_all // 2
    shares = call(
        bound(own_kernel),
        [
            shape((half, LANES), F32),
            shape((half, LANES), F32),
            shape((q_all, LANES), F32),
            shape((1, LANES), F32),
        ],
        [weights, got, gotx],
        200_000_000,
    )
    (back,) = call(
        bound(slices_kernel),
        [shape((chips, 5 * queries, LANES), BF16)],
        [me, weightsx, got, gotx, gain_tiles, *shares],
        200_000_000,
        (0,),
    )
    home = among_chips(back)
    (gain_sent,) = call(
        gain_kernel, [shape((groups, width // LANES, LANES), F32)], [home], 100_000
    )
    gain_groups = lax.all_to_all(gain_sent, "rep", 0, 0, tiled=True)
    query_grad, key_grad, pool_grad = call(
        backward_kernel,
        [
            shape((queries, tokens, width), BF16),
            shape((queries, width), F32),
            shape((2 * queries, width), F32),
        ],
        [lengths, home, query_states[0], gain_row, unit, inv, norm],
        10_000_000,
        (0,),
        (),
        [
            pltpu.VMEM((queries, width), F32),
            pltpu.VMEM((queries, 1, width), F32),
            pltpu.VMEM((queries, tokens, width), BF16),
            pltpu.VMEM((queries, width), F32),
            pltpu.VMEM((2 * queries, width), F32),
            pltpu.SemaphoreType.DMA((queries,)),
            pltpu.SemaphoreType.DMA((2,)),
        ],
        out_hbm=True,
    )
    gain_grad = jnp.sum(gain_groups, axis=0).reshape(width)
    return query_grad[None], key_grad[None], pool_grad[None], gain_grad


def solution(mesh):
    placed = (
        P("rep", "dp", None, None),
        P("rep", "dp"),
        P(),
        P("rep", "dp", None),
        P("rep", "dp", None),
        P("rep", "dp", None),
    )
    return jax.shard_map(
        local,
        mesh=mesh,
        in_specs=placed,
        out_specs=(P("rep", "dp", None, None), P("rep", "dp", None), P("rep", "dp", None), P()),
        check_vma=False,
    )
```
